512 devices in a mesh: tm: 64 (over x, y, core), region: 8 (over z).
Axes of the slice: x: 4, y: 8, z: 8, core: 2. Of those that a mesh axis runs over, the one named last changes fastest.
Arguments:
- cost: bfloat16 [1536, 96, 1024], P('tm', 'region'), may hold values from -25 to 25
- demand: bfloat16 [1536, 96, 256], P('tm', 'region'), may hold values from -25 to 25
- conversion: float32 [1024, 256], replicated, may hold values from -0.1875 to 0.1875
- upper: float32 [96, 1024], P('region'), may hold values from 0.2 to 2
- decay: float32 [1536, 96, 128], P('tm', 'region'), may hold values from 0.4 to 1
- energy_cap: float32 [96, 128], P('region'), may hold values from 0.02 to 0.4
- annual_cap: float32 [96, 1024], P('region'), may hold values from 0.05 to 1
- line_ends: int32 [256, 2], P('region'), may hold values from 0 to 95, as said below
- line_cap: float32 [256], P('region'), may hold values from 0.2 to 2
Outputs:
- primal: bfloat16 [1536, 96, 1024], P('tm', 'region')
- flows: float32 [1536, 256], P('tm', 'region')
- prices: float32 [1536, 96, 256], P('tm', 'region')
- storage_dual: float32 [1536, 96, 128], P('tm', 'region')
- year_dual: float32 [96, 1024], P('region')
The draws below stay inside these ranges and needn't reach their ends.
Inputs may be any that keep to these rules, and one draw needn't show every extreme that they name: `line_ends`: each line joins two different regions, every region is the first end of some line.
All inputs are finite; a program needn't handle non-finite values.
Results may differ from the reference program's by a relative error of at most 0.0012.
Values sent between devices are 32-bit elements; how exact they have to be, the bound alone decides.
No kernel may reach another device: no remote copies, remote signals or barrier semaphores. Data moves between devices by JAX's collectives and lax.ppermute only.
A program may use at most 64 MiB of HBM per device.

```python
import math
import jax
import jax.numpy as jnp
from jax import lax

K = 1024
STORAGE_COUNT = 128
M = 256
ITERS = 2
HOURS_IN_ALL = 1536
REGIONS_IN_ALL = 96
LINES = 256


def scaled_field(key, last_width):
    random_key_list = jax.random.split(key, 3)
    base = jax.random.truncated_normal(random_key_list[0], -3.0, 3.0, (HOURS_IN_ALL, REGIONS_IN_ALL, last_width), jnp.float32)
    hour_scale = jnp.exp(jax.random.uniform(random_key_list[1], (HOURS_IN_ALL, 1, 1), jnp.float32, 0.0, math.log(10.0)))
    column_scale = jnp.exp(jax.random.uniform(random_key_list[2], (1, 1, last_width), jnp.float32, 0.0, math.log(10.0)))
    ramp = jnp.exp(math.log(3.0) * jnp.arange(HOURS_IN_ALL, dtype=jnp.float32) / max(HOURS_IN_ALL - 1, 1))[:, None, None]
    return base * hour_scale * column_scale * ramp / 40.0


def draw_cost(key, part):
    return scaled_field(jax.random.fold_in(key, 11), K).astype(jnp.bfloat16)


def draw_demand(key, part):
    return scaled_field(jax.random.fold_in(key, 23), M).astype(jnp.bfloat16)


def draw_decay(key, part):
    random_key_list = jax.random.split(jax.random.fold_in(key, 37), 7)
    slow_share = 0.4
    middle_share = 0.4
    class_draw = jax.random.uniform(random_key_list[0], (REGIONS_IN_ALL, STORAGE_COUNT), jnp.float32)
    slow = class_draw < slow_share
    middle = jnp.logical_and(class_draw >= slow_share, class_draw < slow_share + middle_share)
    fast_rate = 1.0 / jax.random.uniform(random_key_list[1], (REGIONS_IN_ALL, STORAGE_COUNT), jnp.float32, 20.0, 50.0)
    slow_rate = jax.random.uniform(random_key_list[2], (REGIONS_IN_ALL, STORAGE_COUNT), jnp.float32, 0.1, 1.0) / HOURS_IN_ALL
    middle_rate = 1.0 / jax.random.uniform(random_key_list[6], (REGIONS_IN_ALL, STORAGE_COUNT), jnp.float32, 210.0, 227.0)
    region_factor = jnp.exp(jax.random.uniform(random_key_list[3], (REGIONS_IN_ALL, 1), jnp.float32, math.log(0.5), math.log(2.0)))
    rate = jnp.where(slow, slow_rate * region_factor, jnp.where(middle, middle_rate, fast_rate * region_factor))
    closing_output = jnp.broadcast_to(jnp.exp(-rate)[None], (HOURS_IN_ALL, REGIONS_IN_ALL, STORAGE_COUNT))
    spike_hours = jax.random.permutation(random_key_list[4], HOURS_IN_ALL)[:3]
    spike_keep_mask = jax.random.uniform(random_key_list[5], (3, REGIONS_IN_ALL, STORAGE_COUNT), jnp.float32, 0.6, 0.8)
    hour_index_rows = jnp.arange(HOURS_IN_ALL)
    for spike_count in range(3):
        closing_output = closing_output * jnp.where((hour_index_rows == spike_hours[spike_count])[:, None, None], spike_keep_mask[spike_count][None], 1.0)
    return closing_output


def draw_line_ends(key, part):
    random_key_list = jax.random.split(jax.random.fold_in(key, 41), 2)
    offset = jax.random.randint(random_key_list[0], (), 0, REGIONS_IN_ALL)
    first = (jnp.arange(LINES, dtype=jnp.int32) + offset) % REGIONS_IN_ALL
    second = (first + jax.random.randint(random_key_list[1], (LINES,), 1, REGIONS_IN_ALL)) % REGIONS_IN_ALL
    return jnp.stack([first, second], axis=1).astype(jnp.int32)


def block_scale(own_key, extent, cuts, smallest, high):
    level = 1.0
    for dim, blocks in cuts:
        draws = jax.random.uniform(jax.random.fold_in(jax.random.fold_in(own_key, 6), dim), (blocks,), jnp.float32, smallest / len(cuts), high / len(cuts))
        level = level * jnp.repeat(jnp.exp(draws), extent[dim] // blocks).reshape((-1,) + (1,) * (len(extent) - 1 - dim))
    return level


def normal_values(key, dims, deviation, reach, kind=jnp.bfloat16):
    return jnp.clip(deviation * jax.random.normal(key, dims, jnp.float32), -reach, reach).astype(kind)


def setup_inputs(seed: int = 0) -> dict:
    splits = jax.random.split(jax.random.key(seed), 10)
    return {
        "cost": draw_cost(jax.random.fold_in(splits[9], 71), 0),
        "demand": draw_demand(jax.random.fold_in(splits[9], 71), 0),
        "conversion": normal_values(splits[2], (K, M), K ** -0.5, 0.1875, jnp.float32),
        "upper": jnp.clip(jnp.exp(math.log(2.0) - 2.3025851 * jax.random.uniform(splits[3], (REGIONS_IN_ALL, K), jnp.float32) ** block_scale(splits[3], (REGIONS_IN_ALL, K), ((0, 8),), -0.2, 0.2)), 0.2, 2.0),
        "decay": draw_decay(jax.random.fold_in(splits[9], 71), 0),
        "energy_cap": jnp.clip(jnp.exp(math.log(0.4) - 2.9957323 * jax.random.uniform(splits[5], (REGIONS_IN_ALL, STORAGE_COUNT), jnp.float32) ** block_scale(splits[5], (REGIONS_IN_ALL, STORAGE_COUNT), ((0, 8),), -0.2, 0.2)), 0.02, 0.4),
        "annual_cap": jnp.clip(jnp.exp(math.log(1.0) - 2.9957323 * jax.random.uniform(splits[6], (REGIONS_IN_ALL, K), jnp.float32) ** block_scale(splits[6], (REGIONS_IN_ALL, K), ((0, 8),), -0.2, 0.2)), 0.05, 1.0),
        "line_ends": draw_line_ends(jax.random.fold_in(splits[9], 71), 0),
        "line_cap": jnp.clip(jnp.exp(math.log(2.0) - 2.3025851 * jax.random.uniform(splits[8], (LINES,), jnp.float32) ** block_scale(splits[8], (LINES,), ((0, 8),), -0.2, 0.2)), 0.2, 2.0),
    }


step_ratio = 0.5

def affine(earlier, later):
    return (earlier[0] * later[0], later[0] * earlier[1] + later[1])

def reference(cost, demand, conversion, upper, decay, energy_cap, annual_cap, line_ends, line_cap):
    highest = lax.Precision.HIGHEST
    level_scale = 1.0 / math.sqrt(HOURS_IN_ALL)
    year_scale = 1.0 / math.sqrt(HOURS_IN_ALL)
    year_bound = math.sqrt(HOURS_IN_ALL)
    costs = cost.astype(jnp.float32)
    loads = demand.astype(jnp.float32)
    omega = jnp.sqrt(jnp.sum(costs * costs) / jnp.sum(loads * loads))
    tau_step = step_ratio / omega
    sigma_step = step_ratio * omega
    columns = jnp.arange(K, dtype=jnp.int32)
    lower = jnp.where(columns[None, :] < STORAGE_COUNT, -upper, jnp.float32(0.0))
    region_ids = jnp.arange(REGIONS_IN_ALL, dtype=jnp.int32)
    incidence = (line_ends[:, 1:2] == region_ids[None, :]).astype(jnp.float32) - (line_ends[:, 0:1] == region_ids[None, :]).astype(jnp.float32)

    def levels_of(charge):
        scale_run, offset_run = lax.associative_scan(affine, (decay, charge), axis=0)
        return level_scale * offset_run

    def levels_adjoint(dual):
        weighted = level_scale * dual
        scale_run, offset_run = lax.associative_scan(affine, (decay, decay * weighted), axis=0, reverse=True)
        return weighted + jnp.concatenate([offset_run[1:], jnp.zeros_like(offset_run[:1])], axis=0)
    primal = jnp.zeros((HOURS_IN_ALL, REGIONS_IN_ALL, K), jnp.float32)
    flows = jnp.zeros((HOURS_IN_ALL, LINES), jnp.float32)
    prices = jnp.zeros((HOURS_IN_ALL, REGIONS_IN_ALL, M), jnp.float32)
    storage_dual = jnp.zeros((HOURS_IN_ALL, REGIONS_IN_ALL, STORAGE_COUNT), jnp.float32)
    year_dual = jnp.zeros((REGIONS_IN_ALL, K), jnp.float32)
    for step in range(ITERS):
        back = jnp.dot(prices.reshape(-1, M), conversion.T, precision=highest).reshape(HOURS_IN_ALL, REGIONS_IN_ALL, K)
        stored = levels_adjoint(storage_dual)
        stored = jnp.pad(stored, ((0, 0), (0, 0), (0, K - STORAGE_COUNT)))
        grad = costs + back + stored + year_scale * year_dual[None]
        new_primal = jnp.clip(primal - tau_step * grad, lower[None], upper[None])
        flow_grad = jnp.dot(prices[:, :, 0], incidence.T, precision=highest)
        new_flows = jnp.clip(flows - tau_step * flow_grad, -line_cap[None], line_cap[None])
        bar = 2.0 * new_primal - primal
        flow_bar = 2.0 * new_flows - flows
        inflow = jnp.dot(flow_bar, incidence, precision=highest)
        image = jnp.dot(bar.reshape(-1, K), conversion, precision=highest).reshape(HOURS_IN_ALL, REGIONS_IN_ALL, M)
        image = jnp.concatenate([image[:, :, :1] + inflow[:, :, None], image[:, :, 1:]], axis=2)
        prices = prices + sigma_step * (image - loads)
        storage_dual = jnp.maximum(storage_dual + sigma_step * (levels_of(bar[:, :, :STORAGE_COUNT]) - energy_cap[None]), 0.0)
        year_dual = jnp.maximum(year_dual + sigma_step * (year_scale * lax.optimization_barrier(jnp.sum(bar, axis=0)) - year_bound * annual_cap), 0.0)
        primal = new_primal
        flows = new_flows
    return (primal.astype(jnp.bfloat16), flows, prices, storage_dual, year_dual)
```

```python
import functools
import math

import jax
import jax.numpy as jnp
from jax import lax
from jax.experimental import pallas as pl
from jax.experimental.pallas import tpu as pltpu
from jax.sharding import PartitionSpec as P

F32 = jnp.float32
BF16 = jnp.bfloat16
LANES = 128
PAD_ROWS = 16
step_ratio = 0.5


def call(kernel, out_shape, name, scratch=(), in_specs=None, flops=1000000, nbytes=1000000):
    specs = {} if in_specs is None else {"in_specs": in_specs}
    return pl.pallas_call(
        kernel,
        out_shape=out_shape,
        **specs,
        scratch_shapes=list(scratch),
        name=name,
        compiler_params=pltpu.CompilerParams(vmem_limit_bytes=24 * 1024 * 1024),
        cost_estimate=pl.CostEstimate(flops=flops, bytes_accessed=nbytes, transcendentals=0),
    )


def struct(*shape, dtype=F32):
    return jax.ShapeDtypeStruct(shape, dtype)


def lane_ids(shape):
    return lax.broadcasted_iota(jnp.int32, shape, len(shape) - 1)


def swap_halves(x):
    return pltpu.roll(x, LANES // 2, 1)


def spread(scratch):
    return jnp.transpose(scratch)[: LANES // 2, :]


def collect(received):
    return jnp.transpose(jnp.concatenate([received, jnp.zeros_like(received)], axis=0))


def split(x):
    high = x.astype(BF16)
    return high, (x - high.astype(F32)).astype(BF16)


def dot(a, b, dims):
    return lax.dot_general(a, b, (dims, ((), ())), preferred_element_type=F32)


def dot3(a, b, dims):
    (ah, al), (bh, bl) = a, b
    return dot(ah, bh, dims) + (dot(ah, bl, dims) + dot(al, bh, dims))


def bounds(upper_row, units):
    return jnp.where(lane_ids(upper_row.shape) < units, -upper_row, 0.0), upper_row


def clip(x, low, high):
    return jnp.minimum(jnp.maximum(x, low), high)


def sums_kernel(cost_ref, demand_ref, out_ref):
    regions = cost_ref.shape[0]

    def total(ref):
        acc = None
        for r in range(regions):
            x = ref[r].astype(F32)
            acc = x * x if acc is None else acc + x * x
        return jnp.sum(jnp.sum(acc, axis=0, keepdims=True), axis=1, keepdims=True)

    ids = lane_ids((1, LANES))
    row = jnp.where(ids == 0, total(cost_ref), jnp.where(ids == 1, total(demand_ref), 0.0))
    out_ref[...] = jnp.broadcast_to(row, out_ref.shape)


def turn_kernel(cost_ref, decay_ref, out_ref, rows):
    regions, hours, units = decay_ref.shape
    n = regions * hours
    costs = cost_ref[:, :, :units].astype(F32).reshape(n, units)
    decay = decay_ref[...].reshape(n, units)
    for place, x in enumerate((costs, swap_halves(costs), decay, swap_halves(decay))):
        rows[place * n : (place + 1) * n, :] = x
    out_ref[...] = spread(rows[...])


def year_pieces(rows, out_ref):
    half = rows.shape[0] // 2
    rows[half:, :] = swap_halves(rows[:half, :])
    out_ref[...] = spread(rows[...])


def year_totals(received, regions):
    x = collect(received)
    half = x.shape[0] // 2
    tiles = []
    for t in range(half // PAD_ROWS):
        at = t * PAD_ROWS
        tile = x[at : at + PAD_ROWS, :] + swap_halves(x[half + at : half + at + PAD_ROWS, :])
        tiles.append(tile[:regions, :])
    return tiles


def first_kernel(units, year_scale, sums_ref, cost_ref, upper_ref, omega_ref, out_ref, rows):
    regions, hours, width = cost_ref.shape
    s = jnp.sum(sums_ref[...], axis=0, keepdims=True)
    ids = lane_ids(s.shape)
    cost_sum = jnp.sum(jnp.where(ids == 0, s, 0.0), axis=1, keepdims=True)
    load_sum = jnp.sum(jnp.where(ids == 1, s, 0.0), axis=1, keepdims=True)
    omega = jnp.sqrt(cost_sum / load_sum)
    omega_ref[...] = jnp.broadcast_to(omega, omega_ref.shape)
    tau = step_ratio / omega
    rows[...] = jnp.zeros_like(rows)
    for r in range(regions):
        low, high = bounds(upper_ref[r : r + 1, :], units)
        primal = clip(-tau * cost_ref[r].astype(F32), low, high)
        sums = (2.0 * year_scale) * jnp.sum(primal, axis=0, keepdims=True)
        for t in range(width // LANES):
            rows[t * PAD_ROWS + r : t * PAD_ROWS + r + 1, :] = sums[:, t * LANES : (t + 1) * LANES]
    year_pieces(rows, out_ref)


def prices_kernel(
    units, omega_ref, cost_ref, upper_ref, demand_ref, conversion_ref, ends_ref,
    prices_ref, back_ref, turned_ref, bus_ref, bar, rows,
):
    regions, hours, width = cost_ref.shape
    bus_rows = demand_ref.shape[2]
    n = regions * hours
    omega = omega_ref[0:1, 0:1]
    tau, sigma = step_ratio / omega, step_ratio * omega
    for r in range(regions):
        low, high = bounds(upper_ref[r : r + 1, :], units)
        bar[r * hours : (r + 1) * hours, :] = 2.0 * clip(-tau * cost_ref[r].astype(F32), low, high)
    step = 256
    image = None
    for k in range(0, width, step):
        part = dot3(split(bar[:, k : k + step]), split(conversion_ref[k : k + step, :]), ((1,), (0,)))
        image = part if image is None else image + part
    loads = demand_ref[...].astype(F32).reshape(n, bus_rows)
    prices = sigma * (image - loads)
    prices_ref[...] = prices
    cut = split(prices)
    for k in range(0, width, step):
        back_ref[:, k : k + step] = dot3(cut, split(conversion_ref[k : k + step, :]), ((1,), (1,)))
    stored = back_ref[:, :units]
    rows[:n, :] = stored
    rows[n:, :] = swap_halves(stored)
    turned_ref[...] = spread(rows[...])
    bus = jnp.transpose(prices[:, :LANES])[0:1, :]
    ends = ends_ref[...]
    row = jnp.concatenate([bus, jnp.zeros((1, ends.shape[1] - n), F32)], axis=1) + ends
    bus_ref[...] = jnp.broadcast_to(row, bus_ref.shape)


def sum_rows_kernel(received_ref, out_ref):
    out_ref[...] = jnp.broadcast_to(jnp.sum(received_ref[...], axis=0, keepdims=True), out_ref.shape)


def sum_rows_with_stored_kernel(received_ref, stored_ref, out_ref):
    total = jnp.sum(received_ref[...], axis=0, keepdims=True)
    ids = lane_ids(total.shape)
    total = jnp.where(lax.rem(ids, LANES) < PAD_ROWS, stored_ref[0:1, :], total)
    out_ref[...] = jnp.broadcast_to(total, out_ref.shape)


def before(x, k, reverse):
    ids = lax.rem(lane_ids(x.shape), LANES // 2)
    if reverse:
        return pltpu.roll(x, LANES - k, 1), ids < LANES // 2 - k
    return pltpu.roll(x, k, 1), ids >= k


def carry_in(scale, offset, reverse):
    k = 1
    while k < LANES // 2:
        scale_before, ok = before(scale, k, reverse)
        offset_before, _ = before(offset, k, reverse)
        offset = jnp.where(ok, scale * offset_before + offset, offset)
        scale = jnp.where(ok, scale * scale_before, scale)
        k *= 2
    entering, ok = before(offset, 1, reverse)
    return jnp.where(ok, entering, 0.0)


def storage_kernel(
    level_scale, year_scale, year_bound,
    place_ref, omega_ref, turned_ref, back_ref, upper_ref, energy_ref, annual_ref,
    out_ref, year_ref, costs, decay, back, run, scale, dual, primal, suffix, suffix_scale, rows,
):
    regions, units = energy_ref.shape
    n = costs.shape[0]
    hours = n // regions
    place = place_ref[0]
    omega = omega_ref[0:1, 0:1]
    tau, sigma = step_ratio / omega, step_ratio * omega
    ids = lane_ids((regions, units))
    left = ids < units // 2

    def pair(x):
        first = jnp.sum(jnp.where(ids == place, x, 0.0), axis=1, keepdims=True)
        second = jnp.sum(jnp.where(ids == place + units // 2, x, 0.0), axis=1, keepdims=True)
        return jnp.where(left, first, second)

    def halves(x):
        first = jnp.sum(jnp.where(left, x, 0.0), axis=1, keepdims=True)
        second = jnp.sum(jnp.where(left, 0.0, x), axis=1, keepdims=True)
        return first, second

    high = pair(upper_ref[:, :units])
    energy = pair(energy_ref[...])
    annual = pair(annual_ref[:, :units])
    x = collect(turned_ref[...])
    costs[...] = x[:n] + swap_halves(x[n : 2 * n])
    decay[...] = x[2 * n : 3 * n] + swap_halves(x[3 * n :])
    x = collect(back_ref[...])
    back[...] = x[:n] + swap_halves(x[n:])

    def get(ref, h):
        return ref[pl.ds(h, regions, stride=hours), :]

    def put(ref, h, value):
        ref[pl.ds(h, regions, stride=hours), :] = value

    def first_primal(h):
        return clip(-tau * get(costs, h), -high, high)

    level = jnp.zeros((regions, units), F32)
    kept = jnp.ones((regions, units), F32)
    year = jnp.zeros((regions, units), F32)
    for h in range(hours):
        d = get(decay, h)
        bar = 2.0 * first_primal(h)
        year = year + bar
        level = d * level + bar
        kept = kept * d
        put(run, h, level)
        put(scale, h, kept)
    entering = carry_in(kept, level, False)
    first, second = halves(year)
    year_total = year_scale * jnp.where(left, first, second)
    year_dual = jnp.maximum(sigma * (year_total - year_bound * annual), 0.0)
    after = jnp.zeros((regions, units), F32)
    after_kept = jnp.ones((regions, units), F32)
    for h in reversed(range(hours)):
        d = get(decay, h)
        level = get(run, h) + get(scale, h) * entering
        stored = jnp.maximum(sigma * (level_scale * level - energy), 0.0)
        put(dual, h, stored)
        after = d * (level_scale * stored + after)
        after_kept = after_kept * d
        put(suffix, h, after)
        put(suffix_scale, h, after_kept)
    closing = carry_in(after_kept, after, True)
    level = jnp.zeros((regions, units), F32)
    year = jnp.zeros((regions, units), F32)
    for h in range(hours):
        later = closing if h == hours - 1 else get(suffix, h + 1) + get(suffix_scale, h + 1) * closing
        grad = get(costs, h) + get(back, h) + (level_scale * get(dual, h) + later) + year_scale * year_dual
        old = first_primal(h)
        new = clip(old - tau * grad, -high, high)
        put(primal, h, new)
        bar = 2.0 * new - old
        year = year + bar
        level = get(decay, h) * level + bar
        put(run, h, level)
    entering = carry_in(kept, level, False)
    for h in range(hours):
        level = get(run, h) + get(scale, h) * entering
        put(dual, h, jnp.maximum(get(dual, h) + sigma * (level_scale * level - energy), 0.0))
    rows[:n, :] = primal[...]
    rows[n : 2 * n, :] = swap_halves(primal[...])
    rows[2 * n : 3 * n, :] = dual[...]
    rows[3 * n :, :] = swap_halves(dual[...])
    out_ref[...] = spread(rows[...])
    diagonal = lax.broadcasted_iota(jnp.int32, (regions, units), 0) == ids
    for part, column in enumerate(halves(year)):
        line = jnp.sum(jnp.where(diagonal, year_scale * column, 0.0), axis=0, keepdims=True)
        year_ref[:, part * LANES : (part + 1) * LANES] = jnp.broadcast_to(line, (year_ref.shape[0], LANES))


def second_kernel(
    units, year_scale, year_bound,
    omega_ref, year_ref, cost_ref, back_ref, upper_ref, annual_ref,
    dual_ref, out_ref, rows,
):
    regions, hours, width = cost_ref.shape
    omega = omega_ref[0:1, 0:1]
    tau, sigma = step_ratio / omega, step_ratio * omega
    for t, total in enumerate(year_totals(year_ref[...], regions)):
        at = slice(t * LANES, (t + 1) * LANES)
        dual_ref[:, at] = jnp.maximum(sigma * (total - year_bound * annual_ref[:, at]), 0.0)
    rows[...] = jnp.zeros_like(rows)
    for r in range(regions):
        high = upper_ref[r : r + 1, units:]
        costs = cost_ref[r, :, units:].astype(F32)
        old = clip(-tau * costs, 0.0, high)
        grad = costs + back_ref[r * hours : (r + 1) * hours, units:] + year_scale * dual_ref[r : r + 1, units:]
        bar = 2.0 * clip(old - tau * grad, 0.0, high) - old
        sums = year_scale * jnp.sum(bar, axis=0, keepdims=True)
        for t in range(1, width // LANES):
            rows[t * PAD_ROWS + r : t * PAD_ROWS + r + 1, :] = sums[:, t * LANES - units : (t + 1) * LANES - units]
    year_pieces(rows, out_ref)


def last_kernel(
    units, place_ref, omega_ref, cost_ref, back_ref, upper_ref, dual_ref, returned_ref, conversion_ref,
    demand_ref, prices_ref, bus_ref, ends_ref, caps_ref, own_ends_ref, own_caps_ref,
    primal_ref, flows_ref, new_prices_ref, storage_ref, bar,
):
    regions, hours, width = cost_ref.shape
    bus_rows = demand_ref.shape[2]
    n = regions * hours
    year_scale = 1.0 / math.sqrt(hours * (LANES // 2))
    omega = omega_ref[0:1, 0:1]
    tau, sigma = step_ratio / omega, step_ratio * omega
    x = collect(returned_ref[...])
    storage_ref[...] = x[2 * n : 3 * n] + swap_halves(x[3 * n :])
    bar[:, :units] = x[:n] + swap_halves(x[n : 2 * n])
    for r in range(regions):
        at = slice(r * hours, (r + 1) * hours)
        high = upper_ref[r : r + 1, units:]
        costs = cost_ref[r, :, units:].astype(F32)
        old = clip(-tau * costs, 0.0, high)
        grad = costs + back_ref[at, units:] + year_scale * dual_ref[r : r + 1, units:]
        new = clip(old - tau * grad, 0.0, high)
        bar[at, units:] = 2.0 * new - old
        stored = bar[at, :units]
        primal_ref[r] = jnp.concatenate([stored, new], axis=1).astype(BF16)
        high = upper_ref[r : r + 1, :units]
        old = clip(-tau * cost_ref[r, :, :units].astype(F32), -high, high)
        bar[at, :units] = 2.0 * stored - old
    step = 256
    image = None
    for k in range(0, width, step):
        part = dot3(split(bar[:, k : k + step]), split(conversion_ref[k : k + step, :]), ((1,), (0,)))
        image = part if image is None else image + part
    loads = demand_ref[...].astype(F32).reshape(n, bus_rows)
    new_prices_ref[...] = prices_ref[...] + sigma * (image - loads)

    regions_all = bus_ref.shape[0]
    bus = bus_ref[...]

    def exact(a, b, dims):
        return lax.dot_general(
            a, b, (dims, ((), ())), precision=lax.Precision.HIGHEST, preferred_element_type=F32
        )

    def incidence(ends, first, count):
        ids = lax.broadcasted_iota(jnp.int32, (count, ends.shape[1]), 0) + first
        return (ids == ends[1:2, :]).astype(F32) - (ids == ends[0:1, :]).astype(F32)

    def new_flows(ends, caps):
        grad = exact(bus, incidence(ends, 0, regions_all), ((0,), (0,)))
        return clip(-tau * grad, -caps, caps)

    flows_ref[...] = new_flows(own_ends_ref[...], own_caps_ref[...])
    flow_bar = 2.0 * new_flows(ends_ref[...], caps_ref[...])
    own = incidence(ends_ref[...], place_ref[0] * regions, LANES)
    inflow = exact(flow_bar, own, ((1,), (1,)))
    ids = lane_ids(inflow.shape)
    for r in range(regions):
        moved = inflow if r == 0 else pltpu.roll(inflow, LANES - r, 1)
        at = slice(r * hours, (r + 1) * hours)
        new_prices_ref[at, :LANES] = new_prices_ref[at, :LANES] + sigma * jnp.where(ids == 0, moved, 0.0)


def year_kernel(year_bound, omega_ref, year_ref, dual_ref, annual_ref, out_ref):
    sigma = step_ratio * omega_ref[0:1, 0:1]
    for t, total in enumerate(year_totals(year_ref[...], dual_ref.shape[0])):
        at = slice(t * LANES, (t + 1) * LANES)
        out_ref[:, at] = jnp.maximum(dual_ref[:, at] + sigma * (total - year_bound * annual_ref[:, at]), 0.0)


def exchange(x, axes):
    return lax.all_to_all(x, axes, 0, 0, tiled=True)


def per_device(cost, demand, conversion, upper, decay, energy_cap, annual_cap, line_ends, line_cap):
    hours, regions, width = cost.shape
    bus_rows = demand.shape[2]
    units = decay.shape[2]
    lines = line_ends.shape[0]
    blocks = lax.axis_size("tm")
    groups = lax.axis_size("region")
    hours_all = hours * blocks
    scale = 1.0 / math.sqrt(hours_all)
    bound = math.sqrt(hours_all)
    n = regions * hours
    year_rows = 2 * PAD_ROWS * (width // LANES)
    smem = pl.BlockSpec(memory_space=pltpu.SMEM)
    vmem = pl.BlockSpec(memory_space=pltpu.VMEM)
    rows = lambda k: pltpu.VMEM((k, LANES), F32)
    cost = jnp.transpose(cost, (1, 0, 2))
    demand = jnp.transpose(demand, (1, 0, 2))
    decay = jnp.transpose(decay, (1, 0, 2))

    sums = call(sums_kernel, struct(blocks * groups, LANES), "sums")(cost, demand)
    sums = exchange(sums, ("tm", "region"))
    turned = call(turn_kernel, struct(blocks, 4 * n), "turn", [rows(4 * n)])(cost, decay)
    turned = exchange(turned, "tm")
    omega, year = call(
        functools.partial(first_kernel, units, scale),
        (struct(8, LANES), struct(blocks, year_rows)),
        "first_primal",
        [rows(year_rows)],
    )(sums, cost, upper)
    year = exchange(year, "tm")

    ends_t = line_ends.T.astype(F32)
    own = jnp.concatenate([jnp.zeros((1, n), F32), ends_t.reshape(1, -1), line_cap.reshape(1, -1)], axis=1)
    prices, back, back_turned, bus = call(
        functools.partial(prices_kernel, units),
        (struct(n, bus_rows), struct(n, width), struct(blocks, 2 * n), struct(groups, own.shape[1])),
        "first_prices",
        [pltpu.VMEM((n, width), F32), rows(2 * n)],
        flops=4000000000,
        nbytes=5000000,
    )(omega, cost, upper, demand, conversion, own)
    back_turned = exchange(back_turned, "tm")
    bus = exchange(bus, "region")

    year = call(sum_rows_kernel, struct(blocks, year_rows), "year_sum")(year)
    year = exchange(year, "tm")

    tm_place = lax.axis_index("tm").astype(jnp.int32).reshape(1)
    region_place = lax.axis_index("region").astype(jnp.int32).reshape(1)
    returned, stored_year = call(
        functools.partial(storage_kernel, scale, scale, bound),
        (struct(blocks, 4 * n), struct(8, year_rows)),
        "storage",
        [rows(n) for _ in range(9)] + [rows(4 * n)],
        in_specs=[smem] + [vmem] * 6,
        flops=4000000000,
    )(tm_place, omega, turned, back_turned, upper, energy_cap, annual_cap)
    returned = exchange(returned, "tm")

    year_dual, year = call(
        functools.partial(second_kernel, units, scale, bound),
        (struct(regions, width), struct(blocks, year_rows)),
        "second_primal",
        [rows(year_rows)],
    )(omega, year, cost, back, upper, annual_cap)
    year = exchange(year, "tm")
    year = call(sum_rows_with_stored_kernel, struct(blocks, year_rows), "year_sum_2")(year, stored_year)
    year = exchange(year, "tm")

    ends = bus[:, n:].reshape(groups, 3, lines).transpose(1, 0, 2).reshape(3, groups * lines)
    bus = bus[:, :n].reshape(groups * regions, hours)
    new_primal, flows, new_prices, storage_dual = call(
        functools.partial(last_kernel, units),
        (
            struct(regions, hours, width, dtype=BF16),
            struct(hours, lines),
            struct(n, bus_rows),
            struct(n, units),
        ),
        "second_prices",
        [pltpu.VMEM((n, width), F32)],
        in_specs=[smem] + [vmem] * 14,
        flops=3000000000,
        nbytes=6000000,
    )(
        region_place, omega, cost, back, upper, year_dual, returned, conversion, demand, prices, bus,
        ends[:2].astype(jnp.int32), ends[2:], line_ends.T, line_cap.reshape(1, -1),
    )
    year_dual = call(functools.partial(year_kernel, bound), struct(regions, width), "year_dual")(
        omega, year, year_dual, annual_cap
    )
    turn = lambda x, last: jnp.transpose(x.reshape(regions, hours, last), (1, 0, 2))
    return (
        jnp.transpose(new_primal, (1, 0, 2)),
        flows,
        turn(new_prices, bus_rows),
        turn(storage_dual, units),
        year_dual,
    )


def solution(mesh):
    in_specs = (
        P("tm", "region", None),
        P("tm", "region", None),
        P(),
        P("region", None),
        P("tm", "region", None),
        P("region", None),
        P("region", None),
        P("region", None),
        P("region"),
    )
    out_specs = (
        P("tm", "region", None),
        P("tm", "region"),
        P("tm", "region", None),
        P("tm", "region", None),
        P("region", None),
    )
    return jax.shard_map(
        per_device, mesh=mesh, in_specs=in_specs, out_specs=out_specs, check_vma=False
    )
```

```python
import functools
import math

import jax
import jax.numpy as jnp
from jax import lax
from jax.experimental import pallas as pl
from jax.experimental.pallas import tpu as pltpu
from jax.sharding import PartitionSpec as P

F32 = jnp.float32
BF16 = jnp.bfloat16
LANES = 128
PAD_ROWS = 16
step_ratio = 0.5


def call(kernel, out_shape, name, scratch=(), in_specs=None, flops=1000000, nbytes=1000000):
    specs = {} if in_specs is None else {"in_specs": in_specs}
    return pl.pallas_call(
        kernel,
        out_shape=out_shape,
        **specs,
        scratch_shapes=list(scratch),
        name=name,
        compiler_params=pltpu.CompilerParams(vmem_limit_bytes=24 * 1024 * 1024),
        cost_estimate=pl.CostEstimate(flops=flops, bytes_accessed=nbytes, transcendentals=0),
    )


def struct(*shape, dtype=F32):
    return jax.ShapeDtypeStruct(shape, dtype)


def lane_ids(shape):
    return lax.broadcasted_iota(jnp.int32, shape, len(shape) - 1)


def swap_halves(x):
    return pltpu.roll(x, LANES // 2, 1)


def spread(scratch):
    return jnp.transpose(scratch)[: LANES // 2, :]


def put_pieces(out_ref, first, per, value):
    for q in range(value.shape[1] // LANES):
        out_ref[pl.ds(first + q, LANES // 2, stride=per), :] = value[:, q * LANES : (q + 1) * LANES]


def move_pieces(out_ref, first, per, in_ref):
    count = in_ref.shape[0] // (LANES // 2)
    for q in range(count):
        out_ref[pl.ds(first + q, LANES // 2, stride=per), :] = in_ref[pl.ds(q, LANES // 2, stride=count), :]


def collect(ref, first, count):
    per = ref.shape[0] // (LANES // 2)
    parts = []
    for q in range(first, first + count):
        rows = ref[pl.ds(q, LANES // 2, stride=per), :]
        parts.append(jnp.transpose(jnp.concatenate([rows, jnp.zeros_like(rows)], axis=0)))
    return jnp.concatenate(parts, axis=0)


def sum_pieces(ref, count):
    per = ref.shape[0] // (LANES // 2)
    return [jnp.sum(ref[pl.ds(q, LANES // 2, stride=per), :], axis=0, keepdims=True) for q in range(count)]


def split(x):
    high = x.astype(BF16)
    return high, (x - high.astype(F32)).astype(BF16)


def dot(a, b, dims):
    return lax.dot_general(a, b, (dims, ((), ())), preferred_element_type=F32)


def dot3(a, b, dims):
    (ah, al), (bh, bl) = a, b
    return dot(ah, bh, dims) + (dot(ah, bl, dims) + dot(al, bh, dims))


def bounds(upper_row, units):
    return jnp.where(lane_ids(upper_row.shape) < units, -upper_row, 0.0), upper_row


def clip(x, low, high):
    return jnp.minimum(jnp.maximum(x, low), high)


def sums_kernel(cost_ref, demand_ref, out_ref):
    regions = cost_ref.shape[0]

    def total(ref):
        acc = None
        for r in range(regions):
            x = ref[r].astype(F32)
            acc = x * x if acc is None else acc + x * x
        return jnp.sum(jnp.sum(acc, axis=0, keepdims=True), axis=1, keepdims=True)

    ids = lane_ids((1, LANES))
    row = jnp.where(ids == 0, total(cost_ref), jnp.where(ids == 1, total(demand_ref), 0.0))
    out_ref[...] = row


def turn_kernel(cost_ref, decay_ref, out_ref, rows):
    regions, hours, units = decay_ref.shape
    n = regions * hours
    costs = cost_ref[:, :, :units].astype(F32).reshape(n, units)
    decay = decay_ref[...].reshape(n, units)
    for place, x in enumerate((costs, swap_halves(costs), decay, swap_halves(decay))):
        rows[place * n : (place + 1) * n, :] = x
    put_pieces(out_ref, 0, out_ref.shape[0] // (LANES // 2), spread(rows[...]))


def year_pieces(rows, out_ref):
    half = rows.shape[0] // 2
    rows[half:, :] = swap_halves(rows[:half, :])
    put_pieces(out_ref, 0, out_ref.shape[0] // (LANES // 2), spread(rows[...]))


def year_totals(received_ref, count, regions):
    x = collect(received_ref, 0, count)
    half = x.shape[0] // 2
    tiles = []
    for t in range(half // PAD_ROWS):
        at = t * PAD_ROWS
        tile = x[at : at + PAD_ROWS, :] + swap_halves(x[half + at : half + at + PAD_ROWS, :])
        tiles.append(tile[:regions, :])
    return tiles


def first_kernel(units, year_scale, sums_ref, cost_ref, upper_ref, turned_ref, omega_ref, out_ref, rows):
    regions, hours, width = cost_ref.shape
    s = jnp.sum(sums_ref[...], axis=0, keepdims=True)
    ids = lane_ids(s.shape)
    cost_sum = jnp.sum(jnp.where(ids == 0, s, 0.0), axis=1, keepdims=True)
    load_sum = jnp.sum(jnp.where(ids == 1, s, 0.0), axis=1, keepdims=True)
    omega = jnp.sqrt(cost_sum / load_sum)
    omega_ref[...] = jnp.broadcast_to(omega, omega_ref.shape)
    tau = step_ratio / omega
    rows[...] = jnp.zeros_like(rows)
    for r in range(regions):
        low, high = bounds(upper_ref[r : r + 1, :], units)
        primal = clip(-tau * cost_ref[r].astype(F32), low, high)
        sums = (2.0 * year_scale) * jnp.sum(primal, axis=0, keepdims=True)
        for t in range(width // LANES):
            rows[t * PAD_ROWS + r : t * PAD_ROWS + r + 1, :] = sums[:, t * LANES : (t + 1) * LANES]
    year_pieces(rows, out_ref)
    move_pieces(out_ref, rows.shape[0] // LANES, out_ref.shape[0] // (LANES // 2), turned_ref)


def prices_kernel(
    units, omega_ref, cost_ref, upper_ref, demand_ref, conversion_ref, ends_ref,
    prices_ref, back_ref, turned_ref, bus_ref, bar, rows,
):
    regions, hours, width = cost_ref.shape
    bus_rows = demand_ref.shape[2]
    n = regions * hours
    omega = omega_ref[0:1, 0:1]
    tau, sigma = step_ratio / omega, step_ratio * omega
    for r in range(regions):
        low, high = bounds(upper_ref[r : r + 1, :], units)
        bar[r * hours : (r + 1) * hours, :] = 2.0 * clip(-tau * cost_ref[r].astype(F32), low, high)
    step = 256
    image = None
    for k in range(0, width, step):
        part = dot3(split(bar[:, k : k + step]), split(conversion_ref[k : k + step, :]), ((1,), (0,)))
        image = part if image is None else image + part
    loads = demand_ref[...].astype(F32).reshape(n, bus_rows)
    prices = sigma * (image - loads)
    prices_ref[...] = prices
    cut = split(prices)
    for k in range(0, width, step):
        back_ref[:, k : k + step] = dot3(cut, split(conversion_ref[k : k + step, :]), ((1,), (1,)))
    stored = back_ref[:, :units]
    rows[:n, :] = stored
    rows[n : 2 * n, :] = swap_halves(stored)
    rows[2 * n :, :] = jnp.zeros_like(rows[2 * n :, :])
    put_pieces(turned_ref, 0, turned_ref.shape[0] // (LANES // 2), spread(rows[...]))
    bus = jnp.transpose(prices[:, :LANES])[0:1, :]
    ends = ends_ref[...]
    row = jnp.concatenate([bus, jnp.zeros((1, ends.shape[1] - n), F32)], axis=1) + ends
    bus_ref[...] = row


def sum_kernel(count, received_ref, added_ref, out_ref):
    per = out_ref.shape[0] // (LANES // 2)
    for q, total in enumerate(sum_pieces(received_ref, count)):
        out_ref[pl.ds(q, LANES // 2, stride=per), :] = jnp.broadcast_to(total, (LANES // 2, LANES))
    move_pieces(out_ref, count, per, added_ref)


def sum_with_stored_kernel(count, received_ref, stored_ref, added_ref, out_ref):
    per = out_ref.shape[0] // (LANES // 2)
    for q, total in enumerate(sum_pieces(received_ref, count)):
        if q % (count // 2) == 0:
            stored = stored_ref[0:1, (q // (count // 2)) * LANES : (q // (count // 2) + 1) * LANES]
            total = jnp.where(lane_ids(total.shape) < PAD_ROWS, stored, total)
        out_ref[pl.ds(q, LANES // 2, stride=per), :] = jnp.broadcast_to(total, (LANES // 2, LANES))
    move_pieces(out_ref, count, per, added_ref)


def before(x, k, reverse):
    ids = lax.rem(lane_ids(x.shape), LANES // 2)
    if reverse:
        return pltpu.roll(x, LANES - k, 1), ids < LANES // 2 - k
    return pltpu.roll(x, k, 1), ids >= k


def carry_in(scale, offset, reverse):
    k = 1
    while k < LANES // 2:
        scale_before, ok = before(scale, k, reverse)
        offset_before, _ = before(offset, k, reverse)
        offset = jnp.where(ok, scale * offset_before + offset, offset)
        scale = jnp.where(ok, scale * scale_before, scale)
        k *= 2
    entering, ok = before(offset, 1, reverse)
    return jnp.where(ok, entering, 0.0)


def storage_kernel(
    count, level_scale, year_scale, year_bound,
    place_ref, omega_ref, turned_ref, back_ref, upper_ref, energy_ref, annual_ref,
    out_ref, year_ref, costs, decay, back, run, scale, dual, primal, suffix, suffix_scale, rows,
):
    regions, units = energy_ref.shape
    n = costs.shape[0]
    hours = n // regions
    place = place_ref[0]
    omega = omega_ref[0:1, 0:1]
    tau, sigma = step_ratio / omega, step_ratio * omega
    ids = lane_ids((regions, units))
    left = ids < units // 2

    def pair(x):
        first = jnp.sum(jnp.where(ids == place, x, 0.0), axis=1, keepdims=True)
        second = jnp.sum(jnp.where(ids == place + units // 2, x, 0.0), axis=1, keepdims=True)
        return jnp.where(left, first, second)

    def halves(x):
        first = jnp.sum(jnp.where(left, x, 0.0), axis=1, keepdims=True)
        second = jnp.sum(jnp.where(left, 0.0, x), axis=1, keepdims=True)
        return first, second

    high = pair(upper_ref[:, :units])
    energy = pair(energy_ref[...])
    annual = pair(annual_ref[:, :units])
    x = collect(turned_ref, count, 4 * n // LANES)
    costs[...] = x[:n] + swap_halves(x[n : 2 * n])
    decay[...] = x[2 * n : 3 * n] + swap_halves(x[3 * n :])
    x = collect(back_ref, count, -(-2 * n // LANES))
    back[...] = x[:n] + swap_halves(x[n : 2 * n])

    def get(ref, h):
        return ref[pl.ds(h, regions, stride=hours), :]

    def put(ref, h, value):
        ref[pl.ds(h, regions, stride=hours), :] = value

    def first_primal(h):
        return clip(-tau * get(costs, h), -high, high)

    level = jnp.zeros((regions, units), F32)
    kept = jnp.ones((regions, units), F32)
    year = jnp.zeros((regions, units), F32)
    for h in range(hours):
        d = get(decay, h)
        bar = 2.0 * first_primal(h)
        year = year + bar
        level = d * level + bar
        kept = kept * d
        put(run, h, level)
        put(scale, h, kept)
    entering = carry_in(kept, level, False)
    first, second = halves(year)
    year_total = year_scale * jnp.where(left, first, second)
    year_dual = jnp.maximum(sigma * (year_total - year_bound * annual), 0.0)
    after = jnp.zeros((regions, units), F32)
    after_kept = jnp.ones((regions, units), F32)
    for h in reversed(range(hours)):
        d = get(decay, h)
        level = get(run, h) + get(scale, h) * entering
        stored = jnp.maximum(sigma * (level_scale * level - energy), 0.0)
        put(dual, h, stored)
        after = d * (level_scale * stored + after)
        after_kept = after_kept * d
        put(suffix, h, after)
        put(suffix_scale, h, after_kept)
    closing = carry_in(after_kept, after, True)
    level = jnp.zeros((regions, units), F32)
    year = jnp.zeros((regions, units), F32)
    for h in range(hours):
        later = closing if h == hours - 1 else get(suffix, h + 1) + get(suffix_scale, h + 1) * closing
        grad = get(costs, h) + get(back, h) + (level_scale * get(dual, h) + later) + year_scale * year_dual
        old = first_primal(h)
        new = clip(old - tau * grad, -high, high)
        put(primal, h, new)
        bar = 2.0 * new - old
        year = year + bar
        level = get(decay, h) * level + bar
        put(run, h, level)
    entering = carry_in(kept, level, False)
    for h in range(hours):
        level = get(run, h) + get(scale, h) * entering
        put(dual, h, jnp.maximum(get(dual, h) + sigma * (level_scale * level - energy), 0.0))
    rows[:n, :] = primal[...]
    rows[n : 2 * n, :] = swap_halves(primal[...])
    rows[2 * n : 3 * n, :] = dual[...]
    rows[3 * n :, :] = swap_halves(dual[...])
    put_pieces(out_ref, 0, out_ref.shape[0] // (LANES // 2), spread(rows[...]))
    diagonal = lax.broadcasted_iota(jnp.int32, (regions, units), 0) == ids
    for part, column in enumerate(halves(year)):
        line = jnp.sum(jnp.where(diagonal, year_scale * column, 0.0), axis=0, keepdims=True)
        year_ref[:, part * LANES : (part + 1) * LANES] = jnp.broadcast_to(line, (year_ref.shape[0], LANES))


def second_kernel(
    units, year_scale, year_bound,
    omega_ref, year_ref, cost_ref, back_ref, upper_ref, annual_ref,
    dual_ref, out_ref, rows,
):
    regions, hours, width = cost_ref.shape
    omega = omega_ref[0:1, 0:1]
    tau, sigma = step_ratio / omega, step_ratio * omega
    for t, total in enumerate(year_totals(year_ref, rows.shape[0] // LANES, regions)):
        at = slice(t * LANES, (t + 1) * LANES)
        dual_ref[:, at] = jnp.maximum(sigma * (total - year_bound * annual_ref[:, at]), 0.0)
    rows[...] = jnp.zeros_like(rows)
    for r in range(regions):
        high = upper_ref[r : r + 1, units:]
        costs = cost_ref[r, :, units:].astype(F32)
        old = clip(-tau * costs, 0.0, high)
        grad = costs + back_ref[r * hours : (r + 1) * hours, units:] + year_scale * dual_ref[r : r + 1, units:]
        bar = 2.0 * clip(old - tau * grad, 0.0, high) - old
        sums = year_scale * jnp.sum(bar, axis=0, keepdims=True)
        for t in range(1, width // LANES):
            rows[t * PAD_ROWS + r : t * PAD_ROWS + r + 1, :] = sums[:, t * LANES - units : (t + 1) * LANES - units]
    year_pieces(rows, out_ref)


def last_kernel(
    units, year_scale, place_ref, omega_ref, cost_ref, back_ref, upper_ref, dual_ref, conversion_ref,
    demand_ref, prices_ref, bus_ref, ends_ref, caps_ref,
    primal_ref, flows_ref, new_prices_ref, bar,
):
    regions, hours, width = cost_ref.shape
    bus_rows = demand_ref.shape[2]
    lines = flows_ref.shape[1]
    n = regions * hours
    omega = omega_ref[0:1, 0:1]
    tau, sigma = step_ratio / omega, step_ratio * omega
    bar[:, :units] = jnp.zeros((n, units), F32)
    for r in range(regions):
        at = slice(r * hours, (r + 1) * hours)
        high = upper_ref[r : r + 1, units:]
        costs = cost_ref[r, :, units:].astype(F32)
        old = clip(-tau * costs, 0.0, high)
        grad = costs + back_ref[at, units:] + year_scale * dual_ref[r : r + 1, units:]
        new = clip(old - tau * grad, 0.0, high)
        bar[at, units:] = 2.0 * new - old
        primal_ref[r, :, :units] = jnp.zeros((hours, units), BF16)
        primal_ref[r, :, units:] = new.astype(BF16)
    step = 256
    image = None
    for k in range(0, width, step):
        part = dot3(split(bar[:, k : k + step]), split(conversion_ref[k : k + step, :]), ((1,), (0,)))
        image = part if image is None else image + part
    loads = demand_ref[...].astype(F32).reshape(n, bus_rows)
    new_prices_ref[...] = prices_ref[...] + sigma * (image - loads)

    regions_all = bus_ref.shape[0]
    first_region = place_ref[0] * regions

    def exact(a, b, dims):
        return lax.dot_general(
            a, b, (dims, ((), ())), precision=lax.Precision.HIGHEST, preferred_element_type=F32
        )

    def incidence(count):
        ids = lax.broadcasted_iota(jnp.int32, (count, ends_ref.shape[1]), 0) + first_region
        ids = jnp.where(ids >= regions_all, ids - regions_all, ids)
        return (ids == ends_ref[1:2, :]).astype(F32) - (ids == ends_ref[0:1, :]).astype(F32)

    caps = caps_ref[...]
    flows = clip(-tau * exact(bus_ref[...], incidence(regions_all), ((0,), (0,))), -caps, caps)
    flows_ref[...] = flows[:, :lines]
    inflow = exact(2.0 * flows, incidence(LANES), ((1,), (1,)))
    ids = lane_ids(inflow.shape)
    for r in range(regions):
        moved = inflow if r == 0 else pltpu.roll(inflow, LANES - r, 1)
        at = slice(r * hours, (r + 1) * hours)
        new_prices_ref[at, :LANES] = new_prices_ref[at, :LANES] + sigma * jnp.where(ids == 0, moved, 0.0)


def finish_kernel(
    count, year_bound, omega_ref, received_ref, cost_ref, upper_ref, conversion_ref, prices_ref, primal_ref,
    dual_ref, annual_ref, new_primal_ref, new_prices_ref, storage_ref, year_ref, bar,
):
    regions, hours, units = cost_ref.shape
    n = regions * hours
    omega = omega_ref[0:1, 0:1]
    tau, sigma = step_ratio / omega, step_ratio * omega
    for t, total in enumerate(year_totals(received_ref, count, regions)):
        at = slice(t * LANES, (t + 1) * LANES)
        year_ref[:, at] = jnp.maximum(dual_ref[:, at] + sigma * (total - year_bound * annual_ref[:, at]), 0.0)
    x = collect(received_ref, count, 4 * n // LANES)
    storage_ref[...] = x[2 * n : 3 * n] + swap_halves(x[3 * n :])
    stored = x[:n] + swap_halves(x[n : 2 * n])
    for r in range(regions):
        at = slice(r * hours, (r + 1) * hours)
        high = upper_ref[r : r + 1, :units]
        new = stored[at]
        new_primal_ref[r, :, :units] = new.astype(BF16)
        new_primal_ref[r, :, units:] = primal_ref[r, :, units:]
        bar[at, :] = 2.0 * new - clip(-tau * cost_ref[r].astype(F32), -high, high)
    image = dot3(split(bar[...]), split(conversion_ref[:units, :]), ((1,), (0,)))
    new_prices_ref[...] = prices_ref[...] + sigma * image


def exchange(x):
    blocks = lax.axis_size("tm")
    pieces = x.reshape(blocks, 1, x.size // blocks)
    return lax.all_to_all(pieces, "tm", 0, 0, tiled=True).reshape(x.shape)


def sum_over_all(row):
    blocks, groups = lax.axis_size("tm"), lax.axis_size("region")
    pairs = [[2 * k, 2 * k + 1] for k in range(blocks // 2)]
    pair = jnp.sum(lax.all_gather(row, "tm", axis=0, axis_index_groups=pairs, tiled=True), axis=0, keepdims=True)
    half = blocks * groups // 2
    cores = [[(2 * k + core) * groups + z for k in range(blocks // 2) for z in range(groups)] for core in range(2)]
    pieces = jnp.broadcast_to(pair[:, None, :], (half, 1, LANES))
    return lax.all_to_all(
        pieces, ("tm", "region"), 0, 0, tiled=True, axis_index_groups=cores
    ).reshape(half, LANES)


def per_device(cost, demand, conversion, upper, decay, energy_cap, annual_cap, line_ends, line_cap):
    hours, regions, width = cost.shape
    bus_rows = demand.shape[2]
    units = decay.shape[2]
    lines = line_ends.shape[0]
    blocks = lax.axis_size("tm")
    groups = lax.axis_size("region")
    hours_all = hours * blocks
    scale = 1.0 / math.sqrt(hours_all)
    bound = math.sqrt(hours_all)
    n = regions * hours
    year_rows = 2 * PAD_ROWS * (width // LANES)
    year_count = year_rows // LANES
    turned_count = 4 * n // LANES
    back_count = -(-2 * n // LANES)
    smem = pl.BlockSpec(memory_space=pltpu.SMEM)
    vmem = pl.BlockSpec(memory_space=pltpu.VMEM)
    rows = lambda k: pltpu.VMEM((k, LANES), F32)
    pieces = lambda count: struct(blocks * count, LANES)
    cost = jnp.transpose(cost, (1, 0, 2))
    demand = jnp.transpose(demand, (1, 0, 2))
    decay = jnp.transpose(decay, (1, 0, 2))
    tm_place = lax.axis_index("tm").astype(jnp.int32).reshape(1)
    region_place = lax.axis_index("region").astype(jnp.int32).reshape(1)

    sums = sum_over_all(call(sums_kernel, struct(1, LANES), "sums")(cost, demand))
    turned = call(turn_kernel, pieces(turned_count), "turn", [rows(4 * n)])(cost, decay)
    omega, first = call(
        functools.partial(first_kernel, units, scale),
        (struct(8, LANES), pieces(year_count + turned_count)),
        "first_primal",
        [rows(year_rows)],
    )(sums, cost, upper, turned)
    first = exchange(first)

    ends_t = line_ends.T.astype(F32)
    own = jnp.concatenate([jnp.zeros((1, n), F32), ends_t.reshape(1, -1), line_cap.reshape(1, -1)], axis=1)
    prices, back, back_turned, bus = call(
        functools.partial(prices_kernel, units),
        (struct(n, bus_rows), struct(n, width), pieces(back_count), struct(1, own.shape[1])),
        "first_prices",
        [pltpu.VMEM((n, width), F32), rows(back_count * LANES)],
        flops=4000000000,
        nbytes=5000000,
    )(omega, cost, upper, demand, conversion, own)

    second = call(
        functools.partial(sum_kernel, year_count), pieces(year_count + back_count), "year_sum"
    )(first, back_turned)
    second = exchange(second)

    year_dual, third = call(
        functools.partial(second_kernel, units, scale, bound),
        (struct(regions, width), pieces(year_count)),
        "second_primal",
        [rows(year_rows)],
    )(omega, second, cost, back, upper, annual_cap)
    third = exchange(third)

    returned, stored_year = call(
        functools.partial(storage_kernel, year_count, scale, scale, bound),
        (pieces(turned_count), struct(8, year_rows)),
        "storage",
        [rows(n) for _ in range(9)] + [rows(4 * n)],
        in_specs=[smem] + [vmem] * 6,
        flops=4000000000,
    )(tm_place, omega, first, second, upper, energy_cap, annual_cap)

    fourth = call(
        functools.partial(sum_with_stored_kernel, year_count), pieces(year_count + turned_count), "year_sum_2"
    )(third, stored_year, returned)
    fourth = exchange(fourth)

    reach = 1
    while reach < groups:
        came = lax.ppermute(bus, "region", [((z + reach) % groups, z) for z in range(groups)])
        bus = jnp.concatenate([bus, came], axis=0)
        reach *= 2
    ends = bus[:, n:].reshape(groups, 3, lines).transpose(1, 0, 2).reshape(3, groups * lines)
    bus = bus[:, :n].reshape(groups * regions, hours)
    primal, flows, prices = call(
        functools.partial(last_kernel, units, scale),
        (struct(regions, hours, width, dtype=BF16), struct(hours, lines), struct(n, bus_rows)),
        "second_prices",
        [pltpu.VMEM((n, width), F32)],
        in_specs=[smem] + [vmem] * 11,
        flops=3000000000,
        nbytes=6000000,
    )(
        region_place, omega, cost, back, upper, year_dual, conversion, demand, prices, bus,
        ends[:2].astype(jnp.int32), ends[2:],
    )
    new_primal, prices, storage_dual, year_dual = call(
        functools.partial(finish_kernel, year_count, bound),
        (
            struct(regions, hours, width, dtype=BF16),
            struct(n, bus_rows),
            struct(n, units),
            struct(regions, width),
        ),
        "finish",
        [rows(n)],
    )(omega, fourth, cost[:, :, :units], upper, conversion, prices, primal, year_dual, annual_cap)
    turn = lambda x, last: jnp.transpose(x.reshape(regions, hours, last), (1, 0, 2))
    return (
        jnp.transpose(new_primal, (1, 0, 2)),
        flows,
        turn(prices, bus_rows),
        turn(storage_dual, units),
        year_dual,
    )


def solution(mesh):
    in_specs = (
        P("tm", "region", None),
        P("tm", "region", None),
        P(),
        P("region", None),
        P("tm", "region", None),
        P("region", None),
        P("region", None),
        P("region", None),
        P("region"),
    )
    out_specs = (
        P("tm", "region", None),
        P("tm", "region"),
        P("tm", "region", None),
        P("tm", "region", None),
        P("region", None),
    )
    return jax.shard_map(
        per_device, mesh=mesh, in_specs=in_specs, out_specs=out_specs, check_vma=False
    )
```

```python
import functools
import math

import jax
import jax.numpy as jnp
from jax import lax
from jax.experimental import pallas as pl
from jax.experimental.pallas import tpu as pltpu
from jax.sharding import PartitionSpec as P

F32 = jnp.float32
BF16 = jnp.bfloat16
LANES = 128
PAD_ROWS = 16
step_ratio = 0.5


VMEM = pl.BlockSpec(memory_space=pltpu.VMEM)
SMEM = pl.BlockSpec(memory_space=pltpu.SMEM)
HBM = pl.BlockSpec(memory_space=pltpu.HBM)


def call(kernel, out_shape, name, in_specs, scratch=(), out_specs=None, aliases=None, flops=1000000, nbytes=1000000):
    if out_specs is None:
        out_specs = jax.tree.map(lambda _: VMEM, out_shape)
    return pl.pallas_call(
        kernel,
        out_shape=out_shape,
        in_specs=in_specs,
        out_specs=out_specs,
        scratch_shapes=list(scratch),
        name=name,
        input_output_aliases=aliases or {},
        compiler_params=pltpu.CompilerParams(vmem_limit_bytes=24 * 1024 * 1024),
        cost_estimate=pl.CostEstimate(flops=flops, bytes_accessed=nbytes, transcendentals=0),
    )


def struct(*shape, dtype=F32):
    return jax.ShapeDtypeStruct(shape, dtype)


def begin(source, target, sem):
    copy = pltpu.make_async_copy(source, target, sem)
    copy.start()
    return copy


def lane_ids(shape):
    return lax.broadcasted_iota(jnp.int32, shape, len(shape) - 1)


def swap_halves(x):
    return pltpu.roll(x, LANES // 2, 1)


def spread(scratch):
    return jnp.transpose(scratch)[: LANES // 2, :]


def put_pieces(out_ref, first, per, value):
    for q in range(value.shape[1] // LANES):
        out_ref[pl.ds(first + q, LANES // 2, stride=per), :] = value[:, q * LANES : (q + 1) * LANES]


def move_pieces(out_ref, first, per, in_ref):
    count = in_ref.shape[0] // (LANES // 2)
    for q in range(count):
        out_ref[pl.ds(first + q, LANES // 2, stride=per), :] = in_ref[pl.ds(q, LANES // 2, stride=count), :]


def collect(ref, first, count):
    per = ref.shape[0] // (LANES // 2)
    parts = []
    for q in range(first, first + count):
        rows = ref[pl.ds(q, LANES // 2, stride=per), :]
        parts.append(jnp.transpose(jnp.concatenate([rows, jnp.zeros_like(rows)], axis=0)))
    return jnp.concatenate(parts, axis=0)


def sum_pieces(ref, count):
    per = ref.shape[0] // (LANES // 2)
    return [jnp.sum(ref[pl.ds(q, LANES // 2, stride=per), :], axis=0, keepdims=True) for q in range(count)]


def split(x):
    high = x.astype(BF16)
    return high, (x - high.astype(F32)).astype(BF16)


def dot(a, b, dims):
    return lax.dot_general(a, b, (dims, ((), ())), preferred_element_type=F32)


def dot3(a, b, dims):
    (ah, al), (bh, bl) = a, b
    return dot(ah, bh, dims) + (dot(ah, bl, dims) + dot(al, bh, dims))


def bounds(upper_row, units):
    return jnp.where(lane_ids(upper_row.shape) < units, -upper_row, 0.0), upper_row


def clip(x, low, high):
    return jnp.minimum(jnp.maximum(x, low), high)


def sums_kernel(cost_ref, demand_ref, out_ref):
    regions = cost_ref.shape[0]

    def total(ref):
        acc = None
        for r in range(regions):
            x = ref[r].astype(F32)
            acc = x * x if acc is None else acc + x * x
        return jnp.sum(jnp.sum(acc, axis=0, keepdims=True), axis=1, keepdims=True)

    ids = lane_ids((1, LANES))
    row = jnp.where(ids == 0, total(cost_ref), jnp.where(ids == 1, total(demand_ref), 0.0))
    out_ref[...] = row


def turn_kernel(cost_ref, decay_ref, out_ref, rows):
    regions, hours, units = decay_ref.shape
    n = regions * hours
    costs = cost_ref[:, :, :units].astype(F32).reshape(n, units)
    decay = decay_ref[...].reshape(n, units)
    for place, x in enumerate((costs, swap_halves(costs), decay, swap_halves(decay))):
        rows[place * n : (place + 1) * n, :] = x
    put_pieces(out_ref, 0, out_ref.shape[0] // (LANES // 2), spread(rows[...]))


def year_pieces(rows, out_ref):
    half = rows.shape[0] // 2
    rows[half:, :] = swap_halves(rows[:half, :])
    put_pieces(out_ref, 0, out_ref.shape[0] // (LANES // 2), spread(rows[...]))


def year_totals(received_ref, count, regions):
    x = collect(received_ref, 0, count)
    half = x.shape[0] // 2
    tiles = []
    for t in range(half // PAD_ROWS):
        at = t * PAD_ROWS
        tile = x[at : at + PAD_ROWS, :] + swap_halves(x[half + at : half + at + PAD_ROWS, :])
        tiles.append(tile[:regions, :])
    return tiles


def first_kernel(
    units, year_scale, sums_ref, cost_ref, upper_ref, turned_ref, omega_ref, sent_ref, out_ref, rows, sems
):
    regions, hours, width = cost_ref.shape
    s = jnp.sum(sums_ref[...], axis=0, keepdims=True)
    ids = lane_ids(s.shape)
    cost_sum = jnp.sum(jnp.where(ids == 0, s, 0.0), axis=1, keepdims=True)
    load_sum = jnp.sum(jnp.where(ids == 1, s, 0.0), axis=1, keepdims=True)
    omega = jnp.sqrt(cost_sum / load_sum)
    omega_ref[...] = jnp.broadcast_to(omega, omega_ref.shape)
    tau = step_ratio / omega
    rows[...] = jnp.zeros_like(rows)
    for r in range(regions):
        low, high = bounds(upper_ref[r : r + 1, :], units)
        primal = clip(-tau * cost_ref[r].astype(F32), low, high)
        sums = (2.0 * year_scale) * jnp.sum(primal, axis=0, keepdims=True)
        for t in range(width // LANES):
            rows[t * PAD_ROWS + r : t * PAD_ROWS + r + 1, :] = sums[:, t * LANES : (t + 1) * LANES]
    year_pieces(rows, out_ref)
    move_pieces(out_ref, rows.shape[0] // LANES, out_ref.shape[0] // (LANES // 2), turned_ref)
    begin(out_ref, sent_ref, sems.at[0]).wait()


def prices_kernel(
    units, omega_ref, cost_ref, upper_ref, demand_ref, conversion_ref, ends_ref,
    prices_ref, back_ref, turned_ref, bus_ref, bar, rows, held, sems,
):
    copy = begin(conversion_ref, held, sems.at[0])
    regions, hours, width = cost_ref.shape
    bus_rows = demand_ref.shape[2]
    n = regions * hours
    omega = omega_ref[0:1, 0:1]
    tau, sigma = step_ratio / omega, step_ratio * omega
    for r in range(regions):
        low, high = bounds(upper_ref[r : r + 1, :], units)
        bar[r * hours : (r + 1) * hours, :] = 2.0 * clip(-tau * cost_ref[r].astype(F32), low, high)
    copy.wait()
    step = 256
    image = None
    for k in range(0, width, step):
        part = dot3(split(bar[:, k : k + step]), split(held[k : k + step, :]), ((1,), (0,)))
        image = part if image is None else image + part
    loads = demand_ref[...].astype(F32).reshape(n, bus_rows)
    prices = sigma * (image - loads)
    prices_ref[...] = prices
    cut = split(prices)
    for k in range(0, width, step):
        back_ref[:, k : k + step] = dot3(cut, split(held[k : k + step, :]), ((1,), (1,)))
    stored = back_ref[:, :units]
    rows[:n, :] = stored
    rows[n : 2 * n, :] = swap_halves(stored)
    rows[2 * n :, :] = jnp.zeros_like(rows[2 * n :, :])
    put_pieces(turned_ref, 0, turned_ref.shape[0] // (LANES // 2), spread(rows[...]))
    bus = jnp.transpose(prices[:, :LANES])[0:1, :]
    ends = ends_ref[...]
    row = jnp.concatenate([bus, jnp.zeros((1, ends.shape[1] - n), F32)], axis=1) + ends
    bus_ref[...] = row


def sum_kernel(count, received_ref, added_ref, bus_ref, came_ref, sent_ref, grown_ref, out_ref, sems):
    per = out_ref.shape[0] // (LANES // 2)
    for q, total in enumerate(sum_pieces(received_ref, count)):
        out_ref[pl.ds(q, LANES // 2, stride=per), :] = jnp.broadcast_to(total, (LANES // 2, LANES))
    move_pieces(out_ref, count, per, added_ref)
    copy = begin(out_ref, sent_ref, sems.at[0])
    grow(bus_ref, came_ref, grown_ref)
    copy.wait()


def grow(bus_ref, came_ref, grown_ref):
    grown_ref[: bus_ref.shape[0], :] = bus_ref[...]
    grown_ref[bus_ref.shape[0] :, :] = came_ref[...]


def sum_with_stored_kernel(
    count, received_ref, stored_ref, added_ref, bus_ref, came_ref, sent_ref, grown_ref, out_ref, sems
):
    per = out_ref.shape[0] // (LANES // 2)
    for q, total in enumerate(sum_pieces(received_ref, count)):
        if q % (count // 2) == 0:
            stored = stored_ref[0:1, (q // (count // 2)) * LANES : (q // (count // 2) + 1) * LANES]
            total = jnp.where(lane_ids(total.shape) < PAD_ROWS, stored, total)
        out_ref[pl.ds(q, LANES // 2, stride=per), :] = jnp.broadcast_to(total, (LANES // 2, LANES))
    move_pieces(out_ref, count, per, added_ref)
    copy = begin(out_ref, sent_ref, sems.at[0])
    grow(bus_ref, came_ref, grown_ref)
    copy.wait()


def before(x, k, reverse):
    ids = lax.rem(lane_ids(x.shape), LANES // 2)
    if reverse:
        return pltpu.roll(x, LANES - k, 1), ids < LANES // 2 - k
    return pltpu.roll(x, k, 1), ids >= k


def carry_in(scale, offset, reverse):
    k = 1
    while k < LANES // 2:
        scale_before, ok = before(scale, k, reverse)
        offset_before, _ = before(offset, k, reverse)
        offset = jnp.where(ok, scale * offset_before + offset, offset)
        scale = jnp.where(ok, scale * scale_before, scale)
        k *= 2
    entering, ok = before(offset, 1, reverse)
    return jnp.where(ok, entering, 0.0)


def storage_kernel(
    count, level_scale, year_scale, year_bound,
    place_ref, omega_ref, turned_ref, back_ref, upper_ref, energy_ref, annual_ref,
    out_ref, year_ref, costs, decay, back, run, scale, dual, primal, suffix, suffix_scale, rows,
):
    regions, units = energy_ref.shape
    n = costs.shape[0]
    hours = n // regions
    place = place_ref[0]
    omega = omega_ref[0:1, 0:1]
    tau, sigma = step_ratio / omega, step_ratio * omega
    ids = lane_ids((regions, units))
    left = ids < units // 2

    def pair(x):
        first = jnp.sum(jnp.where(ids == place, x, 0.0), axis=1, keepdims=True)
        second = jnp.sum(jnp.where(ids == place + units // 2, x, 0.0), axis=1, keepdims=True)
        return jnp.where(left, first, second)

    def halves(x):
        first = jnp.sum(jnp.where(left, x, 0.0), axis=1, keepdims=True)
        second = jnp.sum(jnp.where(left, 0.0, x), axis=1, keepdims=True)
        return first, second

    high = pair(upper_ref[:, :units])
    energy = pair(energy_ref[...])
    annual = pair(annual_ref[:, :units])
    x = collect(turned_ref, count, 4 * n // LANES)
    costs[...] = x[:n] + swap_halves(x[n : 2 * n])
    decay[...] = x[2 * n : 3 * n] + swap_halves(x[3 * n :])
    x = collect(back_ref, count, -(-2 * n // LANES))
    back[...] = x[:n] + swap_halves(x[n : 2 * n])

    def get(ref, h):
        return ref[pl.ds(h, regions, stride=hours), :]

    def put(ref, h, value):
        ref[pl.ds(h, regions, stride=hours), :] = value

    def first_primal(h):
        return clip(-tau * get(costs, h), -high, high)

    level = jnp.zeros((regions, units), F32)
    kept = jnp.ones((regions, units), F32)
    year = jnp.zeros((regions, units), F32)
    for h in range(hours):
        d = get(decay, h)
        bar = 2.0 * first_primal(h)
        year = year + bar
        level = d * level + bar
        kept = kept * d
        put(run, h, level)
        put(scale, h, kept)
    entering = carry_in(kept, level, False)
    first, second = halves(year)
    year_total = year_scale * jnp.where(left, first, second)
    year_dual = jnp.maximum(sigma * (year_total - year_bound * annual), 0.0)
    after = jnp.zeros((regions, units), F32)
    after_kept = jnp.ones((regions, units), F32)
    for h in reversed(range(hours)):
        d = get(decay, h)
        level = get(run, h) + get(scale, h) * entering
        stored = jnp.maximum(sigma * (level_scale * level - energy), 0.0)
        put(dual, h, stored)
        after = d * (level_scale * stored + after)
        after_kept = after_kept * d
        put(suffix, h, after)
        put(suffix_scale, h, after_kept)
    closing = carry_in(after_kept, after, True)
    level = jnp.zeros((regions, units), F32)
    year = jnp.zeros((regions, units), F32)
    for h in range(hours):
        later = closing if h == hours - 1 else get(suffix, h + 1) + get(suffix_scale, h + 1) * closing
        grad = get(costs, h) + get(back, h) + (level_scale * get(dual, h) + later) + year_scale * year_dual
        old = first_primal(h)
        new = clip(old - tau * grad, -high, high)
        put(primal, h, new)
        bar = 2.0 * new - old
        year = year + bar
        level = get(decay, h) * level + bar
        put(run, h, level)
    entering = carry_in(kept, level, False)
    for h in range(hours):
        level = get(run, h) + get(scale, h) * entering
        put(dual, h, jnp.maximum(get(dual, h) + sigma * (level_scale * level - energy), 0.0))
    rows[:n, :] = primal[...]
    rows[n : 2 * n, :] = swap_halves(primal[...])
    rows[2 * n : 3 * n, :] = dual[...]
    rows[3 * n :, :] = swap_halves(dual[...])
    put_pieces(out_ref, 0, out_ref.shape[0] // (LANES // 2), spread(rows[...]))
    diagonal = lax.broadcasted_iota(jnp.int32, (regions, units), 0) == ids
    for part, column in enumerate(halves(year)):
        line = jnp.sum(jnp.where(diagonal, year_scale * column, 0.0), axis=0, keepdims=True)
        year_ref[:, part * LANES : (part + 1) * LANES] = jnp.broadcast_to(line, (year_ref.shape[0], LANES))


def second_kernel(
    units, year_scale, year_bound,
    omega_ref, received_ref, cost_ref, back_ref, upper_ref, annual_ref, bus_ref, came_ref,
    sent_ref, dual_ref, grown_ref, rows, annual, dual, out, sems,
):
    coming = begin(annual_ref, annual, sems.at[0])
    regions, hours, width = cost_ref.shape
    omega = omega_ref[0:1, 0:1]
    tau, sigma = step_ratio / omega, step_ratio * omega
    rows[...] = jnp.zeros_like(rows)
    grow(bus_ref, came_ref, grown_ref)
    totals = year_totals(received_ref, rows.shape[0] // LANES, regions)
    coming.wait()
    for t, total in enumerate(totals):
        at = slice(t * LANES, (t + 1) * LANES)
        dual[:, at] = jnp.maximum(sigma * (total - year_bound * annual[:, at]), 0.0)
    leaving = begin(dual, dual_ref, sems.at[1])
    for r in range(regions):
        high = upper_ref[r : r + 1, units:]
        costs = cost_ref[r, :, units:].astype(F32)
        old = clip(-tau * costs, 0.0, high)
        grad = costs + back_ref[r * hours : (r + 1) * hours, units:] + year_scale * dual[r : r + 1, units:]
        bar = 2.0 * clip(old - tau * grad, 0.0, high) - old
        sums = year_scale * jnp.sum(bar, axis=0, keepdims=True)
        for t in range(1, width // LANES):
            rows[t * PAD_ROWS + r : t * PAD_ROWS + r + 1, :] = sums[:, t * LANES - units : (t + 1) * LANES - units]
    year_pieces(rows, out)
    begin(out, sent_ref, sems.at[0]).wait()
    leaving.wait()


def last_kernel(
    units, year_scale, place_ref, omega_ref, cost_ref, back_ref, upper_ref, dual_ref, conversion_ref,
    demand_ref, prices_ref, bus_ref, ends_ref, caps_ref,
    primal_ref, flows_ref, new_prices_ref, bar, held, sems,
):
    copy = begin(conversion_ref, held, sems.at[0])
    regions, hours, width = cost_ref.shape
    bus_rows = demand_ref.shape[2]
    lines = flows_ref.shape[1]
    n = regions * hours
    omega = omega_ref[0:1, 0:1]
    tau, sigma = step_ratio / omega, step_ratio * omega
    bar[:, :units] = jnp.zeros((n, units), F32)
    for r in range(regions):
        at = slice(r * hours, (r + 1) * hours)
        high = upper_ref[r : r + 1, units:]
        costs = cost_ref[r, :, units:].astype(F32)
        old = clip(-tau * costs, 0.0, high)
        grad = costs + back_ref[at, units:] + year_scale * dual_ref[r : r + 1, units:]
        new = clip(old - tau * grad, 0.0, high)
        bar[at, units:] = 2.0 * new - old
        primal_ref[r, :, :units] = jnp.zeros((hours, units), BF16)
        primal_ref[r, :, units:] = new.astype(BF16)
    copy.wait()
    step = 256
    image = None
    for k in range(0, width, step):
        part = dot3(split(bar[:, k : k + step]), split(held[k : k + step, :]), ((1,), (0,)))
        image = part if image is None else image + part
    loads = demand_ref[...].astype(F32).reshape(n, bus_rows)
    new_prices_ref[...] = prices_ref[...] + sigma * (image - loads)

    regions_all = bus_ref.shape[0]
    first_region = place_ref[0] * regions

    def exact(a, b, dims):
        return lax.dot_general(
            a, b, (dims, ((), ())), precision=lax.Precision.HIGHEST, preferred_element_type=F32
        )

    def incidence(count):
        ids = lax.broadcasted_iota(jnp.int32, (count, ends_ref.shape[1]), 0) + first_region
        ids = jnp.where(ids >= regions_all, ids - regions_all, ids)
        return (ids == ends_ref[1:2, :]).astype(F32) - (ids == ends_ref[0:1, :]).astype(F32)

    caps = caps_ref[...]
    flows = clip(-tau * exact(bus_ref[...], incidence(regions_all), ((0,), (0,))), -caps, caps)
    flows_ref[...] = flows[:, :lines]
    inflow = exact(2.0 * flows, incidence(LANES), ((1,), (1,)))
    ids = lane_ids(inflow.shape)
    for r in range(regions):
        moved = inflow if r == 0 else pltpu.roll(inflow, LANES - r, 1)
        at = slice(r * hours, (r + 1) * hours)
        new_prices_ref[at, :LANES] = new_prices_ref[at, :LANES] + sigma * jnp.where(ids == 0, moved, 0.0)


def finish_kernel(
    count, year_bound, omega_ref, received_ref, cost_ref, upper_ref, conversion_ref, prices_ref, primal_ref,
    dual_ref, annual_ref, new_primal_ref, new_prices_ref, storage_ref, year_ref,
    bar, held, prices, dual, annual, stored_primal, sems,
):
    regions, hours, units = cost_ref.shape
    n = regions * hours
    coming = [
        begin(source, target, sems.at[k])
        for k, (source, target) in enumerate(
            ((dual_ref, dual), (annual_ref, annual), (conversion_ref.at[pl.ds(0, units)], held), (prices_ref, prices))
        )
    ]
    omega = omega_ref[0:1, 0:1]
    tau, sigma = step_ratio / omega, step_ratio * omega
    x = collect(received_ref, count, 4 * n // LANES)
    storage_ref[...] = x[2 * n : 3 * n] + swap_halves(x[3 * n :])
    stored = x[:n] + swap_halves(x[n : 2 * n])
    for r in range(regions):
        at = slice(r * hours, (r + 1) * hours)
        high = upper_ref[r : r + 1, :units]
        new = stored[at]
        stored_primal[r] = new.astype(BF16)
        bar[at, :] = 2.0 * new - clip(-tau * cost_ref[r].astype(F32), -high, high)
    leaving = begin(stored_primal, new_primal_ref.at[:, :, pl.ds(0, units)], sems.at[4])
    totals = year_totals(received_ref, count, regions)
    for copy in coming:
        copy.wait()
    for t, total in enumerate(totals):
        at = slice(t * LANES, (t + 1) * LANES)
        year_ref[:, at] = jnp.maximum(dual[:, at] + sigma * (total - year_bound * annual[:, at]), 0.0)
    image = dot3(split(bar[...]), split(held[...]), ((1,), (0,)))
    new_prices_ref[...] = prices[...] + sigma * image
    leaving.wait()


def exchange(x):
    blocks = lax.axis_size("tm")
    pieces = x.reshape(blocks, 1, x.size // blocks)
    return lax.all_to_all(pieces, "tm", 0, 0, tiled=True).reshape(x.shape)


def sum_over_all(cost, demand):
    blocks, groups = lax.axis_size("tm"), lax.axis_size("region")
    row = call(sums_kernel, struct(1, LANES), "sums", [VMEM] * 2)(cost, demand)
    pairs = [[2 * k, 2 * k + 1] for k in range(blocks // 2)]
    pair = jnp.sum(lax.all_gather(row, "tm", axis=0, axis_index_groups=pairs, tiled=True), axis=0, keepdims=True)
    half = blocks * groups // 2
    cores = [[(2 * k + core) * groups + z for k in range(blocks // 2) for z in range(groups)] for core in range(2)]
    pieces = jnp.broadcast_to(pair[:, None, :], (half, 1, LANES))
    return lax.all_to_all(
        pieces, ("tm", "region"), 0, 0, tiled=True, axis_index_groups=cores
    ).reshape(half, LANES)


def per_device(cost, demand, conversion, upper, decay, energy_cap, annual_cap, line_ends, line_cap):
    hours, regions, width = cost.shape
    bus_rows = demand.shape[2]
    units = decay.shape[2]
    lines = line_ends.shape[0]
    blocks = lax.axis_size("tm")
    groups = lax.axis_size("region")
    hours_all = hours * blocks
    scale = 1.0 / math.sqrt(hours_all)
    bound = math.sqrt(hours_all)
    n = regions * hours
    year_rows = 2 * PAD_ROWS * (width // LANES)
    year_count = year_rows // LANES
    turned_count = 4 * n // LANES
    back_count = -(-2 * n // LANES)
    rows = lambda k: pltpu.VMEM((k, LANES), F32)
    sems = lambda k: pltpu.SemaphoreType.DMA((k,))
    pieces = lambda count: struct(blocks * count, LANES)
    cost = jnp.transpose(cost, (1, 0, 2))
    demand = jnp.transpose(demand, (1, 0, 2))
    decay = jnp.transpose(decay, (1, 0, 2))
    tm_place = lax.axis_index("tm").astype(jnp.int32).reshape(1)
    region_place = lax.axis_index("region").astype(jnp.int32).reshape(1)

    def from_ahead(x, reach):
        return lax.ppermute(x, "region", [((z + reach) % groups, z) for z in range(groups)])

    sums = sum_over_all(cost, demand)
    turned = call(turn_kernel, pieces(turned_count), "turn", [VMEM] * 2, [rows(4 * n)])(cost, decay)
    first_count = year_count + turned_count
    omega, first = call(
        functools.partial(first_kernel, units, scale),
        (struct(8, LANES), pieces(first_count)),
        "first_primal",
        [VMEM] * 4,
        [rows(blocks * first_count), rows(year_rows), sems(1)],
        (VMEM, HBM),
    )(sums, cost, upper, turned)
    first = exchange(first)

    ends_t = line_ends.T.astype(F32)
    own = jnp.concatenate([jnp.zeros((1, n), F32), ends_t.reshape(1, -1), line_cap.reshape(1, -1)], axis=1)
    prices, back, back_turned, bus = call(
        functools.partial(prices_kernel, units),
        (struct(n, bus_rows), struct(n, width), pieces(back_count), struct(1, own.shape[1])),
        "first_prices",
        [VMEM] * 4 + [HBM, VMEM],
        [pltpu.VMEM((n, width), F32), rows(back_count * LANES), pltpu.VMEM((width, bus_rows), F32), sems(1)],
        flops=4000000000,
        nbytes=5000000,
    )(omega, cost, upper, demand, conversion, own)

    second_count = year_count + back_count
    second, bus = call(
        functools.partial(sum_kernel, year_count),
        (pieces(second_count), struct(2, own.shape[1])),
        "year_sum",
        [VMEM] * 4,
        [rows(blocks * second_count), sems(1)],
        (HBM, VMEM),
    )(first, back_turned, bus, from_ahead(bus, 1))
    second = exchange(second)

    third, year_dual, bus = call(
        functools.partial(second_kernel, units, scale, bound),
        (pieces(year_count), struct(regions, width), struct(4, own.shape[1])),
        "second_primal",
        [VMEM] * 5 + [HBM] + [VMEM] * 2,
        [
            rows(year_rows),
            pltpu.VMEM((regions, width), F32),
            pltpu.VMEM((regions, width), F32),
            rows(blocks * year_count),
            sems(2),
        ],
        (HBM, HBM, VMEM),
    )(omega, second, cost, back, upper, annual_cap, bus, from_ahead(bus, 2))
    third = exchange(third)

    returned, stored_year = call(
        functools.partial(storage_kernel, year_count, scale, scale, bound),
        (pieces(turned_count), struct(8, year_rows)),
        "storage",
        [SMEM] + [VMEM] * 6,
        [rows(n) for _ in range(9)] + [rows(4 * n)],
        flops=4000000000,
    )(tm_place, omega, first, second, upper, energy_cap, annual_cap)

    fourth, bus = call(
        functools.partial(sum_with_stored_kernel, year_count),
        (pieces(first_count), struct(8, own.shape[1])),
        "year_sum_2",
        [VMEM] * 5,
        [rows(blocks * first_count), sems(1)],
        (HBM, VMEM),
    )(third, stored_year, returned, bus, from_ahead(bus, 4))
    fourth = exchange(fourth)

    ends = bus[:, n:].reshape(groups, 3, lines).transpose(1, 0, 2).reshape(3, groups * lines)
    bus = bus[:, :n].reshape(groups * regions, hours)
    primal, flows, prices = call(
        functools.partial(last_kernel, units, scale),
        (struct(regions, hours, width, dtype=BF16), struct(hours, lines), struct(n, bus_rows)),
        "second_prices",
        [SMEM] + [VMEM] * 5 + [HBM] + [VMEM] * 5,
        [pltpu.VMEM((n, width), F32), pltpu.VMEM((width, bus_rows), F32), sems(1)],
        flops=3000000000,
        nbytes=6000000,
    )(
        region_place, omega, cost, back, upper, year_dual, conversion, demand, prices, bus,
        ends[:2].astype(jnp.int32), ends[2:],
    )
    new_primal, prices, storage_dual, year_dual = call(
        functools.partial(finish_kernel, year_count, bound),
        (
            struct(regions, hours, width, dtype=BF16),
            struct(n, bus_rows),
            struct(n, units),
            struct(regions, width),
        ),
        "finish",
        [VMEM] * 4 + [HBM] * 5,
        [
            rows(n),
            pltpu.VMEM((units, bus_rows), F32),
            pltpu.VMEM((n, bus_rows), F32),
            pltpu.VMEM((regions, width), F32),
            pltpu.VMEM((regions, width), F32),
            pltpu.VMEM((regions, hours, units), BF16),
            sems(5),
        ],
        (HBM, VMEM, VMEM, VMEM),
        {6: 0},
    )(omega, fourth, cost[:, :, :units], upper, conversion, prices, primal, year_dual, annual_cap)
    turn = lambda x, last: jnp.transpose(x.reshape(regions, hours, last), (1, 0, 2))
    return (
        jnp.transpose(new_primal, (1, 0, 2)),
        flows,
        turn(prices, bus_rows),
        turn(storage_dual, units),
        year_dual,
    )


def solution(mesh):
    in_specs = (
        P("tm", "region", None),
        P("tm", "region", None),
        P(),
        P("region", None),
        P("tm", "region", None),
        P("region", None),
        P("region", None),
        P("region", None),
        P("region"),
    )
    out_specs = (
        P("tm", "region", None),
        P("tm", "region"),
        P("tm", "region", None),
        P("tm", "region", None),
        P("region", None),
    )
    return jax.shard_map(
        per_device, mesh=mesh, in_specs=in_specs, out_specs=out_specs, check_vma=False
    )
```

```python
import functools
import math

import jax
import jax.numpy as jnp
from jax import lax
from jax.experimental import pallas as pl
from jax.experimental.pallas import tpu as pltpu
from jax.sharding import PartitionSpec as P

F32 = jnp.float32
BF16 = jnp.bfloat16
LANES = 128
PAD_ROWS = 16
step_ratio = 0.5


VMEM = pl.BlockSpec(memory_space=pltpu.VMEM)
SMEM = pl.BlockSpec(memory_space=pltpu.SMEM)
HBM = pl.BlockSpec(memory_space=pltpu.HBM)
ANY = pl.BlockSpec(memory_space=pl.ANY)


def call(kernel, out_shape, name, in_specs, scratch=(), out_specs=None, aliases=None, flops=1000000, nbytes=1000000):
    if out_specs is None:
        out_specs = jax.tree.map(lambda _: VMEM, out_shape)
    return pl.pallas_call(
        kernel,
        out_shape=out_shape,
        in_specs=in_specs,
        out_specs=out_specs,
        scratch_shapes=list(scratch),
        name=name,
        input_output_aliases=aliases or {},
        compiler_params=pltpu.CompilerParams(vmem_limit_bytes=24 * 1024 * 1024),
        cost_estimate=pl.CostEstimate(flops=flops, bytes_accessed=nbytes, transcendentals=0),
    )


def struct(*shape, dtype=F32):
    return jax.ShapeDtypeStruct(shape, dtype)


def begin(source, target, sem):
    copy = pltpu.make_async_copy(source, target, sem)
    copy.start()
    return copy


def in_hbm(*shape, dtype=F32):
    return pltpu.HBM(shape, dtype)


def keep(x):
    return pltpu.with_memory_space_constraint(x, pltpu.HBM)


def lane_ids(shape):
    return lax.broadcasted_iota(jnp.int32, shape, len(shape) - 1)


def swap_halves(x):
    return pltpu.roll(x, LANES // 2, 1)


def spread(scratch):
    return jnp.transpose(scratch)[: LANES // 2, :]


def put_pieces(out_ref, first, per, value):
    for q in range(value.shape[1] // LANES):
        out_ref[pl.ds(first + q, LANES // 2, stride=per), :] = value[:, q * LANES : (q + 1) * LANES]


def move_pieces(out_ref, first, per, in_ref):
    count = in_ref.shape[0] // (LANES // 2)
    for q in range(count):
        out_ref[pl.ds(first + q, LANES // 2, stride=per), :] = in_ref[pl.ds(q, LANES // 2, stride=count), :]


def collect(ref, first, count):
    per = ref.shape[0] // (LANES // 2)
    parts = []
    for q in range(first, first + count):
        rows = ref[pl.ds(q, LANES // 2, stride=per), :]
        parts.append(jnp.transpose(jnp.concatenate([rows, jnp.zeros_like(rows)], axis=0)))
    return jnp.concatenate(parts, axis=0)


def sum_pieces(ref, count):
    per = ref.shape[0] // (LANES // 2)
    return [jnp.sum(ref[pl.ds(q, LANES // 2, stride=per), :], axis=0, keepdims=True) for q in range(count)]


def split(x):
    high = x.astype(BF16)
    return high, (x - high.astype(F32)).astype(BF16)


def dot(a, b, dims):
    return lax.dot_general(a, b, (dims, ((), ())), preferred_element_type=F32)


def dot3(a, b, dims):
    (ah, al), (bh, bl) = a, b
    return dot(ah, bh, dims) + (dot(ah, bl, dims) + dot(al, bh, dims))


def bounds(upper_row, units):
    return jnp.where(lane_ids(upper_row.shape) < units, -upper_row, 0.0), upper_row


def clip(x, low, high):
    return jnp.minimum(jnp.maximum(x, low), high)


def sums_kernel(cost_ref, demand_ref, sent_ref, out, sems):
    regions = cost_ref.shape[0]

    def total(ref):
        acc = None
        for r in range(regions):
            x = ref[r].astype(F32)
            acc = x * x if acc is None else acc + x * x
        return jnp.sum(jnp.sum(acc, axis=0, keepdims=True), axis=1, keepdims=True)

    ids = lane_ids((1, LANES))
    row = jnp.where(ids == 0, total(cost_ref), jnp.where(ids == 1, total(demand_ref), 0.0))
    out[...] = jnp.broadcast_to(row, out.shape)
    begin(out, sent_ref, sems.at[0]).wait()


def join_kernel(sums_ref, turned_ref, sent_ref, out, sems):
    per = out.shape[0] // (LANES // 2)
    row = jnp.sum(sums_ref[...], axis=0, keepdims=True)
    out[pl.ds(0, LANES // 2, stride=per), :] = jnp.broadcast_to(row, (LANES // 2, LANES))
    move_pieces(out, 1, per, turned_ref)
    begin(out, sent_ref, sems.at[0]).wait()


def turn_kernel(cost_ref, decay_ref, out_ref, rows):
    regions, hours, units = decay_ref.shape
    n = regions * hours
    costs = cost_ref[:, :, :units].astype(F32).reshape(n, units)
    decay = decay_ref[...].reshape(n, units)
    for place, x in enumerate((costs, swap_halves(costs), decay, swap_halves(decay))):
        rows[place * n : (place + 1) * n, :] = x
    put_pieces(out_ref, 0, out_ref.shape[0] // (LANES // 2), spread(rows[...]))


def year_pieces(rows, out_ref):
    half = rows.shape[0] // 2
    rows[half:, :] = swap_halves(rows[:half, :])
    put_pieces(out_ref, 0, out_ref.shape[0] // (LANES // 2), spread(rows[...]))


def year_totals(received_ref, count, regions):
    x = collect(received_ref, 0, count)
    half = x.shape[0] // 2
    tiles = []
    for t in range(half // PAD_ROWS):
        at = t * PAD_ROWS
        tile = x[at : at + PAD_ROWS, :] + swap_halves(x[half + at : half + at + PAD_ROWS, :])
        tiles.append(tile[:regions, :])
    return tiles


def first_kernel(
    units, year_scale, joined_ref, cost_ref, upper_ref, omega_ref, sent_ref, out_ref, rows, sems
):
    regions, hours, width = cost_ref.shape
    (s,) = sum_pieces(joined_ref, 1)
    ids = lane_ids(s.shape)
    cost_sum = jnp.sum(jnp.where(ids == 0, s, 0.0), axis=1, keepdims=True)
    load_sum = jnp.sum(jnp.where(ids == 1, s, 0.0), axis=1, keepdims=True)
    omega = jnp.sqrt(cost_sum / load_sum)
    omega_ref[...] = jnp.broadcast_to(omega, omega_ref.shape)
    tau = step_ratio / omega
    rows[...] = jnp.zeros_like(rows)
    for r in range(regions):
        low, high = bounds(upper_ref[r : r + 1, :], units)
        primal = clip(-tau * cost_ref[r].astype(F32), low, high)
        sums = (2.0 * year_scale) * jnp.sum(primal, axis=0, keepdims=True)
        for t in range(width // LANES):
            rows[t * PAD_ROWS + r : t * PAD_ROWS + r + 1, :] = sums[:, t * LANES : (t + 1) * LANES]
    year_pieces(rows, out_ref)
    begin(out_ref, sent_ref, sems.at[0]).wait()


def prices_kernel(
    units, omega_ref, cost_ref, upper_ref, demand_ref, conversion_ref, ends_ref,
    prices_ref, back_ref, turned_ref, bus_ref, bar, rows, held, demand, new_prices, sems,
):
    copy = begin(conversion_ref, held, sems.at[0])
    demand_copy = begin(demand_ref, demand, sems.at[1])
    regions, hours, width = cost_ref.shape
    bus_rows = demand_ref.shape[2]
    n = regions * hours
    omega = omega_ref[0:1, 0:1]
    tau, sigma = step_ratio / omega, step_ratio * omega
    for r in range(regions):
        low, high = bounds(upper_ref[r : r + 1, :], units)
        bar[r * hours : (r + 1) * hours, :] = 2.0 * clip(-tau * cost_ref[r].astype(F32), low, high)
    copy.wait()
    step = 256
    image = None
    for k in range(0, width, step):
        part = dot3(split(bar[:, k : k + step]), split(held[k : k + step, :]), ((1,), (0,)))
        image = part if image is None else image + part
    demand_copy.wait()
    loads = demand[...].astype(F32).reshape(n, bus_rows)
    prices = sigma * (image - loads)
    new_prices[...] = prices
    leaving = begin(new_prices, prices_ref, sems.at[0])
    cut = split(prices)
    for k in range(0, width, step):
        back_ref[:, k : k + step] = dot3(cut, split(held[k : k + step, :]), ((1,), (1,)))
    stored = back_ref[:, :units]
    rows[:n, :] = stored
    rows[n : 2 * n, :] = swap_halves(stored)
    rows[2 * n :, :] = jnp.zeros_like(rows[2 * n :, :])
    put_pieces(turned_ref, 0, turned_ref.shape[0] // (LANES // 2), spread(rows[...]))
    bus = jnp.transpose(prices[:, :LANES])[0:1, :]
    ends = ends_ref[...]
    row = jnp.concatenate([bus, jnp.zeros((1, ends.shape[1] - n), F32)], axis=1) + ends
    bus_ref[...] = row
    leaving.wait()


def sum_kernel(count, received_ref, added_ref, bus_ref, came_ref, sent_ref, grown_ref, out_ref, sems):
    per = out_ref.shape[0] // (LANES // 2)
    for q, total in enumerate(sum_pieces(received_ref, count)):
        out_ref[pl.ds(q, LANES // 2, stride=per), :] = jnp.broadcast_to(total, (LANES // 2, LANES))
    move_pieces(out_ref, count, per, added_ref)
    copy = begin(out_ref, sent_ref, sems.at[0])
    grow(bus_ref, came_ref, grown_ref)
    copy.wait()


def grow(bus_ref, came_ref, grown_ref):
    grown_ref[: bus_ref.shape[0], :] = bus_ref[...]
    grown_ref[bus_ref.shape[0] :, :] = came_ref[...]


def sum_with_stored_kernel(count, received_ref, stored_ref, added_ref, sent_ref, out_ref, sems):
    per = out_ref.shape[0] // (LANES // 2)
    for q, total in enumerate(sum_pieces(received_ref, count)):
        if q % (count // 2) == 0:
            stored = stored_ref[0:1, (q // (count // 2)) * LANES : (q // (count // 2) + 1) * LANES]
            total = jnp.where(lane_ids(total.shape) < PAD_ROWS, stored, total)
        out_ref[pl.ds(q, LANES // 2, stride=per), :] = jnp.broadcast_to(total, (LANES // 2, LANES))
    move_pieces(out_ref, count, per, added_ref)
    begin(out_ref, sent_ref, sems.at[0]).wait()


def before(x, k, reverse):
    ids = lax.rem(lane_ids(x.shape), LANES // 2)
    if reverse:
        return pltpu.roll(x, LANES - k, 1), ids < LANES // 2 - k
    return pltpu.roll(x, k, 1), ids >= k


def carry_in(scale, offset, reverse):
    k = 1
    while k < LANES // 2:
        scale_before, ok = before(scale, k, reverse)
        offset_before, _ = before(offset, k, reverse)
        offset = jnp.where(ok, scale * offset_before + offset, offset)
        scale = jnp.where(ok, scale * scale_before, scale)
        k *= 2
    entering, ok = before(offset, 1, reverse)
    return jnp.where(ok, entering, 0.0)


def strided(regions, hours):
    def get(ref, h):
        return ref[pl.ds(h, regions, stride=hours), :]

    def put(ref, h, value):
        ref[pl.ds(h, regions, stride=hours), :] = value

    return get, put


def owned(place, x):
    ids = lane_ids(x.shape)
    half = LANES // 2
    first = jnp.sum(jnp.where(ids == place, x, 0.0), axis=1, keepdims=True)
    second = jnp.sum(jnp.where(ids == place + half, x, 0.0), axis=1, keepdims=True)
    return jnp.where(ids < half, first, second)


def halves(x):
    left = lane_ids(x.shape) < LANES // 2
    return (
        jnp.sum(jnp.where(left, x, 0.0), axis=1, keepdims=True),
        jnp.sum(jnp.where(left, 0.0, x), axis=1, keepdims=True),
    )


def carry_pieces(out_ref, rows, carries):
    regions = carries[0].shape[0]
    rows[...] = jnp.zeros_like(rows)
    for k, carry in enumerate(carries):
        at = 2 * k * PAD_ROWS
        rows[at : at + regions, :] = carry
        rows[at + PAD_ROWS : at + PAD_ROWS + regions, :] = swap_halves(carry)
    put_pieces(out_ref, 0, 1, spread(rows[...]))


def collect_carries(ref, q, regions, count):
    x = collect(ref, q, 1)
    found = []
    for k in range(count):
        at = 2 * k * PAD_ROWS
        found.append(x[at : at + regions, :] + swap_halves(x[at + PAD_ROWS : at + PAD_ROWS + regions, :]))
    return found


def storage_kernel(
    level_scale, year_scale, year_bound,
    place_ref, omega_ref, joined_ref, order_ref, upper_ref, energy_ref, annual_ref,
    carries_ref, costs, decay, grad, block_ref, run, scale, dual, suffix, suffix_scale, rows,
):
    del order_ref
    regions, units = energy_ref.shape
    n = costs.shape[0]
    hours = n // regions
    get, put = strided(regions, hours)
    place = place_ref[0]
    omega = omega_ref[0:1, 0:1]
    tau, sigma = step_ratio / omega, step_ratio * omega
    high = owned(place, upper_ref[:, :units])
    energy = owned(place, energy_ref[...])
    annual = owned(place, annual_ref[:, :units])
    x = collect(joined_ref, 1, 4 * n // LANES)
    costs[...] = x[:n] + swap_halves(x[n : 2 * n])
    decay[...] = x[2 * n : 3 * n] + swap_halves(x[3 * n :])

    level = jnp.zeros((regions, units), F32)
    kept = jnp.ones((regions, units), F32)
    year = jnp.zeros((regions, units), F32)
    for h in range(hours):
        d = get(decay, h)
        bar = 2.0 * clip(-tau * get(costs, h), -high, high)
        year = year + bar
        level = d * level + bar
        kept = kept * d
        put(run, h, level)
        put(scale, h, kept)
    entering = carry_in(kept, level, False)
    first, second = halves(year)
    total = year_scale * jnp.where(lane_ids(year.shape) < LANES // 2, first, second)
    block_ref[...] = jnp.zeros_like(block_ref)
    block_ref[:regions, :] = kept
    block_ref[PAD_ROWS : PAD_ROWS + regions, :] = jnp.maximum(sigma * (total - year_bound * annual), 0.0)
    after = jnp.zeros((regions, units), F32)
    after_kept = jnp.ones((regions, units), F32)
    for h in reversed(range(hours)):
        d = get(decay, h)
        level = get(run, h) + get(scale, h) * entering
        stored = level_scale * jnp.maximum(sigma * (level_scale * level - energy), 0.0)
        put(dual, h, stored)
        after = d * (stored + after)
        after_kept = after_kept * d
        put(suffix, h, after)
        put(suffix_scale, h, after_kept)
    closing = carry_in(after_kept, after, True)
    for h in range(hours):
        later = closing if h == hours - 1 else get(suffix, h + 1) + get(suffix_scale, h + 1) * closing
        put(grad, h, get(costs, h) + (get(dual, h) + later))
    carry_pieces(carries_ref, rows, (entering, closing))


def storage_again_kernel(
    count, year_scale, place_ref, omega_ref, costs, decay, grad, block_ref, received_ref, upper_ref,
    bus_ref, came_ref, carries_ref, year_ref, grown_ref, back, rows,
):
    n, units = costs.shape
    regions = upper_ref.shape[0]
    hours = n // regions
    get, _ = strided(regions, hours)
    grow(bus_ref, came_ref, grown_ref)
    omega = omega_ref[0:1, 0:1]
    tau = step_ratio / omega
    high = owned(place_ref[0], upper_ref[:, :units])
    kept = block_ref[:regions, :]
    year_dual = block_ref[PAD_ROWS : PAD_ROWS + regions, :]
    x = collect(received_ref, count, -(-2 * n // LANES))
    back[...] = x[:n] + swap_halves(x[n : 2 * n])
    level = jnp.zeros((regions, units), F32)
    year = jnp.zeros((regions, units), F32)
    for h in range(hours):
        old = clip(-tau * get(costs, h), -high, high)
        new = clip(old - tau * (get(grad, h) + get(back, h) + year_scale * year_dual), -high, high)
        bar = 2.0 * new - old
        year = year + bar
        level = get(decay, h) * level + bar
    carry_pieces(carries_ref, rows, (carry_in(kept, level, False),))
    diagonal = lax.broadcasted_iota(jnp.int32, (regions, units), 0) == lane_ids((regions, units))
    for part, column in enumerate(halves(year)):
        line = jnp.sum(jnp.where(diagonal, year_scale * column, 0.0), axis=0, keepdims=True)
        year_ref[:, part * LANES : (part + 1) * LANES] = jnp.broadcast_to(line, (year_ref.shape[0], LANES))


def second_kernel(
    units, year_scale, year_bound,
    omega_ref, received_ref, cost_ref, back_ref, upper_ref, annual_ref, carries_ref,
    sent_ref, dual_ref, rows, annual, dual, out, sems,
):
    coming = begin(annual_ref, annual, sems.at[0])
    regions, hours, width = cost_ref.shape
    omega = omega_ref[0:1, 0:1]
    tau, sigma = step_ratio / omega, step_ratio * omega
    rows[...] = jnp.zeros_like(rows)
    totals = year_totals(received_ref, rows.shape[0] // LANES, regions)
    coming.wait()
    for t, total in enumerate(totals):
        at = slice(t * LANES, (t + 1) * LANES)
        dual[:, at] = jnp.maximum(sigma * (total - year_bound * annual[:, at]), 0.0)
    leaving = begin(dual, dual_ref, sems.at[1])
    for r in range(regions):
        high = upper_ref[r : r + 1, units:]
        costs = cost_ref[r, :, units:].astype(F32)
        old = clip(-tau * costs, 0.0, high)
        grad = costs + back_ref[r * hours : (r + 1) * hours, units:] + year_scale * dual[r : r + 1, units:]
        bar = 2.0 * clip(old - tau * grad, 0.0, high) - old
        sums = year_scale * jnp.sum(bar, axis=0, keepdims=True)
        for t in range(1, width // LANES):
            rows[t * PAD_ROWS + r : t * PAD_ROWS + r + 1, :] = sums[:, t * LANES - units : (t + 1) * LANES - units]
    year_pieces(rows, out)
    move_pieces(out, rows.shape[0] // LANES, out.shape[0] // (LANES // 2), carries_ref)
    begin(out, sent_ref, sems.at[0]).wait()
    leaving.wait()


def last_kernel(
    units, count, level_scale, year_scale,
    place_ref, omega_ref, cost_ref, back_ref, upper_ref, dual_ref, conversion_ref, demand_ref, prices_ref,
    bus_ref, ends_ref, caps_ref, received_ref, decay_ref, energy_ref,
    primal_ref, flows_ref, new_prices_ref, base_ref, slope_ref,
    bar, held, demand, old_prices, dual, costs, decay, back, stored, new_stored, sems,
):
    copy, *others = [
        begin(source, target, sems.at[k])
        for k, (source, target) in enumerate(
            ((dual_ref, dual), (conversion_ref, held), (demand_ref, demand), (prices_ref, old_prices))
        )
    ]
    regions, hours, width = cost_ref.shape
    bus_rows = demand_ref.shape[2]
    lines = flows_ref.shape[1]
    n = regions * hours
    get, put = strided(regions, hours)
    omega = omega_ref[0:1, 0:1]
    tau, sigma = step_ratio / omega, step_ratio * omega

    costs[...] = cost_ref[:, :, :units].astype(F32).reshape(n, units)
    decay[...] = decay_ref[...].reshape(n, units)
    back[...] = back_ref[:, :units]
    high = upper_ref[:, :units]
    energy = energy_ref[...]
    level, later = collect_carries(received_ref, count, regions, 2)
    for h in range(hours):
        level = get(decay, h) * level + 2.0 * clip(-tau * get(costs, h), -high, high)
        put(stored, h, jnp.maximum(sigma * (level_scale * level - energy), 0.0))
    copy.wait()
    year_part = year_scale * dual[:, :units]
    for h in reversed(range(hours)):
        weight = level_scale * get(stored, h) + later
        later = get(decay, h) * weight
        old = clip(-tau * get(costs, h), -high, high)
        put(new_stored, h, clip(old - tau * (get(costs, h) + get(back, h) + weight + year_part), -high, high))
    level = jnp.zeros((regions, units), F32)
    kept = jnp.ones((regions, units), F32)
    for h in range(hours):
        d = get(decay, h)
        second = 2.0 * get(new_stored, h) - clip(-tau * get(costs, h), -high, high)
        level = d * level + second
        kept = d * kept
        put(base_ref, h, get(stored, h) + sigma * (level_scale * level - energy))
        put(slope_ref, h, (sigma * level_scale) * kept)
        put(back, h, second)
    bar[:, :units] = back[...]
    for r in range(regions):
        at = slice(r * hours, (r + 1) * hours)
        high = upper_ref[r : r + 1, units:]
        row_costs = cost_ref[r, :, units:].astype(F32)
        old = clip(-tau * row_costs, 0.0, high)
        grad = row_costs + back_ref[at, units:] + year_scale * dual[r : r + 1, units:]
        new = clip(old - tau * grad, 0.0, high)
        bar[at, units:] = 2.0 * new - old
        primal_ref[r, :, :units] = new_stored[at, :].astype(BF16)
        primal_ref[r, :, units:] = new.astype(BF16)
    for other in others:
        other.wait()
    step = 256
    image = None
    for k in range(0, width, step):
        part = dot3(split(bar[:, k : k + step]), split(held[k : k + step, :]), ((1,), (0,)))
        image = part if image is None else image + part
    loads = demand[...].astype(F32).reshape(n, bus_rows)
    new_prices_ref[...] = old_prices[...] + sigma * (image - loads)

    regions_all = bus_ref.shape[0]
    first_region = place_ref[0] * regions

    def exact(a, b, dims):
        return lax.dot_general(
            a, b, (dims, ((), ())), precision=lax.Precision.HIGHEST, preferred_element_type=F32
        )

    def incidence(count):
        ids = lax.broadcasted_iota(jnp.int32, (count, ends_ref.shape[1]), 0) + first_region
        ids = jnp.where(ids >= regions_all, ids - regions_all, ids)
        return (ids == ends_ref[1:2, :]).astype(F32) - (ids == ends_ref[0:1, :]).astype(F32)

    caps = caps_ref[...]
    flows = clip(-tau * exact(bus_ref[...], incidence(regions_all), ((0,), (0,))), -caps, caps)
    flows_ref[...] = flows[:, :lines]
    inflow = exact(2.0 * flows, incidence(LANES), ((1,), (1,)))
    ids = lane_ids(inflow.shape)
    for r in range(regions):
        moved = inflow if r == 0 else pltpu.roll(inflow, LANES - r, 1)
        at = slice(r * hours, (r + 1) * hours)
        new_prices_ref[at, :LANES] = new_prices_ref[at, :LANES] + sigma * jnp.where(ids == 0, moved, 0.0)


def finish_kernel(
    count, year_bound, omega_ref, received_ref, base_ref, slope_ref, dual_ref, annual_ref,
    storage_ref, year_ref, dual, annual, sems,
):
    copies = [begin(dual_ref, dual, sems.at[0]), begin(annual_ref, annual, sems.at[1])]
    regions = annual_ref.shape[0]
    hours = base_ref.shape[0] // regions
    sigma = step_ratio * omega_ref[0:1, 0:1]
    (entering,) = collect_carries(received_ref, count, regions, 1)
    for r in range(regions):
        at = slice(r * hours, (r + 1) * hours)
        storage_ref[at, :] = jnp.maximum(base_ref[at, :] + slope_ref[at, :] * entering[r : r + 1, :], 0.0)
    totals = year_totals(received_ref, count, regions)
    for copy in copies:
        copy.wait()
    for t, total in enumerate(totals):
        at = slice(t * LANES, (t + 1) * LANES)
        year_ref[:, at] = jnp.maximum(dual[:, at] + sigma * (total - year_bound * annual[:, at]), 0.0)


def exchange(x):
    blocks = lax.axis_size("tm")
    pieces = x.reshape(blocks, 1, x.size // blocks)
    return lax.all_to_all(pieces, "tm", 0, 0, tiled=True).reshape(x.shape)


def per_device(cost, demand, conversion, upper, decay, energy_cap, annual_cap, line_ends, line_cap):
    hours, regions, width = cost.shape
    bus_rows = demand.shape[2]
    units = decay.shape[2]
    lines = line_ends.shape[0]
    blocks = lax.axis_size("tm")
    groups = lax.axis_size("region")
    hours_all = hours * blocks
    scale = 1.0 / math.sqrt(hours_all)
    bound = math.sqrt(hours_all)
    n = regions * hours
    year_rows = 2 * PAD_ROWS * (width // LANES)
    year_count = year_rows // LANES
    turned_count = 4 * n // LANES
    back_count = -(-2 * n // LANES)
    rows = lambda k: pltpu.VMEM((k, LANES), F32)
    sems = lambda k: pltpu.SemaphoreType.DMA((k,))
    pieces = lambda count: struct(blocks * count, LANES)
    sent = lambda count: in_hbm(blocks * count, LANES)
    cost = jnp.transpose(cost, (1, 0, 2))
    demand = jnp.transpose(demand, (1, 0, 2))
    decay = jnp.transpose(decay, (1, 0, 2))
    tm_place = lax.axis_index("tm").astype(jnp.int32).reshape(1)
    region_place = lax.axis_index("region").astype(jnp.int32).reshape(1)

    def from_ahead(x, reach):
        return lax.ppermute(x, "region", [((z + reach) % groups, z) for z in range(groups)])

    sums = call(
        sums_kernel, in_hbm(groups, LANES), "sums", [VMEM] * 2, [rows(groups), sems(1)], HBM
    )(cost, demand)
    sums = lax.all_to_all(sums.reshape(groups, 1, LANES), "region", 0, 0, tiled=True).reshape(groups, LANES)
    turned = call(turn_kernel, pieces(turned_count), "turn", [VMEM] * 2, [rows(4 * n)])(cost, decay)
    joined_count = 1 + turned_count
    joined = call(
        join_kernel, sent(joined_count), "join", [VMEM] * 2, [rows(blocks * joined_count), sems(1)], HBM
    )(sums, turned)
    joined = exchange(joined)
    omega, first = call(
        functools.partial(first_kernel, units, scale),
        (struct(8, LANES), sent(year_count)),
        "first_primal",
        [VMEM] * 3,
        [rows(blocks * year_count), rows(year_rows), sems(1)],
        (VMEM, HBM),
    )(joined, cost, upper)
    first = exchange(first)

    ends_t = line_ends.T.astype(F32)
    own = jnp.concatenate([jnp.zeros((1, n), F32), ends_t.reshape(1, -1), line_cap.reshape(1, -1)], axis=1)
    prices, back, back_turned, bus = call(
        functools.partial(prices_kernel, units),
        (in_hbm(n, bus_rows), struct(n, width), pieces(back_count), struct(1, own.shape[1])),
        "first_prices",
        [VMEM] * 3 + [HBM] * 2 + [VMEM],
        [
            pltpu.VMEM((n, width), F32),
            rows(back_count * LANES),
            pltpu.VMEM((width, bus_rows), F32),
            pltpu.VMEM((regions, hours, bus_rows), BF16),
            pltpu.VMEM((n, bus_rows), F32),
            sems(2),
        ],
        (HBM, VMEM, VMEM, VMEM),
        flops=4000000000,
        nbytes=5000000,
    )(omega, cost, upper, keep(demand), keep(conversion), own)

    second_count = year_count + back_count
    second, bus = call(
        functools.partial(sum_kernel, year_count),
        (sent(second_count), struct(2, own.shape[1])),
        "year_sum",
        [VMEM] * 4,
        [rows(blocks * second_count), sems(1)],
        (HBM, VMEM),
    )(first, back_turned, bus, from_ahead(bus, 1))
    second = exchange(second)

    carries, costs_all, decay_all, grad_all, block = call(
        functools.partial(storage_kernel, scale, scale, bound),
        (pieces(1), struct(n, units), struct(n, units), struct(n, units), struct(2 * PAD_ROWS, units)),
        "storage",
        [SMEM] + [VMEM] * 2 + [ANY] + [VMEM] * 3,
        [rows(n) for _ in range(5)] + [rows(LANES)],
        flops=4000000000,
    )(tm_place, omega, joined, first, upper, energy_cap, annual_cap)

    third, year_dual = call(
        functools.partial(second_kernel, units, scale, bound),
        (sent(year_count + 1), in_hbm(regions, width)),
        "second_primal",
        [VMEM] * 5 + [HBM] + [VMEM],
        [
            rows(year_rows),
            pltpu.VMEM((regions, width), F32),
            pltpu.VMEM((regions, width), F32),
            rows(blocks * (year_count + 1)),
            sems(2),
        ],
        (HBM, HBM),
    )(omega, second, cost, back, upper, keep(annual_cap), carries)
    third = exchange(third)

    carry, stored_year, bus = call(
        functools.partial(storage_again_kernel, year_count, scale),
        (pieces(1), struct(8, year_rows), struct(4, own.shape[1])),
        "storage_again",
        [SMEM] + [VMEM] * 9,
        [rows(n), rows(LANES)],
        flops=4000000000,
    )(tm_place, omega, costs_all, decay_all, grad_all, block, second, upper, bus, from_ahead(bus, 2))

    fourth = call(
        functools.partial(sum_with_stored_kernel, year_count),
        sent(year_count + 1),
        "year_sum_2",
        [VMEM] * 3,
        [rows(blocks * (year_count + 1)), sems(1)],
        HBM,
    )(third, stored_year, carry)
    fourth = exchange(fourth)

    bus = jnp.concatenate([bus, from_ahead(bus, 4)], axis=0)
    ends = bus[:, n:].reshape(groups, 3, lines).transpose(1, 0, 2).reshape(3, groups * lines)
    bus = bus[:, :n].reshape(groups * regions, hours)
    new_primal, flows, prices, base, slope = call(
        functools.partial(last_kernel, units, year_count, scale, scale),
        (
            struct(regions, hours, width, dtype=BF16),
            struct(hours, lines),
            struct(n, bus_rows),
            struct(n, units),
            struct(n, units),
        ),
        "second_prices",
        [SMEM] + [VMEM] * 4 + [HBM] * 4 + [VMEM] * 6,
        [
            pltpu.VMEM((n, width), F32),
            pltpu.VMEM((width, bus_rows), F32),
            pltpu.VMEM((regions, hours, bus_rows), BF16),
            pltpu.VMEM((n, bus_rows), F32),
            pltpu.VMEM((regions, width), F32),
        ]
        + [rows(n) for _ in range(5)]
        + [sems(4)],
        flops=3000000000,
        nbytes=6000000,
    )(
        region_place, omega, cost, back, upper, keep(year_dual), keep(conversion), keep(demand), keep(prices), bus,
        ends[:2].astype(jnp.int32), ends[2:], third, decay, energy_cap,
    )
    storage_dual, year_dual = call(
        functools.partial(finish_kernel, year_count, bound),
        (struct(n, units), struct(regions, width)),
        "finish",
        [VMEM] * 4 + [HBM] * 2,
        [pltpu.VMEM((regions, width), F32), pltpu.VMEM((regions, width), F32), sems(2)],
    )(omega, fourth, base, slope, keep(year_dual), keep(annual_cap))
    turn = lambda x, last: jnp.transpose(x.reshape(regions, hours, last), (1, 0, 2))
    return (
        jnp.transpose(new_primal, (1, 0, 2)),
        flows,
        turn(prices, bus_rows),
        turn(storage_dual, units),
        year_dual,
    )


def solution(mesh):
    in_specs = (
        P("tm", "region", None),
        P("tm", "region", None),
        P(),
        P("region", None),
        P("tm", "region", None),
        P("region", None),
        P("region", None),
        P("region", None),
        P("region"),
    )
    out_specs = (
        P("tm", "region", None),
        P("tm", "region"),
        P("tm", "region", None),
        P("tm", "region", None),
        P("region", None),
    )
    return jax.shard_map(
        per_device, mesh=mesh, in_specs=in_specs, out_specs=out_specs, check_vma=False
    )
```

```python
import functools
import math

import jax
import jax.numpy as jnp
from jax import lax
from jax.experimental import pallas as pl
from jax.experimental.pallas import tpu as pltpu
from jax.sharding import PartitionSpec as P

F32 = jnp.float32
BF16 = jnp.bfloat16
LANES = 128
PAD_ROWS = 16
step_ratio = 0.5


VMEM = pl.BlockSpec(memory_space=pltpu.VMEM)
SMEM = pl.BlockSpec(memory_space=pltpu.SMEM)
HBM = pl.BlockSpec(memory_space=pltpu.HBM)
ANY = pl.BlockSpec(memory_space=pl.ANY)


def call(kernel, out_shape, name, in_specs, scratch=(), out_specs=None, aliases=None, flops=1000000, nbytes=1000000):
    if out_specs is None:
        out_specs = jax.tree.map(lambda _: VMEM, out_shape)
    return pl.pallas_call(
        kernel,
        out_shape=out_shape,
        in_specs=in_specs,
        out_specs=out_specs,
        scratch_shapes=list(scratch),
        name=name,
        input_output_aliases=aliases or {},
        compiler_params=pltpu.CompilerParams(vmem_limit_bytes=24 * 1024 * 1024),
        cost_estimate=pl.CostEstimate(flops=flops, bytes_accessed=nbytes, transcendentals=0),
    )


def struct(*shape, dtype=F32):
    return jax.ShapeDtypeStruct(shape, dtype)


def begin(source, target, sem):
    copy = pltpu.make_async_copy(source, target, sem)
    copy.start()
    return copy


def in_hbm(*shape, dtype=F32):
    return pltpu.HBM(shape, dtype)


def keep(x):
    return pltpu.with_memory_space_constraint(x, pltpu.HBM)


def lane_ids(shape):
    return lax.broadcasted_iota(jnp.int32, shape, len(shape) - 1)


def swap_halves(x):
    return pltpu.roll(x, LANES // 2, 1)


def spread(scratch):
    return jnp.transpose(scratch)[: LANES // 2, :]


def put_pieces(out_ref, first, per, value):
    for q in range(value.shape[1] // LANES):
        out_ref[pl.ds(first + q, LANES // 2, stride=per), :] = value[:, q * LANES : (q + 1) * LANES]


def move_pieces(out_ref, first, per, in_ref):
    count = in_ref.shape[0] // (LANES // 2)
    for q in range(count):
        out_ref[pl.ds(first + q, LANES // 2, stride=per), :] = in_ref[pl.ds(q, LANES // 2, stride=count), :]


def collect(ref, first, count):
    per = ref.shape[0] // (LANES // 2)
    parts = []
    for q in range(first, first + count):
        rows = ref[pl.ds(q, LANES // 2, stride=per), :]
        parts.append(jnp.transpose(jnp.concatenate([rows, jnp.zeros_like(rows)], axis=0)))
    return jnp.concatenate(parts, axis=0)


def sum_pieces(ref, count):
    per = ref.shape[0] // (LANES // 2)
    return [jnp.sum(ref[pl.ds(q, LANES // 2, stride=per), :], axis=0, keepdims=True) for q in range(count)]


def split(x):
    high = x.astype(BF16)
    return high, (x - high.astype(F32)).astype(BF16)


def dot(a, b, dims):
    return lax.dot_general(a, b, (dims, ((), ())), preferred_element_type=F32)


def dot3(a, b, dims):
    (ah, al), (bh, bl) = a, b
    return dot(ah, bh, dims) + (dot(ah, bl, dims) + dot(al, bh, dims))


def bounds(upper_row, units):
    return jnp.where(lane_ids(upper_row.shape) < units, -upper_row, 0.0), upper_row


def clip(x, low, high):
    return jnp.minimum(jnp.maximum(x, low), high)


def sums_kernel(
    cost_ref, demand_ref, ends_ref, caps_ref, sent_ref, cost, demand, ends, caps, out, sems
):
    regions = cost.shape[0]
    half = regions // 2
    copies = [
        begin(source, target, sems.at[k])
        for k, (source, target) in enumerate(
            (
                (cost_ref.at[pl.ds(0, half)], cost.at[pl.ds(0, half)]),
                (cost_ref.at[pl.ds(half, regions - half)], cost.at[pl.ds(half, regions - half)]),
                (demand_ref, demand),
                (ends_ref, ends),
                (caps_ref, caps),
            )
        )
    ]

    def add(ref, first, last, acc):
        for r in range(first, last):
            x = ref[r].astype(F32)
            acc = x * x if acc is None else acc + x * x
        return acc

    def total(acc):
        return jnp.sum(jnp.sum(acc, axis=0, keepdims=True), axis=1, keepdims=True)

    copies[0].wait()
    acc = add(cost, 0, half, None)
    copies[1].wait()
    cost_sum = total(add(cost, half, regions, acc))
    copies[2].wait()
    load_sum = total(add(demand, 0, regions, None))
    ids = lane_ids((1, LANES))
    row = jnp.where(ids == 0, cost_sum, jnp.where(ids == 1, load_sum, 0.0))
    copies[3].wait()
    copies[4].wait()
    lines = ends.shape[1]
    ends_row = ends[...].astype(F32)
    row = row + jnp.concatenate(
        [jnp.zeros((1, LANES - 3 * lines), F32), ends_row[0:1, :], ends_row[1:2, :], caps[...]], axis=1
    )
    out[...] = jnp.broadcast_to(row, out.shape)
    begin(out, sent_ref, sems.at[0]).wait()


def join_kernel(sums_ref, turned_ref, sent_ref, out, sems):
    per = out.shape[0] // (LANES // 2)
    row = jnp.sum(sums_ref[...], axis=0, keepdims=True)
    out[pl.ds(0, LANES // 2, stride=per), :] = jnp.broadcast_to(row, (LANES // 2, LANES))
    move_pieces(out, 1, per, turned_ref)
    begin(out, sent_ref, sems.at[0]).wait()


def turn_kernel(cost_ref, decay_ref, out_ref, rows):
    regions, hours, units = decay_ref.shape
    n = regions * hours
    costs = cost_ref[:, :, :units].astype(F32).reshape(n, units)
    decay = decay_ref[...].reshape(n, units)
    for place, x in enumerate((costs, swap_halves(costs), decay, swap_halves(decay))):
        rows[place * n : (place + 1) * n, :] = x
    put_pieces(out_ref, 0, out_ref.shape[0] // (LANES // 2), spread(rows[...]))


def year_pieces(rows, out_ref):
    half = rows.shape[0] // 2
    rows[half:, :] = swap_halves(rows[:half, :])
    put_pieces(out_ref, 0, out_ref.shape[0] // (LANES // 2), spread(rows[...]))


def year_totals(received_ref, count, regions):
    x = collect(received_ref, 0, count)
    half = x.shape[0] // 2
    tiles = []
    for t in range(half // PAD_ROWS):
        at = t * PAD_ROWS
        tile = x[at : at + PAD_ROWS, :] + swap_halves(x[half + at : half + at + PAD_ROWS, :])
        tiles.append(tile[:regions, :])
    return tiles


def first_kernel(
    units, year_scale, joined_ref, cost_ref, upper_ref, omega_ref, sent_ref, out_ref, rows, sems
):
    regions, hours, width = cost_ref.shape
    (s,) = sum_pieces(joined_ref, 1)
    ids = lane_ids(s.shape)
    cost_sum = jnp.sum(jnp.where(ids == 0, s, 0.0), axis=1, keepdims=True)
    load_sum = jnp.sum(jnp.where(ids == 1, s, 0.0), axis=1, keepdims=True)
    omega = jnp.sqrt(cost_sum / load_sum)
    omega_ref[...] = jnp.broadcast_to(omega, omega_ref.shape)
    tau = step_ratio / omega
    rows[...] = jnp.zeros_like(rows)
    for r in range(regions):
        low, high = bounds(upper_ref[r : r + 1, :], units)
        primal = clip(-tau * cost_ref[r].astype(F32), low, high)
        sums = (2.0 * year_scale) * jnp.sum(primal, axis=0, keepdims=True)
        for t in range(width // LANES):
            rows[t * PAD_ROWS + r : t * PAD_ROWS + r + 1, :] = sums[:, t * LANES : (t + 1) * LANES]
    year_pieces(rows, out_ref)
    begin(out_ref, sent_ref, sems.at[0]).wait()


def prices_kernel(
    units, omega_ref, cost_ref, upper_ref, demand_ref, conversion_ref,
    prices_ref, back_ref, turned_ref, bus_ref, bar, rows, held, demand, new_prices, sems,
):
    copy = begin(conversion_ref, held, sems.at[0])
    demand_copy = begin(demand_ref, demand, sems.at[1])
    regions, hours, width = cost_ref.shape
    bus_rows = demand_ref.shape[2]
    n = regions * hours
    omega = omega_ref[0:1, 0:1]
    tau, sigma = step_ratio / omega, step_ratio * omega
    for r in range(regions):
        low, high = bounds(upper_ref[r : r + 1, :], units)
        bar[r * hours : (r + 1) * hours, :] = 2.0 * clip(-tau * cost_ref[r].astype(F32), low, high)
    copy.wait()
    step = 256
    image = None
    for k in range(0, width, step):
        part = dot3(split(bar[:, k : k + step]), split(held[k : k + step, :]), ((1,), (0,)))
        image = part if image is None else image + part
    demand_copy.wait()
    loads = demand[...].astype(F32).reshape(n, bus_rows)
    prices = sigma * (image - loads)
    new_prices[...] = prices
    leaving = begin(new_prices, prices_ref, sems.at[0])
    cut = split(prices)
    for k in range(0, width, step):
        back_ref[:, k : k + step] = dot3(cut, split(held[k : k + step, :]), ((1,), (1,)))
    stored = back_ref[:, :units]
    rows[:n, :] = stored
    rows[n : 2 * n, :] = swap_halves(stored)
    rows[2 * n :, :] = jnp.zeros_like(rows[2 * n :, :])
    put_pieces(turned_ref, 0, turned_ref.shape[0] // (LANES // 2), spread(rows[...]))
    bus = jnp.transpose(prices[:, :LANES])[0:1, :]
    bus_ref[...] = jnp.concatenate([bus, jnp.zeros((1, bus_ref.shape[1] - n), F32)], axis=1)
    leaving.wait()


def sum_kernel(count, received_ref, added_ref, sent_ref, out_ref, sems):
    per = out_ref.shape[0] // (LANES // 2)
    for q, total in enumerate(sum_pieces(received_ref, count)):
        out_ref[pl.ds(q, LANES // 2, stride=per), :] = jnp.broadcast_to(total, (LANES // 2, LANES))
    move_pieces(out_ref, count, per, added_ref)
    begin(out_ref, sent_ref, sems.at[0]).wait()


def grow(bus_ref, came_ref, grown_ref):
    grown_ref[: bus_ref.shape[0], :] = bus_ref[...]
    grown_ref[bus_ref.shape[0] :, :] = came_ref[...]


def sum_with_stored_kernel(count, received_ref, stored_ref, added_ref, sent_ref, out_ref, sems):
    per = out_ref.shape[0] // (LANES // 2)
    for q, total in enumerate(sum_pieces(received_ref, count)):
        if q % (count // 2) == 0:
            stored = stored_ref[0:1, (q // (count // 2)) * LANES : (q // (count // 2) + 1) * LANES]
            total = jnp.where(lane_ids(total.shape) < PAD_ROWS, stored, total)
        out_ref[pl.ds(q, LANES // 2, stride=per), :] = jnp.broadcast_to(total, (LANES // 2, LANES))
    move_pieces(out_ref, count, per, added_ref)
    begin(out_ref, sent_ref, sems.at[0]).wait()


def before(x, k, reverse):
    ids = lax.rem(lane_ids(x.shape), LANES // 2)
    if reverse:
        return pltpu.roll(x, LANES - k, 1), ids < LANES // 2 - k
    return pltpu.roll(x, k, 1), ids >= k


def carry_in(scale, offset, reverse):
    k = 1
    while k < LANES // 2:
        scale_before, ok = before(scale, k, reverse)
        offset_before, _ = before(offset, k, reverse)
        offset = jnp.where(ok, scale * offset_before + offset, offset)
        scale = jnp.where(ok, scale * scale_before, scale)
        k *= 2
    entering, ok = before(offset, 1, reverse)
    return jnp.where(ok, entering, 0.0)


def strided(regions, hours):
    def get(ref, h):
        return ref[pl.ds(h, regions, stride=hours), :]

    def put(ref, h, value):
        ref[pl.ds(h, regions, stride=hours), :] = value

    return get, put


def owned(place, x):
    ids = lane_ids(x.shape)
    half = LANES // 2
    first = jnp.sum(jnp.where(ids == place, x, 0.0), axis=1, keepdims=True)
    second = jnp.sum(jnp.where(ids == place + half, x, 0.0), axis=1, keepdims=True)
    return jnp.where(ids < half, first, second)


def halves(x):
    left = lane_ids(x.shape) < LANES // 2
    return (
        jnp.sum(jnp.where(left, x, 0.0), axis=1, keepdims=True),
        jnp.sum(jnp.where(left, 0.0, x), axis=1, keepdims=True),
    )


def carry_pieces(out_ref, rows, carries):
    regions = carries[0].shape[0]
    rows[...] = jnp.zeros_like(rows)
    for k, carry in enumerate(carries):
        at = 2 * k * PAD_ROWS
        rows[at : at + regions, :] = carry
        rows[at + PAD_ROWS : at + PAD_ROWS + regions, :] = swap_halves(carry)
    put_pieces(out_ref, 0, 1, spread(rows[...]))


def collect_carries(ref, q, regions, count):
    x = collect(ref, q, 1)
    found = []
    for k in range(count):
        at = 2 * k * PAD_ROWS
        found.append(x[at : at + regions, :] + swap_halves(x[at + PAD_ROWS : at + PAD_ROWS + regions, :]))
    return found


def storage_kernel(
    level_scale, year_scale, year_bound,
    place_ref, omega_ref, joined_ref, order_ref, upper_ref, energy_ref, annual_ref, bus_ref, came_ref,
    carries_ref, costs, decay, grad, block_ref, grown_ref, run, scale, dual, suffix, suffix_scale, rows,
):
    del order_ref
    grow(bus_ref, came_ref, grown_ref)
    regions, units = energy_ref.shape
    n = costs.shape[0]
    hours = n // regions
    get, put = strided(regions, hours)
    place = place_ref[0]
    omega = omega_ref[0:1, 0:1]
    tau, sigma = step_ratio / omega, step_ratio * omega
    high = owned(place, upper_ref[:, :units])
    energy = owned(place, energy_ref[...])
    annual = owned(place, annual_ref[:, :units])
    x = collect(joined_ref, 1, 4 * n // LANES)
    costs[...] = x[:n] + swap_halves(x[n : 2 * n])
    decay[...] = x[2 * n : 3 * n] + swap_halves(x[3 * n :])

    level = jnp.zeros((regions, units), F32)
    kept = jnp.ones((regions, units), F32)
    year = jnp.zeros((regions, units), F32)
    for h in range(hours):
        d = get(decay, h)
        bar = 2.0 * clip(-tau * get(costs, h), -high, high)
        year = year + bar
        level = d * level + bar
        kept = kept * d
        put(run, h, level)
        put(scale, h, kept)
    entering = carry_in(kept, level, False)
    first, second = halves(year)
    total = year_scale * jnp.where(lane_ids(year.shape) < LANES // 2, first, second)
    block_ref[...] = jnp.zeros_like(block_ref)
    block_ref[:regions, :] = kept
    block_ref[PAD_ROWS : PAD_ROWS + regions, :] = jnp.maximum(sigma * (total - year_bound * annual), 0.0)
    after = jnp.zeros((regions, units), F32)
    after_kept = jnp.ones((regions, units), F32)
    for h in reversed(range(hours)):
        d = get(decay, h)
        level = get(run, h) + get(scale, h) * entering
        stored = level_scale * jnp.maximum(sigma * (level_scale * level - energy), 0.0)
        put(dual, h, stored)
        after = d * (stored + after)
        after_kept = after_kept * d
        put(suffix, h, after)
        put(suffix_scale, h, after_kept)
    closing = carry_in(after_kept, after, True)
    for h in range(hours):
        later = closing if h == hours - 1 else get(suffix, h + 1) + get(suffix_scale, h + 1) * closing
        put(grad, h, get(costs, h) + (get(dual, h) + later))
    carry_pieces(carries_ref, rows, (entering, closing))


def storage_again_kernel(
    count, year_scale, place_ref, omega_ref, costs, decay, grad, block_ref, received_ref, upper_ref,
    bus_ref, came_ref, order_ref, carries_ref, year_ref, grown_ref, back, rows,
):
    del order_ref
    n, units = costs.shape
    regions = upper_ref.shape[0]
    hours = n // regions
    get, _ = strided(regions, hours)
    grow(bus_ref, came_ref, grown_ref)
    omega = omega_ref[0:1, 0:1]
    tau = step_ratio / omega
    high = owned(place_ref[0], upper_ref[:, :units])
    kept = block_ref[:regions, :]
    year_dual = block_ref[PAD_ROWS : PAD_ROWS + regions, :]
    x = collect(received_ref, count, -(-2 * n // LANES))
    back[...] = x[:n] + swap_halves(x[n : 2 * n])
    level = jnp.zeros((regions, units), F32)
    year = jnp.zeros((regions, units), F32)
    for h in range(hours):
        old = clip(-tau * get(costs, h), -high, high)
        new = clip(old - tau * (get(grad, h) + get(back, h) + year_scale * year_dual), -high, high)
        bar = 2.0 * new - old
        year = year + bar
        level = get(decay, h) * level + bar
    carry_pieces(carries_ref, rows, (carry_in(kept, level, False),))
    diagonal = lax.broadcasted_iota(jnp.int32, (regions, units), 0) == lane_ids((regions, units))
    for part, column in enumerate(halves(year)):
        line = jnp.sum(jnp.where(diagonal, year_scale * column, 0.0), axis=0, keepdims=True)
        year_ref[:, part * LANES : (part + 1) * LANES] = jnp.broadcast_to(line, (year_ref.shape[0], LANES))


def second_kernel(
    units, year_scale, year_bound,
    omega_ref, received_ref, cost_ref, back_ref, upper_ref, annual_ref, carries_ref,
    sent_ref, dual_ref, rows, dual, out, sems,
):
    regions, hours, width = cost_ref.shape
    omega = omega_ref[0:1, 0:1]
    tau, sigma = step_ratio / omega, step_ratio * omega
    rows[...] = jnp.zeros_like(rows)
    totals = year_totals(received_ref, rows.shape[0] // LANES, regions)
    for t, total in enumerate(totals):
        at = slice(t * LANES, (t + 1) * LANES)
        dual[:, at] = jnp.maximum(sigma * (total - year_bound * annual_ref[:, at]), 0.0)
    leaving = begin(dual, dual_ref, sems.at[1])
    for r in range(regions):
        high = upper_ref[r : r + 1, units:]
        costs = cost_ref[r, :, units:].astype(F32)
        old = clip(-tau * costs, 0.0, high)
        grad = costs + back_ref[r * hours : (r + 1) * hours, units:] + year_scale * dual[r : r + 1, units:]
        bar = 2.0 * clip(old - tau * grad, 0.0, high) - old
        sums = year_scale * jnp.sum(bar, axis=0, keepdims=True)
        for t in range(1, width // LANES):
            rows[t * PAD_ROWS + r : t * PAD_ROWS + r + 1, :] = sums[:, t * LANES - units : (t + 1) * LANES - units]
    year_pieces(rows, out)
    move_pieces(out, rows.shape[0] // LANES, out.shape[0] // (LANES // 2), carries_ref)
    begin(out, sent_ref, sems.at[0]).wait()
    leaving.wait()


def last_kernel(
    units, count, level_scale, year_scale, year_bound,
    place_ref, omega_ref, cost_ref, back_ref, upper_ref, dual_ref, conversion_ref, demand_ref, prices_ref,
    ends_ref, annual_ref, bus_ref, came_ref, received_ref, decay_ref, energy_ref,
    primal_ref, flows_ref, new_prices_ref, base_ref, slope_ref, year_ref,
    bar, held, demand, old_prices, dual, ends, annual, bus, bus_rows_ref, costs, decay, back, stored, new_stored, sems,
):
    copy, *others = [
        begin(source, target, sems.at[k])
        for k, (source, target) in enumerate(
            (
                (dual_ref, dual),
                (conversion_ref, held),
                (demand_ref, demand),
                (prices_ref, old_prices),
                (ends_ref, ends),
                (annual_ref, annual),
            )
        )
    ]
    regions, hours, width = cost_ref.shape
    bus_rows = demand_ref.shape[2]
    lines = flows_ref.shape[1]
    n = regions * hours
    get, put = strided(regions, hours)
    omega = omega_ref[0:1, 0:1]
    tau, sigma = step_ratio / omega, step_ratio * omega

    costs[...] = cost_ref[:, :, :units].astype(F32).reshape(n, units)
    decay[...] = decay_ref[...].reshape(n, units)
    back[...] = back_ref[:, :units]
    high = upper_ref[:, :units]
    energy = energy_ref[...]
    level, later = collect_carries(received_ref, count, regions, 2)
    for h in range(hours):
        level = get(decay, h) * level + 2.0 * clip(-tau * get(costs, h), -high, high)
        put(stored, h, jnp.maximum(sigma * (level_scale * level - energy), 0.0))
    copy.wait()
    year_part = year_scale * dual[:, :units]
    for h in reversed(range(hours)):
        weight = level_scale * get(stored, h) + later
        later = get(decay, h) * weight
        old = clip(-tau * get(costs, h), -high, high)
        put(new_stored, h, clip(old - tau * (get(costs, h) + get(back, h) + weight + year_part), -high, high))
    level = jnp.zeros((regions, units), F32)
    kept = jnp.ones((regions, units), F32)
    for h in range(hours):
        d = get(decay, h)
        second = 2.0 * get(new_stored, h) - clip(-tau * get(costs, h), -high, high)
        level = d * level + second
        kept = d * kept
        put(base_ref, h, get(stored, h) + sigma * (level_scale * level - energy))
        put(slope_ref, h, (sigma * level_scale) * kept)
        put(back, h, second)
    bar[:, :units] = back[...]
    for r in range(regions):
        at = slice(r * hours, (r + 1) * hours)
        high = upper_ref[r : r + 1, units:]
        row_costs = cost_ref[r, :, units:].astype(F32)
        old = clip(-tau * row_costs, 0.0, high)
        grad = row_costs + back_ref[at, units:] + year_scale * dual[r : r + 1, units:]
        new = clip(old - tau * grad, 0.0, high)
        bar[at, units:] = 2.0 * new - old
        primal_ref[r, :, :units] = new_stored[at, :].astype(BF16)
        primal_ref[r, :, units:] = new.astype(BF16)
    for other in others:
        other.wait()
    step = 256
    image = None
    for k in range(0, width, step):
        part = dot3(split(bar[:, k : k + step]), split(held[k : k + step, :]), ((1,), (0,)))
        image = part if image is None else image + part
    loads = demand[...].astype(F32).reshape(n, bus_rows)
    new_prices_ref[...] = old_prices[...] + sigma * (image - loads)

    year_ref[...] = dual[...] - (sigma * year_bound) * annual[...]
    grow(bus_ref, came_ref, bus)
    groups, reach = bus.shape
    regions_all = groups * regions
    first_region = place_ref[0] * regions
    for r in range(regions):
        moved = bus[...] if r == 0 else pltpu.roll(bus[...], reach - r * hours, 1)
        bus_rows_ref[r * groups : (r + 1) * groups, :] = moved[:, :LANES]

    def exact(a, b, dims):
        return lax.dot_general(
            a, b, (dims, ((), ())), precision=lax.Precision.HIGHEST, preferred_element_type=F32
        )

    def incidence(ids):
        ids = ids + first_region
        ids = jnp.where(ids >= regions_all, ids - regions_all, ids).astype(F32)
        return (ids == ends[1:2, :]).astype(F32) - (ids == ends[0:1, :]).astype(F32)

    def rows_like(count):
        return lax.broadcasted_iota(jnp.int32, (count, ends.shape[1]), 0)

    caps = ends[2:3, :]
    at = rows_like(regions_all)
    place = lax.bitwise_and(at, groups - 1) * regions + lax.shift_right_logical(at, groups.bit_length() - 1)
    grad = exact(bus_rows_ref[...], incidence(place), ((0,), (0,)))
    flows = clip(-tau * grad[:hours, :], -caps, caps)
    own = flows[:, :lines]
    for g in range(1, groups):
        own = jnp.where(place_ref[0] == g, flows[:, g * lines : (g + 1) * lines], own)
    flows_ref[...] = own
    inflow = exact(2.0 * flows, incidence(rows_like(LANES)), ((1,), (1,)))
    ids = lane_ids(inflow.shape)
    for r in range(regions):
        moved = inflow if r == 0 else pltpu.roll(inflow, LANES - r, 1)
        at = slice(r * hours, (r + 1) * hours)
        new_prices_ref[at, :LANES] = new_prices_ref[at, :LANES] + sigma * jnp.where(ids == 0, moved, 0.0)


def finish_kernel(count, omega_ref, received_ref, base_ref, slope_ref, rest_ref, storage_ref, year_ref):
    regions = rest_ref.shape[0]
    hours = base_ref.shape[0] // regions
    sigma = step_ratio * omega_ref[0:1, 0:1]
    for t, total in enumerate(year_totals(received_ref, count, regions)):
        at = slice(t * LANES, (t + 1) * LANES)
        year_ref[:, at] = jnp.maximum(rest_ref[:, at] + sigma * total, 0.0)
    (entering,) = collect_carries(received_ref, count, regions, 1)
    for r in range(regions):
        at = slice(r * hours, (r + 1) * hours)
        storage_ref[at, :] = jnp.maximum(base_ref[at, :] + slope_ref[at, :] * entering[r : r + 1, :], 0.0)


def exchange(x):
    blocks = lax.axis_size("tm")
    pieces = x.reshape(blocks, 1, x.size // blocks)
    return lax.all_to_all(pieces, "tm", 0, 0, tiled=True).reshape(x.shape)


def per_device(cost, demand, conversion, upper, decay, energy_cap, annual_cap, line_ends, line_cap):
    hours, regions, width = cost.shape
    bus_rows = demand.shape[2]
    units = decay.shape[2]
    lines = line_ends.shape[0]
    blocks = lax.axis_size("tm")
    groups = lax.axis_size("region")
    hours_all = hours * blocks
    scale = 1.0 / math.sqrt(hours_all)
    bound = math.sqrt(hours_all)
    n = regions * hours
    year_rows = 2 * PAD_ROWS * (width // LANES)
    year_count = year_rows // LANES
    turned_count = 4 * n // LANES
    back_count = -(-2 * n // LANES)
    rows = lambda k: pltpu.VMEM((k, LANES), F32)
    sems = lambda k: pltpu.SemaphoreType.DMA((k,))
    pieces = lambda count: struct(blocks * count, LANES)
    sent = lambda count: in_hbm(blocks * count, LANES)
    cost = jnp.transpose(cost, (1, 0, 2))
    demand = jnp.transpose(demand, (1, 0, 2))
    decay = jnp.transpose(decay, (1, 0, 2))
    tm_place = lax.axis_index("tm").astype(jnp.int32).reshape(1)
    region_place = lax.axis_index("region").astype(jnp.int32).reshape(1)

    def from_ahead(x, reach):
        return lax.ppermute(x, "region", [((z + reach) % groups, z) for z in range(groups)])

    sums = call(
        sums_kernel,
        in_hbm(groups, LANES),
        "sums",
        [HBM] * 4,
        [
            pltpu.VMEM((regions, hours, width), BF16),
            pltpu.VMEM((regions, hours, bus_rows), BF16),
            pltpu.VMEM((2, lines), jnp.int32),
            pltpu.VMEM((1, lines), F32),
            rows(groups),
            sems(5),
        ],
        HBM,
    )(keep(cost), keep(demand), keep(line_ends.T), keep(line_cap.reshape(1, -1)))
    sums = lax.all_to_all(sums.reshape(groups, 1, LANES), "region", 0, 0, tiled=True).reshape(groups, LANES)
    ends = sums[:, LANES - 3 * lines :].reshape(groups, 3, lines).transpose(1, 0, 2).reshape(3, groups * lines)
    turned = call(turn_kernel, pieces(turned_count), "turn", [VMEM] * 2, [rows(4 * n)])(cost, decay)
    joined_count = 1 + turned_count
    joined = call(
        join_kernel, sent(joined_count), "join", [VMEM] * 2, [rows(blocks * joined_count), sems(1)], HBM
    )(sums, turned)
    joined = exchange(joined)
    omega, first = call(
        functools.partial(first_kernel, units, scale),
        (struct(8, LANES), sent(year_count)),
        "first_primal",
        [VMEM] * 3,
        [rows(blocks * year_count), rows(year_rows), sems(1)],
        (VMEM, HBM),
    )(joined, cost, upper)
    first = exchange(first)

    reach = -(-n // LANES) * LANES
    prices, back, back_turned, bus = call(
        functools.partial(prices_kernel, units),
        (in_hbm(n, bus_rows), struct(n, width), pieces(back_count), struct(1, reach)),
        "first_prices",
        [VMEM] * 3 + [HBM] * 2,
        [
            pltpu.VMEM((n, width), F32),
            rows(back_count * LANES),
            pltpu.VMEM((width, bus_rows), F32),
            pltpu.VMEM((regions, hours, bus_rows), BF16),
            pltpu.VMEM((n, bus_rows), F32),
            sems(2),
        ],
        (HBM, VMEM, VMEM, VMEM),
        flops=4000000000,
        nbytes=5000000,
    )(omega, cost, upper, keep(demand), keep(conversion))

    second_count = year_count + back_count
    second = call(
        functools.partial(sum_kernel, year_count),
        sent(second_count),
        "year_sum",
        [VMEM] * 2,
        [rows(blocks * second_count), sems(1)],
        HBM,
    )(first, back_turned)
    second = exchange(second)

    carries, costs_all, decay_all, grad_all, block, bus = call(
        functools.partial(storage_kernel, scale, scale, bound),
        (pieces(1),) + (struct(n, units),) * 3 + (struct(2 * PAD_ROWS, units), struct(2, reach)),
        "storage",
        [SMEM] + [VMEM] * 2 + [ANY] + [VMEM] * 5,
        [rows(n) for _ in range(5)] + [rows(LANES)],
        flops=4000000000,
    )(tm_place, omega, joined, first, upper, energy_cap, annual_cap, bus, from_ahead(bus, 1))

    third, year_dual = call(
        functools.partial(second_kernel, units, scale, bound),
        (sent(year_count + 1), in_hbm(regions, width)),
        "second_primal",
        [VMEM] * 7,
        [
            rows(year_rows),
            pltpu.VMEM((regions, width), F32),
            rows(blocks * (year_count + 1)),
            sems(2),
        ],
        (HBM, HBM),
    )(omega, second, cost, back, upper, annual_cap, carries)
    third = exchange(third)

    carry, stored_year, bus = call(
        functools.partial(storage_again_kernel, year_count, scale),
        (pieces(1), struct(8, year_rows), struct(4, reach)),
        "storage_again",
        [SMEM] + [VMEM] * 9 + [ANY],
        [rows(n), rows(LANES)],
        flops=4000000000,
    )(tm_place, omega, costs_all, decay_all, grad_all, block, second, upper, bus, from_ahead(bus, 2), year_dual)

    fourth = call(
        functools.partial(sum_with_stored_kernel, year_count),
        sent(year_count + 1),
        "year_sum_2",
        [VMEM] * 3,
        [rows(blocks * (year_count + 1)), sems(1)],
        HBM,
    )(third, stored_year, carry)
    fourth = exchange(fourth)

    new_primal, flows, prices, base, slope, rest = call(
        functools.partial(last_kernel, units, year_count, scale, scale, bound),
        (
            struct(regions, hours, width, dtype=BF16),
            struct(hours, lines),
            struct(n, bus_rows),
            struct(n, units),
            struct(n, units),
            struct(regions, width),
        ),
        "second_prices",
        [SMEM] + [VMEM] * 4 + [HBM] * 6 + [VMEM] * 5,
        [
            pltpu.VMEM((n, width), F32),
            pltpu.VMEM((width, bus_rows), F32),
            pltpu.VMEM((regions, hours, bus_rows), BF16),
            pltpu.VMEM((n, bus_rows), F32),
            pltpu.VMEM((regions, width), F32),
            pltpu.VMEM((3, groups * lines), F32),
            pltpu.VMEM((regions, width), F32),
            pltpu.VMEM((groups, reach), F32),
            rows(groups * regions),
        ]
        + [rows(n) for _ in range(5)]
        + [sems(6)],
        flops=3000000000,
        nbytes=6000000,
    )(
        region_place, omega, cost, back, upper, keep(year_dual), keep(conversion), keep(demand), keep(prices),
        keep(ends), keep(annual_cap), bus, from_ahead(bus, 4), third, decay, energy_cap,
    )
    storage_dual, year_dual = call(
        functools.partial(finish_kernel, year_count),
        (struct(n, units), struct(regions, width)),
        "finish",
        [VMEM] * 5,
    )(omega, fourth, base, slope, rest)
    turn = lambda x, last: jnp.transpose(x.reshape(regions, hours, last), (1, 0, 2))
    return (
        jnp.transpose(new_primal, (1, 0, 2)),
        flows,
        turn(prices, bus_rows),
        turn(storage_dual, units),
        year_dual,
    )


def solution(mesh):
    in_specs = (
        P("tm", "region", None),
        P("tm", "region", None),
        P(),
        P("region", None),
        P("tm", "region", None),
        P("region", None),
        P("region", None),
        P("region", None),
        P("region"),
    )
    out_specs = (
        P("tm", "region", None),
        P("tm", "region"),
        P("tm", "region", None),
        P("tm", "region", None),
        P("region", None),
    )
    return jax.shard_map(
        per_device, mesh=mesh, in_specs=in_specs, out_specs=out_specs, check_vma=False
    )
```

```python
import functools
import math

import jax
import jax.numpy as jnp
from jax import lax
from jax.experimental import pallas as pl
from jax.experimental.pallas import tpu as pltpu
from jax.sharding import PartitionSpec as P

F32 = jnp.float32
BF16 = jnp.bfloat16
LANES = 128
PAD_ROWS = 16
step_ratio = 0.5


VMEM = pl.BlockSpec(memory_space=pltpu.VMEM)
SMEM = pl.BlockSpec(memory_space=pltpu.SMEM)
HBM = pl.BlockSpec(memory_space=pltpu.HBM)
ANY = pl.BlockSpec(memory_space=pl.ANY)


def call(kernel, out_shape, name, in_specs, scratch=(), out_specs=None, aliases=None, flops=1000000, nbytes=1000000):
    if out_specs is None:
        out_specs = jax.tree.map(lambda _: VMEM, out_shape)
    return pl.pallas_call(
        kernel,
        out_shape=out_shape,
        in_specs=in_specs,
        out_specs=out_specs,
        scratch_shapes=list(scratch),
        name=name,
        input_output_aliases=aliases or {},
        compiler_params=pltpu.CompilerParams(vmem_limit_bytes=24 * 1024 * 1024),
        cost_estimate=pl.CostEstimate(flops=flops, bytes_accessed=nbytes, transcendentals=0),
    )


def struct(*shape, dtype=F32):
    return jax.ShapeDtypeStruct(shape, dtype)


def begin(source, target, sem):
    copy = pltpu.make_async_copy(source, target, sem)
    copy.start()
    return copy


def in_hbm(*shape, dtype=F32):
    return pltpu.HBM(shape, dtype)


def keep(x):
    return pltpu.with_memory_space_constraint(x, pltpu.HBM)


def lane_ids(shape):
    return lax.broadcasted_iota(jnp.int32, shape, len(shape) - 1)


def swap_halves(x):
    return pltpu.roll(x, LANES // 2, 1)


def spread(scratch):
    return jnp.transpose(scratch)[: LANES // 2, :]


def put_pieces(out_ref, first, per, value):
    for q in range(value.shape[1] // LANES):
        out_ref[pl.ds(first + q, LANES // 2, stride=per), :] = value[:, q * LANES : (q + 1) * LANES]


def move_pieces(out_ref, first, per, in_ref):
    count = in_ref.shape[0] // (LANES // 2)
    for q in range(count):
        out_ref[pl.ds(first + q, LANES // 2, stride=per), :] = in_ref[pl.ds(q, LANES // 2, stride=count), :]


def collect(ref, first, count):
    per = ref.shape[0] // (LANES // 2)
    parts = []
    for q in range(first, first + count):
        rows = ref[pl.ds(q, LANES // 2, stride=per), :]
        parts.append(jnp.transpose(jnp.concatenate([rows, jnp.zeros_like(rows)], axis=0)))
    return jnp.concatenate(parts, axis=0)


def sum_pieces(ref, count):
    per = ref.shape[0] // (LANES // 2)
    return [jnp.sum(ref[pl.ds(q, LANES // 2, stride=per), :], axis=0, keepdims=True) for q in range(count)]


def split(x):
    high = x.astype(BF16)
    return high, (x - high.astype(F32)).astype(BF16)


def dot(a, b, dims):
    return lax.dot_general(a, b, (dims, ((), ())), preferred_element_type=F32)


def dot3(a, b, dims):
    (ah, al), (bh, bl) = a, b
    return dot(ah, bh, dims) + (dot(ah, bl, dims) + dot(al, bh, dims))


def bounds(upper_row, units):
    return jnp.where(lane_ids(upper_row.shape) < units, -upper_row, 0.0), upper_row


def clip(x, low, high):
    return jnp.minimum(jnp.maximum(x, low), high)


def sums_kernel(
    cost_ref, demand_ref, ends_ref, caps_ref, sent_ref, cost, demand, ends, caps, out, sems
):
    regions = cost.shape[0]
    half = regions // 2
    copies = [
        begin(source, target, sems.at[k])
        for k, (source, target) in enumerate(
            (
                (cost_ref.at[pl.ds(0, half)], cost.at[pl.ds(0, half)]),
                (cost_ref.at[pl.ds(half, regions - half)], cost.at[pl.ds(half, regions - half)]),
                (demand_ref, demand),
                (ends_ref, ends),
                (caps_ref, caps),
            )
        )
    ]

    def add(ref, first, last, acc):
        for r in range(first, last):
            x = ref[r].astype(F32)
            acc = x * x if acc is None else acc + x * x
        return acc

    def total(acc):
        return jnp.sum(jnp.sum(acc, axis=0, keepdims=True), axis=1, keepdims=True)

    copies[0].wait()
    acc = add(cost, 0, half, None)
    copies[1].wait()
    cost_sum = total(add(cost, half, regions, acc))
    copies[2].wait()
    load_sum = total(add(demand, 0, regions, None))
    ids = lane_ids((1, LANES))
    row = jnp.where(ids == 0, cost_sum, jnp.where(ids == 1, load_sum, 0.0))
    copies[3].wait()
    copies[4].wait()
    lines = ends.shape[1]
    ends_row = ends[...].astype(F32)
    row = row + jnp.concatenate(
        [jnp.zeros((1, LANES - 3 * lines), F32), ends_row[0:1, :], ends_row[1:2, :], caps[...]], axis=1
    )
    out[...] = jnp.broadcast_to(row, out.shape)
    begin(out, sent_ref, sems.at[0]).wait()


def join_kernel(sums_ref, turned_ref, sent_ref, out, sems):
    per = out.shape[0] // (LANES // 2)
    row = jnp.sum(sums_ref[...], axis=0, keepdims=True)
    out[pl.ds(0, LANES // 2, stride=per), :] = jnp.broadcast_to(row, (LANES // 2, LANES))
    move_pieces(out, 1, per, turned_ref)
    begin(out, sent_ref, sems.at[0]).wait()


def turn_kernel(cost_ref, decay_ref, out_ref, rows):
    regions, hours, units = decay_ref.shape
    n = regions * hours
    costs = cost_ref[:, :, :units].astype(F32).reshape(n, units)
    decay = decay_ref[...].reshape(n, units)
    for place, x in enumerate((costs, swap_halves(costs), decay, swap_halves(decay))):
        rows[place * n : (place + 1) * n, :] = x
    put_pieces(out_ref, 0, out_ref.shape[0] // (LANES // 2), spread(rows[...]))


def year_pieces(rows, out_ref):
    half = rows.shape[0] // 2
    rows[half:, :] = swap_halves(rows[:half, :])
    put_pieces(out_ref, 0, out_ref.shape[0] // (LANES // 2), spread(rows[...]))


def year_totals(received_ref, count, regions):
    x = collect(received_ref, 0, count)
    half = x.shape[0] // 2
    tiles = []
    for t in range(half // PAD_ROWS):
        at = t * PAD_ROWS
        tile = x[at : at + PAD_ROWS, :] + swap_halves(x[half + at : half + at + PAD_ROWS, :])
        tiles.append(tile[:regions, :])
    return tiles


def first_kernel(
    units, year_scale, joined_ref, cost_ref, upper_ref, omega_ref, sent_ref, out_ref, rows, sems
):
    regions, hours, width = cost_ref.shape
    (s,) = sum_pieces(joined_ref, 1)
    ids = lane_ids(s.shape)
    cost_sum = jnp.sum(jnp.where(ids == 0, s, 0.0), axis=1, keepdims=True)
    load_sum = jnp.sum(jnp.where(ids == 1, s, 0.0), axis=1, keepdims=True)
    omega = jnp.sqrt(cost_sum / load_sum)
    omega_ref[...] = jnp.broadcast_to(omega, omega_ref.shape)
    tau = step_ratio / omega
    rows[...] = jnp.zeros_like(rows)
    for r in range(regions):
        low, high = bounds(upper_ref[r : r + 1, :], units)
        primal = clip(-tau * cost_ref[r].astype(F32), low, high)
        sums = (2.0 * year_scale) * jnp.sum(primal, axis=0, keepdims=True)
        for t in range(width // LANES):
            rows[t * PAD_ROWS + r : t * PAD_ROWS + r + 1, :] = sums[:, t * LANES : (t + 1) * LANES]
    year_pieces(rows, out_ref)
    begin(out_ref, sent_ref, sems.at[0]).wait()


def prices_kernel(
    units, omega_ref, cost_ref, upper_ref, demand_ref, conversion_ref,
    prices_ref, bus_ref, bar, held, demand, new_prices, sems,
):
    copy = begin(conversion_ref, held, sems.at[0])
    demand_copy = begin(demand_ref, demand, sems.at[1])
    regions, hours, width = cost_ref.shape
    bus_rows = demand_ref.shape[2]
    n = regions * hours
    omega = omega_ref[0:1, 0:1]
    tau, sigma = step_ratio / omega, step_ratio * omega
    for r in range(regions):
        low, high = bounds(upper_ref[r : r + 1, :], units)
        bar[r * hours : (r + 1) * hours, :] = 2.0 * clip(-tau * cost_ref[r].astype(F32), low, high)
    copy.wait()
    step = 256
    image = None
    for k in range(0, width, step):
        part = dot3(split(bar[:, k : k + step]), split(held[k : k + step, :]), ((1,), (0,)))
        image = part if image is None else image + part
    demand_copy.wait()
    loads = demand[...].astype(F32).reshape(n, bus_rows)
    prices = sigma * (image - loads)
    new_prices[...] = prices
    leaving = begin(new_prices, prices_ref, sems.at[0])
    bus = jnp.transpose(prices[:, :LANES])[0:1, :]
    bus_ref[...] = jnp.concatenate([bus, jnp.zeros((1, bus_ref.shape[1] - n), F32)], axis=1)
    leaving.wait()


def back_kernel(units, prices_ref, conversion_ref, back_ref, turned_ref, rows, prices, held, sems):
    copies = [begin(prices_ref, prices, sems.at[0]), begin(conversion_ref, held, sems.at[1])]
    n, width = back_ref.shape
    for copy in copies:
        copy.wait()
    cut = split(prices[...])
    step = 256
    for k in range(0, width, step):
        back_ref[:, k : k + step] = dot3(cut, split(held[k : k + step, :]), ((1,), (1,)))
    stored = back_ref[:, :units]
    rows[:n, :] = stored
    rows[n : 2 * n, :] = swap_halves(stored)
    rows[2 * n :, :] = jnp.zeros_like(rows[2 * n :, :])
    put_pieces(turned_ref, 0, turned_ref.shape[0] // (LANES // 2), spread(rows[...]))


def sum_kernel(count, received_ref, added_ref, bus_ref, came_ref, sent_ref, grown_ref, out_ref, sems):
    per = out_ref.shape[0] // (LANES // 2)
    for q, total in enumerate(sum_pieces(received_ref, count)):
        out_ref[pl.ds(q, LANES // 2, stride=per), :] = jnp.broadcast_to(total, (LANES // 2, LANES))
    move_pieces(out_ref, count, per, added_ref)
    copy = begin(out_ref, sent_ref, sems.at[0])
    grow(bus_ref, came_ref, grown_ref)
    copy.wait()


def grow(bus_ref, came_ref, grown_ref):
    grown_ref[: bus_ref.shape[0], :] = bus_ref[...]
    grown_ref[bus_ref.shape[0] :, :] = came_ref[...]


def sum_with_stored_kernel(count, received_ref, stored_ref, added_ref, order_ref, sent_ref, out_ref, sems):
    del order_ref
    per = out_ref.shape[0] // (LANES // 2)
    for q, total in enumerate(sum_pieces(received_ref, count)):
        if q % (count // 2) == 0:
            stored = stored_ref[0:1, (q // (count // 2)) * LANES : (q // (count // 2) + 1) * LANES]
            total = jnp.where(lane_ids(total.shape) < PAD_ROWS, stored, total)
        out_ref[pl.ds(q, LANES // 2, stride=per), :] = jnp.broadcast_to(total, (LANES // 2, LANES))
    move_pieces(out_ref, count, per, added_ref)
    begin(out_ref, sent_ref, sems.at[0]).wait()


def before(x, k, reverse):
    ids = lax.rem(lane_ids(x.shape), LANES // 2)
    if reverse:
        return pltpu.roll(x, LANES - k, 1), ids < LANES // 2 - k
    return pltpu.roll(x, k, 1), ids >= k


def carry_in(scale, offset, reverse):
    k = 1
    while k < LANES // 2:
        scale_before, ok = before(scale, k, reverse)
        offset_before, _ = before(offset, k, reverse)
        offset = jnp.where(ok, scale * offset_before + offset, offset)
        scale = jnp.where(ok, scale * scale_before, scale)
        k *= 2
    entering, ok = before(offset, 1, reverse)
    return jnp.where(ok, entering, 0.0)


def strided(regions, hours):
    def get(ref, h):
        return ref[pl.ds(h, regions, stride=hours), :]

    def put(ref, h, value):
        ref[pl.ds(h, regions, stride=hours), :] = value

    return get, put


def owned(place, x):
    ids = lane_ids(x.shape)
    half = LANES // 2
    first = jnp.sum(jnp.where(ids == place, x, 0.0), axis=1, keepdims=True)
    second = jnp.sum(jnp.where(ids == place + half, x, 0.0), axis=1, keepdims=True)
    return jnp.where(ids < half, first, second)


def halves(x):
    left = lane_ids(x.shape) < LANES // 2
    return (
        jnp.sum(jnp.where(left, x, 0.0), axis=1, keepdims=True),
        jnp.sum(jnp.where(left, 0.0, x), axis=1, keepdims=True),
    )


def carry_pieces(out_ref, rows, carries):
    regions = carries[0].shape[0]
    rows[...] = jnp.zeros_like(rows)
    for k, carry in enumerate(carries):
        at = 2 * k * PAD_ROWS
        rows[at : at + regions, :] = carry
        rows[at + PAD_ROWS : at + PAD_ROWS + regions, :] = swap_halves(carry)
    put_pieces(out_ref, 0, 1, spread(rows[...]))


def collect_carries(ref, q, regions, count):
    x = collect(ref, q, 1)
    found = []
    for k in range(count):
        at = 2 * k * PAD_ROWS
        found.append(x[at : at + regions, :] + swap_halves(x[at + PAD_ROWS : at + PAD_ROWS + regions, :]))
    return found


def storage_kernel(
    level_scale, year_scale, year_bound,
    place_ref, omega_ref, joined_ref, order_ref, upper_ref, energy_ref, annual_ref,
    carries_ref, costs, decay, grad, block_ref, run, scale, dual, suffix, suffix_scale, rows,
):
    del order_ref
    regions, units = energy_ref.shape
    n = costs.shape[0]
    hours = n // regions
    get, put = strided(regions, hours)
    place = place_ref[0]
    omega = omega_ref[0:1, 0:1]
    tau, sigma = step_ratio / omega, step_ratio * omega
    high = owned(place, upper_ref[:, :units])
    energy = owned(place, energy_ref[...])
    annual = owned(place, annual_ref[:, :units])
    x = collect(joined_ref, 1, 4 * n // LANES)
    costs[...] = x[:n] + swap_halves(x[n : 2 * n])
    decay[...] = x[2 * n : 3 * n] + swap_halves(x[3 * n :])

    level = jnp.zeros((regions, units), F32)
    kept = jnp.ones((regions, units), F32)
    year = jnp.zeros((regions, units), F32)
    for h in range(hours):
        d = get(decay, h)
        bar = 2.0 * clip(-tau * get(costs, h), -high, high)
        year = year + bar
        level = d * level + bar
        kept = kept * d
        put(run, h, level)
        put(scale, h, kept)
    entering = carry_in(kept, level, False)
    first, second = halves(year)
    total = year_scale * jnp.where(lane_ids(year.shape) < LANES // 2, first, second)
    block_ref[...] = jnp.zeros_like(block_ref)
    block_ref[:regions, :] = kept
    block_ref[PAD_ROWS : PAD_ROWS + regions, :] = jnp.maximum(sigma * (total - year_bound * annual), 0.0)
    after = jnp.zeros((regions, units), F32)
    after_kept = jnp.ones((regions, units), F32)
    for h in reversed(range(hours)):
        d = get(decay, h)
        level = get(run, h) + get(scale, h) * entering
        stored = level_scale * jnp.maximum(sigma * (level_scale * level - energy), 0.0)
        put(dual, h, stored)
        after = d * (stored + after)
        after_kept = after_kept * d
        put(suffix, h, after)
        put(suffix_scale, h, after_kept)
    closing = carry_in(after_kept, after, True)
    for h in range(hours):
        later = closing if h == hours - 1 else get(suffix, h + 1) + get(suffix_scale, h + 1) * closing
        put(grad, h, get(costs, h) + (get(dual, h) + later))
    carry_pieces(carries_ref, rows, (entering, closing))


def storage_again_kernel(
    count, year_scale, place_ref, omega_ref, costs, decay, grad, block_ref, received_ref, upper_ref,
    bus_ref, came_ref, order_ref, carries_ref, year_ref, grown_ref, back, rows,
):
    del order_ref
    n, units = costs.shape
    regions = upper_ref.shape[0]
    hours = n // regions
    get, _ = strided(regions, hours)
    grow(bus_ref, came_ref, grown_ref)
    omega = omega_ref[0:1, 0:1]
    tau = step_ratio / omega
    high = owned(place_ref[0], upper_ref[:, :units])
    kept = block_ref[:regions, :]
    year_dual = block_ref[PAD_ROWS : PAD_ROWS + regions, :]
    x = collect(received_ref, count, -(-2 * n // LANES))
    back[...] = x[:n] + swap_halves(x[n : 2 * n])
    level = jnp.zeros((regions, units), F32)
    year = jnp.zeros((regions, units), F32)
    for h in range(hours):
        old = clip(-tau * get(costs, h), -high, high)
        new = clip(old - tau * (get(grad, h) + get(back, h) + year_scale * year_dual), -high, high)
        bar = 2.0 * new - old
        year = year + bar
        level = get(decay, h) * level + bar
    carry_pieces(carries_ref, rows, (carry_in(kept, level, False),))
    diagonal = lax.broadcasted_iota(jnp.int32, (regions, units), 0) == lane_ids((regions, units))
    for part, column in enumerate(halves(year)):
        line = jnp.sum(jnp.where(diagonal, year_scale * column, 0.0), axis=0, keepdims=True)
        year_ref[:, part * LANES : (part + 1) * LANES] = jnp.broadcast_to(line, (year_ref.shape[0], LANES))


def second_kernel(
    units, year_scale, year_bound,
    omega_ref, received_ref, cost_ref, back_ref, upper_ref, annual_ref, carries_ref, order_ref,
    sent_ref, dual_ref, rows, dual, out, sems,
):
    del order_ref
    regions, hours, width = cost_ref.shape
    omega = omega_ref[0:1, 0:1]
    tau, sigma = step_ratio / omega, step_ratio * omega
    rows[...] = jnp.zeros_like(rows)
    totals = year_totals(received_ref, rows.shape[0] // LANES, regions)
    for t, total in enumerate(totals):
        at = slice(t * LANES, (t + 1) * LANES)
        dual[:, at] = jnp.maximum(sigma * (total - year_bound * annual_ref[:, at]), 0.0)
    leaving = begin(dual, dual_ref, sems.at[1])
    for r in range(regions):
        high = upper_ref[r : r + 1, units:]
        costs = cost_ref[r, :, units:].astype(F32)
        old = clip(-tau * costs, 0.0, high)
        grad = costs + back_ref[r * hours : (r + 1) * hours, units:] + year_scale * dual[r : r + 1, units:]
        bar = 2.0 * clip(old - tau * grad, 0.0, high) - old
        sums = year_scale * jnp.sum(bar, axis=0, keepdims=True)
        for t in range(1, width // LANES):
            rows[t * PAD_ROWS + r : t * PAD_ROWS + r + 1, :] = sums[:, t * LANES - units : (t + 1) * LANES - units]
    year_pieces(rows, out)
    move_pieces(out, rows.shape[0] // LANES, out.shape[0] // (LANES // 2), carries_ref)
    begin(out, sent_ref, sems.at[0]).wait()
    leaving.wait()


def last_kernel(
    shifts, units, count, level_scale, year_scale, year_bound,
    place_ref, omega_ref, cost_ref, back_ref, upper_ref, dual_ref, conversion_ref, demand_ref, prices_ref,
    ends_ref, annual_ref, bus_ref, came_ref, received_ref, decay_ref, energy_ref,
    primal_ref, flows_ref, new_prices_ref, base_ref, slope_ref, year_ref,
    bar, held, demand, old_prices, dual, ends, annual, bus, bus_rows_ref, costs, decay, back, stored, new_stored, sems,
):
    copy, *others = [
        begin(source, target, sems.at[k])
        for k, (source, target) in enumerate(
            (
                (dual_ref, dual),
                (conversion_ref, held),
                (demand_ref, demand),
                (prices_ref, old_prices),
                (ends_ref, ends),
                (annual_ref, annual),
            )
        )
    ]
    regions, hours, width = cost_ref.shape
    bus_rows = demand_ref.shape[2]
    lines = flows_ref.shape[1]
    n = regions * hours
    get, put = strided(regions, hours)
    omega = omega_ref[0:1, 0:1]
    tau, sigma = step_ratio / omega, step_ratio * omega

    costs[...] = cost_ref[:, :, :units].astype(F32).reshape(n, units)
    decay[...] = decay_ref[...].reshape(n, units)
    back[...] = back_ref[:, :units]
    high = upper_ref[:, :units]
    energy = energy_ref[...]
    level, later = collect_carries(received_ref, count, regions, 2)
    for h in range(hours):
        level = get(decay, h) * level + 2.0 * clip(-tau * get(costs, h), -high, high)
        put(stored, h, jnp.maximum(sigma * (level_scale * level - energy), 0.0))
    copy.wait()
    year_part = year_scale * dual[:, :units]
    for h in reversed(range(hours)):
        weight = level_scale * get(stored, h) + later
        later = get(decay, h) * weight
        old = clip(-tau * get(costs, h), -high, high)
        put(new_stored, h, clip(old - tau * (get(costs, h) + get(back, h) + weight + year_part), -high, high))
    level = jnp.zeros((regions, units), F32)
    kept = jnp.ones((regions, units), F32)
    for h in range(hours):
        d = get(decay, h)
        second = 2.0 * get(new_stored, h) - clip(-tau * get(costs, h), -high, high)
        level = d * level + second
        kept = d * kept
        put(base_ref, h, get(stored, h) + sigma * (level_scale * level - energy))
        put(slope_ref, h, (sigma * level_scale) * kept)
        put(back, h, second)
    bar[:, :units] = back[...]
    for r in range(regions):
        at = slice(r * hours, (r + 1) * hours)
        high = upper_ref[r : r + 1, units:]
        row_costs = cost_ref[r, :, units:].astype(F32)
        old = clip(-tau * row_costs, 0.0, high)
        grad = row_costs + back_ref[at, units:] + year_scale * dual[r : r + 1, units:]
        new = clip(old - tau * grad, 0.0, high)
        bar[at, units:] = 2.0 * new - old
        primal_ref[r, :, :units] = new_stored[at, :].astype(BF16)
        primal_ref[r, :, units:] = new.astype(BF16)
    for other in others:
        other.wait()
    step = 256
    image = None
    for k in range(0, width, step):
        part = dot3(split(bar[:, k : k + step]), split(held[k : k + step, :]), ((1,), (0,)))
        image = part if image is None else image + part
    loads = demand[...].astype(F32).reshape(n, bus_rows)
    new_prices_ref[...] = old_prices[...] + sigma * (image - loads)

    year_ref[...] = dual[...] - (sigma * year_bound) * annual[...]
    grow(bus_ref, came_ref, bus)
    groups, reach = bus.shape
    regions_all = groups * regions
    first_region = place_ref[0] * regions
    for r in range(regions):
        moved = bus[...] if r == 0 else pltpu.roll(bus[...], reach - r * hours, 1)
        bus_rows_ref[r * groups : (r + 1) * groups, :] = moved[:, :LANES]

    def exact(a, b, dims):
        return lax.dot_general(
            a, b, (dims, ((), ())), precision=lax.Precision.HIGHEST, preferred_element_type=F32
        )

    def incidence(ids):
        ids = ids + first_region
        ids = jnp.where(ids >= regions_all, ids - regions_all, ids).astype(F32)
        return (ids == ends[1:2, :]).astype(F32) - (ids == ends[0:1, :]).astype(F32)

    def rows_like(count):
        return lax.broadcasted_iota(jnp.int32, (count, ends.shape[1]), 0)

    caps = ends[2:3, :]
    at = rows_like(regions_all)
    place = lax.shift_right_logical(at, groups.bit_length() - 1)
    for k, shift in enumerate(shifts):
        bit = lax.bitwise_and(lax.shift_right_logical(at, k), 1)
        place = place + bit * (shift * regions)
    grad = exact(bus_rows_ref[...], incidence(place), ((0,), (0,)))
    flows = clip(-tau * grad[:hours, :], -caps, caps)
    own = flows[:, :lines]
    for g in range(1, groups):
        own = jnp.where(place_ref[0] == g, flows[:, g * lines : (g + 1) * lines], own)
    flows_ref[...] = own
    inflow = exact(2.0 * flows, incidence(rows_like(LANES)), ((1,), (1,)))
    ids = lane_ids(inflow.shape)
    for r in range(regions):
        moved = inflow if r == 0 else pltpu.roll(inflow, LANES - r, 1)
        at = slice(r * hours, (r + 1) * hours)
        new_prices_ref[at, :LANES] = new_prices_ref[at, :LANES] + sigma * jnp.where(ids == 0, moved, 0.0)


def finish_kernel(count, omega_ref, received_ref, base_ref, slope_ref, rest_ref, storage_ref, year_ref):
    regions = rest_ref.shape[0]
    hours = base_ref.shape[0] // regions
    sigma = step_ratio * omega_ref[0:1, 0:1]
    for t, total in enumerate(year_totals(received_ref, count, regions)):
        at = slice(t * LANES, (t + 1) * LANES)
        year_ref[:, at] = jnp.maximum(rest_ref[:, at] + sigma * total, 0.0)
    (entering,) = collect_carries(received_ref, count, regions, 1)
    for r in range(regions):
        at = slice(r * hours, (r + 1) * hours)
        storage_ref[at, :] = jnp.maximum(base_ref[at, :] + slope_ref[at, :] * entering[r : r + 1, :], 0.0)


def exchange(x):
    blocks = lax.axis_size("tm")
    pieces = x.reshape(blocks, 1, x.size // blocks)
    return lax.all_to_all(pieces, "tm", 0, 0, tiled=True).reshape(x.shape)


def per_device(cost, demand, conversion, upper, decay, energy_cap, annual_cap, line_ends, line_cap):
    hours, regions, width = cost.shape
    bus_rows = demand.shape[2]
    units = decay.shape[2]
    lines = line_ends.shape[0]
    blocks = lax.axis_size("tm")
    groups = lax.axis_size("region")
    hours_all = hours * blocks
    scale = 1.0 / math.sqrt(hours_all)
    bound = math.sqrt(hours_all)
    n = regions * hours
    year_rows = 2 * PAD_ROWS * (width // LANES)
    year_count = year_rows // LANES
    turned_count = 4 * n // LANES
    back_count = -(-2 * n // LANES)
    rows = lambda k: pltpu.VMEM((k, LANES), F32)
    sems = lambda k: pltpu.SemaphoreType.DMA((k,))
    pieces = lambda count: struct(blocks * count, LANES)
    sent = lambda count: in_hbm(blocks * count, LANES)
    cost = jnp.transpose(cost, (1, 0, 2))
    demand = jnp.transpose(demand, (1, 0, 2))
    decay = jnp.transpose(decay, (1, 0, 2))
    tm_place = lax.axis_index("tm").astype(jnp.int32).reshape(1)
    region_place = lax.axis_index("region").astype(jnp.int32).reshape(1)

    shifts = (2, 4, 1)

    def from_ahead(x, reach):
        return lax.ppermute(x, "region", [((z + reach) % groups, z) for z in range(groups)])

    sums = call(
        sums_kernel,
        in_hbm(groups, LANES),
        "sums",
        [HBM] * 4,
        [
            pltpu.VMEM((regions, hours, width), BF16),
            pltpu.VMEM((regions, hours, bus_rows), BF16),
            pltpu.VMEM((2, lines), jnp.int32),
            pltpu.VMEM((1, lines), F32),
            rows(groups),
            sems(5),
        ],
        HBM,
    )(keep(cost), keep(demand), keep(line_ends.T), keep(line_cap.reshape(1, -1)))
    sums = lax.all_to_all(sums.reshape(groups, 1, LANES), "region", 0, 0, tiled=True).reshape(groups, LANES)
    ends = sums[:, LANES - 3 * lines :].reshape(groups, 3, lines).transpose(1, 0, 2).reshape(3, groups * lines)
    turned = call(turn_kernel, pieces(turned_count), "turn", [VMEM] * 2, [rows(4 * n)])(cost, decay)
    joined_count = 1 + turned_count
    joined = call(
        join_kernel, sent(joined_count), "join", [VMEM] * 2, [rows(blocks * joined_count), sems(1)], HBM
    )(sums, turned)
    joined = exchange(joined)
    omega, first = call(
        functools.partial(first_kernel, units, scale),
        (struct(8, LANES), sent(year_count)),
        "first_primal",
        [VMEM] * 3,
        [rows(blocks * year_count), rows(year_rows), sems(1)],
        (VMEM, HBM),
    )(joined, cost, upper)
    first = exchange(first)

    reach = -(-n // LANES) * LANES
    prices, bus = call(
        functools.partial(prices_kernel, units),
        (in_hbm(n, bus_rows), struct(1, reach)),
        "first_prices",
        [VMEM] * 3 + [HBM] * 2,
        [
            pltpu.VMEM((n, width), F32),
            pltpu.VMEM((width, bus_rows), F32),
            pltpu.VMEM((regions, hours, bus_rows), BF16),
            pltpu.VMEM((n, bus_rows), F32),
            sems(2),
        ],
        (HBM, VMEM),
        flops=2000000000,
        nbytes=3000000,
    )(omega, cost, upper, keep(demand), keep(conversion))
    came = from_ahead(bus, shifts[0])
    back, back_turned = call(
        functools.partial(back_kernel, units),
        (struct(n, width), pieces(back_count)),
        "back",
        [HBM] * 2,
        [rows(back_count * LANES), pltpu.VMEM((n, bus_rows), F32), pltpu.VMEM((width, bus_rows), F32), sems(2)],
        flops=2000000000,
        nbytes=3000000,
    )(keep(prices), keep(conversion))

    second_count = year_count + back_count
    second, bus = call(
        functools.partial(sum_kernel, year_count),
        (sent(second_count), struct(2, reach)),
        "year_sum",
        [VMEM] * 4,
        [rows(blocks * second_count), sems(1)],
        (HBM, VMEM),
    )(first, back_turned, bus, came)
    came = from_ahead(bus, shifts[1])
    second = exchange(second)

    carries, costs_all, decay_all, grad_all, block = call(
        functools.partial(storage_kernel, scale, scale, bound),
        (pieces(1),) + (struct(n, units),) * 3 + (struct(2 * PAD_ROWS, units),),
        "storage",
        [SMEM] + [VMEM] * 2 + [ANY] + [VMEM] * 3,
        [rows(n) for _ in range(5)] + [rows(LANES)],
        flops=4000000000,
    )(tm_place, omega, joined, first, upper, energy_cap, annual_cap)

    third, year_dual = call(
        functools.partial(second_kernel, units, scale, bound),
        (sent(year_count + 1), in_hbm(regions, width)),
        "second_primal",
        [VMEM] * 7 + [ANY],
        [
            rows(year_rows),
            pltpu.VMEM((regions, width), F32),
            rows(blocks * (year_count + 1)),
            sems(2),
        ],
        (HBM, HBM),
    )(omega, second, cost, back, upper, annual_cap, carries, came)
    third = exchange(third)

    carry, stored_year, bus = call(
        functools.partial(storage_again_kernel, year_count, scale),
        (pieces(1), struct(8, year_rows), struct(4, reach)),
        "storage_again",
        [SMEM] + [VMEM] * 9 + [ANY],
        [rows(n), rows(LANES)],
        flops=4000000000,
    )(tm_place, omega, costs_all, decay_all, grad_all, block, second, upper, bus, came, year_dual)
    came = from_ahead(bus, shifts[2])

    fourth = call(
        functools.partial(sum_with_stored_kernel, year_count),
        sent(year_count + 1),
        "year_sum_2",
        [VMEM] * 3 + [ANY],
        [rows(blocks * (year_count + 1)), sems(1)],
        HBM,
    )(third, stored_year, carry, came)
    fourth = exchange(fourth)

    new_primal, flows, prices, base, slope, rest = call(
        functools.partial(last_kernel, shifts, units, year_count, scale, scale, bound),
        (
            struct(regions, hours, width, dtype=BF16),
            struct(hours, lines),
            struct(n, bus_rows),
            struct(n, units),
            struct(n, units),
            struct(regions, width),
        ),
        "second_prices",
        [SMEM] + [VMEM] * 4 + [HBM] * 6 + [VMEM] * 5,
        [
            pltpu.VMEM((n, width), F32),
            pltpu.VMEM((width, bus_rows), F32),
            pltpu.VMEM((regions, hours, bus_rows), BF16),
            pltpu.VMEM((n, bus_rows), F32),
            pltpu.VMEM((regions, width), F32),
            pltpu.VMEM((3, groups * lines), F32),
            pltpu.VMEM((regions, width), F32),
            pltpu.VMEM((groups, reach), F32),
            rows(groups * regions),
        ]
        + [rows(n) for _ in range(5)]
        + [sems(6)],
        flops=3000000000,
        nbytes=6000000,
    )(
        region_place, omega, cost, back, upper, keep(year_dual), keep(conversion), keep(demand), keep(prices),
        keep(ends), keep(annual_cap), bus, came, third, decay, energy_cap,
    )
    storage_dual, year_dual = call(
        functools.partial(finish_kernel, year_count),
        (struct(n, units), struct(regions, width)),
        "finish",
        [VMEM] * 5,
    )(omega, fourth, base, slope, rest)
    turn = lambda x, last: jnp.transpose(x.reshape(regions, hours, last), (1, 0, 2))
    return (
        jnp.transpose(new_primal, (1, 0, 2)),
        flows,
        turn(prices, bus_rows),
        turn(storage_dual, units),
        year_dual,
    )


def solution(mesh):
    in_specs = (
        P("tm", "region", None),
        P("tm", "region", None),
        P(),
        P("region", None),
        P("tm", "region", None),
        P("region", None),
        P("region", None),
        P("region", None),
        P("region"),
    )
    out_specs = (
        P("tm", "region", None),
        P("tm", "region"),
        P("tm", "region", None),
        P("tm", "region", None),
        P("region", None),
    )
    return jax.shard_map(
        per_device, mesh=mesh, in_specs=in_specs, out_specs=out_specs, check_vma=False
    )
```

```python
import functools
import math

import jax
import jax.numpy as jnp
from jax import lax
from jax.experimental import pallas as pl
from jax.experimental.pallas import tpu as pltpu
from jax.sharding import PartitionSpec as P

F32 = jnp.float32
BF16 = jnp.bfloat16
LANES = 128
PAD_ROWS = 16
step_ratio = 0.5


VMEM = pl.BlockSpec(memory_space=pltpu.VMEM)
SMEM = pl.BlockSpec(memory_space=pltpu.SMEM)
HBM = pl.BlockSpec(memory_space=pltpu.HBM)
ANY = pl.BlockSpec(memory_space=pl.ANY)


def call(kernel, out_shape, name, in_specs, scratch=(), out_specs=None, aliases=None, flops=1000000, nbytes=1000000):
    if out_specs is None:
        out_specs = jax.tree.map(lambda _: VMEM, out_shape)
    return pl.pallas_call(
        kernel,
        out_shape=out_shape,
        in_specs=in_specs,
        out_specs=out_specs,
        scratch_shapes=list(scratch),
        name=name,
        input_output_aliases=aliases or {},
        compiler_params=pltpu.CompilerParams(vmem_limit_bytes=24 * 1024 * 1024),
        cost_estimate=pl.CostEstimate(flops=flops, bytes_accessed=nbytes, transcendentals=0),
    )


def struct(*shape, dtype=F32):
    return jax.ShapeDtypeStruct(shape, dtype)


def begin(source, target, sem):
    copy = pltpu.make_async_copy(source, target, sem)
    copy.start()
    return copy


def in_hbm(*shape, dtype=F32):
    return pltpu.HBM(shape, dtype)


def keep(x):
    return pltpu.with_memory_space_constraint(x, pltpu.HBM)


def lane_ids(shape):
    return lax.broadcasted_iota(jnp.int32, shape, len(shape) - 1)


def swap_halves(x):
    return pltpu.roll(x, LANES // 2, 1)


def spread(scratch):
    return jnp.transpose(scratch)[: LANES // 2, :]


def put_pieces(out_ref, first, per, value):
    for q in range(value.shape[1] // LANES):
        out_ref[pl.ds(first + q, LANES // 2, stride=per), :] = value[:, q * LANES : (q + 1) * LANES]


def move_pieces(out_ref, first, per, in_ref):
    count = in_ref.shape[0] // (LANES // 2)
    for q in range(count):
        out_ref[pl.ds(first + q, LANES // 2, stride=per), :] = in_ref[pl.ds(q, LANES // 2, stride=count), :]


def collect(ref, first, count):
    per = ref.shape[0] // (LANES // 2)
    parts = []
    for q in range(first, first + count):
        rows = ref[pl.ds(q, LANES // 2, stride=per), :]
        parts.append(jnp.transpose(jnp.concatenate([rows, jnp.zeros_like(rows)], axis=0)))
    return jnp.concatenate(parts, axis=0)


def sum_pieces(ref, count):
    per = ref.shape[0] // (LANES // 2)
    return [jnp.sum(ref[pl.ds(q, LANES // 2, stride=per), :], axis=0, keepdims=True) for q in range(count)]


def split(x):
    high = x.astype(BF16)
    return high, (x - high.astype(F32)).astype(BF16)


def dot(a, b, dims):
    return lax.dot_general(a, b, (dims, ((), ())), preferred_element_type=F32)


def dot3(a, b, dims):
    (ah, al), (bh, bl) = a, b
    return dot(ah, bh, dims) + (dot(ah, bl, dims) + dot(al, bh, dims))


def bounds(upper_row, units):
    return jnp.where(lane_ids(upper_row.shape) < units, -upper_row, 0.0), upper_row


def clip(x, low, high):
    return jnp.minimum(jnp.maximum(x, low), high)


def sums_kernel(
    cost_ref, demand_ref, ends_ref, caps_ref, sent_ref, cost, demand, ends, caps, out, sems
):
    regions = cost.shape[0]
    half = regions // 2
    copies = [
        begin(source, target, sems.at[k])
        for k, (source, target) in enumerate(
            (
                (cost_ref.at[pl.ds(0, half)], cost.at[pl.ds(0, half)]),
                (cost_ref.at[pl.ds(half, regions - half)], cost.at[pl.ds(half, regions - half)]),
                (demand_ref, demand),
                (ends_ref, ends),
                (caps_ref, caps),
            )
        )
    ]

    def add(ref, first, last, acc):
        for r in range(first, last):
            x = ref[r].astype(F32)
            acc = x * x if acc is None else acc + x * x
        return acc

    def total(acc):
        return jnp.sum(jnp.sum(acc, axis=0, keepdims=True), axis=1, keepdims=True)

    copies[0].wait()
    acc = add(cost, 0, half, None)
    copies[1].wait()
    cost_sum = total(add(cost, half, regions, acc))
    copies[2].wait()
    load_sum = total(add(demand, 0, regions, None))
    ids = lane_ids((1, LANES))
    row = jnp.where(ids == 0, cost_sum, jnp.where(ids == 1, load_sum, 0.0))
    copies[3].wait()
    copies[4].wait()
    lines = ends.shape[1]
    ends_row = ends[...].astype(F32)
    row = row + jnp.concatenate(
        [jnp.zeros((1, LANES - 3 * lines), F32), ends_row[0:1, :], ends_row[1:2, :], caps[...]], axis=1
    )
    out[...] = jnp.broadcast_to(row, out.shape)
    begin(out, sent_ref, sems.at[0]).wait()


def join_kernel(sums_ref, turned_ref, sent_ref, out, sems):
    per = out.shape[0] // (LANES // 2)
    row = jnp.sum(sums_ref[...], axis=0, keepdims=True)
    out[pl.ds(0, LANES // 2, stride=per), :] = jnp.broadcast_to(row, (LANES // 2, LANES))
    move_pieces(out, 1, per, turned_ref)
    begin(out, sent_ref, sems.at[0]).wait()


def turn_kernel(cost_ref, decay_ref, out_ref, rows):
    regions, hours, units = decay_ref.shape
    n = regions * hours
    costs = cost_ref[:, :, :units].astype(F32).reshape(n, units)
    decay = decay_ref[...].reshape(n, units)
    for place, x in enumerate((costs, swap_halves(costs), decay, swap_halves(decay))):
        rows[place * n : (place + 1) * n, :] = x
    put_pieces(out_ref, 0, out_ref.shape[0] // (LANES // 2), spread(rows[...]))


def year_pieces(rows, out_ref):
    half = rows.shape[0] // 2
    rows[half:, :] = swap_halves(rows[:half, :])
    put_pieces(out_ref, 0, out_ref.shape[0] // (LANES // 2), spread(rows[...]))


def year_totals(received_ref, count, regions):
    x = collect(received_ref, 0, count)
    half = x.shape[0] // 2
    tiles = []
    for t in range(half // PAD_ROWS):
        at = t * PAD_ROWS
        tile = x[at : at + PAD_ROWS, :] + swap_halves(x[half + at : half + at + PAD_ROWS, :])
        tiles.append(tile[:regions, :])
    return tiles


def first_kernel(
    units, year_scale, joined_ref, cost_ref, upper_ref, demand_ref, line_ref,
    omega_ref, bus_ref, sent_ref, out_ref, rows, column, sems
):
    regions, hours, width = cost_ref.shape
    (s,) = sum_pieces(joined_ref, 1)
    ids = lane_ids(s.shape)
    cost_sum = jnp.sum(jnp.where(ids == 0, s, 0.0), axis=1, keepdims=True)
    load_sum = jnp.sum(jnp.where(ids == 1, s, 0.0), axis=1, keepdims=True)
    omega = jnp.sqrt(cost_sum / load_sum)
    omega_ref[...] = jnp.broadcast_to(omega, omega_ref.shape)
    tau, sigma = step_ratio / omega, step_ratio * omega
    column[...] = jnp.zeros_like(column)
    rows[...] = jnp.zeros_like(rows)
    for r in range(regions):
        low, high = bounds(upper_ref[r : r + 1, :], units)
        primal = clip(-tau * cost_ref[r].astype(F32), low, high)
        image = jnp.sum((2.0 * primal) * line_ref[...], axis=1, keepdims=True)
        price = sigma * (image - demand_ref[r, :, 0:1].astype(F32))
        column[r * hours : (r + 1) * hours, :] = jnp.broadcast_to(price, (hours, LANES))
        sums = (2.0 * year_scale) * jnp.sum(primal, axis=0, keepdims=True)
        for t in range(width // LANES):
            rows[t * PAD_ROWS + r : t * PAD_ROWS + r + 1, :] = sums[:, t * LANES : (t + 1) * LANES]
    year_pieces(rows, out_ref)
    copy = begin(out_ref, sent_ref, sems.at[0])
    bus_ref[...] = jnp.transpose(column[...])[0:1, :]
    copy.wait()


def prices_kernel(
    units, omega_ref, cost_ref, upper_ref, demand_ref, conversion_ref,
    prices_ref, back_ref, turned_ref, bar, rows, demand, new_prices, sems,
):
    demand_copy = begin(demand_ref, demand, sems.at[1])
    regions, hours, width = cost_ref.shape
    bus_rows = demand_ref.shape[2]
    n = regions * hours
    omega = omega_ref[0:1, 0:1]
    tau, sigma = step_ratio / omega, step_ratio * omega
    for r in range(regions):
        low, high = bounds(upper_ref[r : r + 1, :], units)
        bar[r * hours : (r + 1) * hours, :] = 2.0 * clip(-tau * cost_ref[r].astype(F32), low, high)
    step = 256
    image = None
    for k in range(0, width, step):
        part = dot3(split(bar[:, k : k + step]), split(conversion_ref[k : k + step, :]), ((1,), (0,)))
        image = part if image is None else image + part
    demand_copy.wait()
    loads = demand[...].astype(F32).reshape(n, bus_rows)
    prices = sigma * (image - loads)
    new_prices[...] = prices
    leaving = begin(new_prices, prices_ref, sems.at[0])
    cut = split(prices)
    for k in range(0, width, step):
        back_ref[:, k : k + step] = dot3(cut, split(conversion_ref[k : k + step, :]), ((1,), (1,)))
    stored = back_ref[:, :units]
    rows[:n, :] = stored
    rows[n : 2 * n, :] = swap_halves(stored)
    rows[2 * n :, :] = jnp.zeros_like(rows[2 * n :, :])
    put_pieces(turned_ref, 0, turned_ref.shape[0] // (LANES // 2), spread(rows[...]))
    leaving.wait()


def sum_kernel(count, received_ref, added_ref, bus_ref, came_ref, sent_ref, grown_ref, out_ref, sems):
    per = out_ref.shape[0] // (LANES // 2)
    for q, total in enumerate(sum_pieces(received_ref, count)):
        out_ref[pl.ds(q, LANES // 2, stride=per), :] = jnp.broadcast_to(total, (LANES // 2, LANES))
    move_pieces(out_ref, count, per, added_ref)
    copy = begin(out_ref, sent_ref, sems.at[0])
    grow(bus_ref, came_ref, grown_ref)
    copy.wait()


def grow(bus_ref, came_ref, grown_ref):
    grown_ref[: bus_ref.shape[0], :] = bus_ref[...]
    grown_ref[bus_ref.shape[0] :, :] = came_ref[...]


def sum_with_stored_kernel(count, received_ref, stored_ref, added_ref, sent_ref, out_ref, sems):
    per = out_ref.shape[0] // (LANES // 2)
    for q, total in enumerate(sum_pieces(received_ref, count)):
        if q % (count // 2) == 0:
            stored = stored_ref[0:1, (q // (count // 2)) * LANES : (q // (count // 2) + 1) * LANES]
            total = jnp.where(lane_ids(total.shape) < PAD_ROWS, stored, total)
        out_ref[pl.ds(q, LANES // 2, stride=per), :] = jnp.broadcast_to(total, (LANES // 2, LANES))
    move_pieces(out_ref, count, per, added_ref)
    begin(out_ref, sent_ref, sems.at[0]).wait()


def before(x, k, reverse):
    ids = lax.rem(lane_ids(x.shape), LANES // 2)
    if reverse:
        return pltpu.roll(x, LANES - k, 1), ids < LANES // 2 - k
    return pltpu.roll(x, k, 1), ids >= k


def carry_in(scale, offset, reverse):
    k = 1
    while k < LANES // 2:
        scale_before, ok = before(scale, k, reverse)
        offset_before, _ = before(offset, k, reverse)
        offset = jnp.where(ok, scale * offset_before + offset, offset)
        scale = jnp.where(ok, scale * scale_before, scale)
        k *= 2
    entering, ok = before(offset, 1, reverse)
    return jnp.where(ok, entering, 0.0)


def strided(regions, hours):
    def get(ref, h):
        return ref[pl.ds(h, regions, stride=hours), :]

    def put(ref, h, value):
        ref[pl.ds(h, regions, stride=hours), :] = value

    return get, put


def owned(place, x):
    ids = lane_ids(x.shape)
    half = LANES // 2
    first = jnp.sum(jnp.where(ids == place, x, 0.0), axis=1, keepdims=True)
    second = jnp.sum(jnp.where(ids == place + half, x, 0.0), axis=1, keepdims=True)
    return jnp.where(ids < half, first, second)


def halves(x):
    left = lane_ids(x.shape) < LANES // 2
    return (
        jnp.sum(jnp.where(left, x, 0.0), axis=1, keepdims=True),
        jnp.sum(jnp.where(left, 0.0, x), axis=1, keepdims=True),
    )


def carry_pieces(out_ref, rows, carries):
    regions = carries[0].shape[0]
    rows[...] = jnp.zeros_like(rows)
    for k, carry in enumerate(carries):
        at = 2 * k * PAD_ROWS
        rows[at : at + regions, :] = carry
        rows[at + PAD_ROWS : at + PAD_ROWS + regions, :] = swap_halves(carry)
    put_pieces(out_ref, 0, 1, spread(rows[...]))


def collect_carries(ref, q, regions, count):
    x = collect(ref, q, 1)
    found = []
    for k in range(count):
        at = 2 * k * PAD_ROWS
        found.append(x[at : at + regions, :] + swap_halves(x[at + PAD_ROWS : at + PAD_ROWS + regions, :]))
    return found


def storage_kernel(
    level_scale, year_scale, year_bound,
    place_ref, omega_ref, joined_ref, order_ref, upper_ref, energy_ref, annual_ref,
    carries_ref, costs, decay, grad, block_ref, run, scale, dual, suffix, suffix_scale, rows,
):
    del order_ref
    regions, units = energy_ref.shape
    n = costs.shape[0]
    hours = n // regions
    get, put = strided(regions, hours)
    place = place_ref[0]
    omega = omega_ref[0:1, 0:1]
    tau, sigma = step_ratio / omega, step_ratio * omega
    high = owned(place, upper_ref[:, :units])
    energy = owned(place, energy_ref[...])
    annual = owned(place, annual_ref[:, :units])
    x = collect(joined_ref, 1, 4 * n // LANES)
    costs[...] = x[:n] + swap_halves(x[n : 2 * n])
    decay[...] = x[2 * n : 3 * n] + swap_halves(x[3 * n :])

    level = jnp.zeros((regions, units), F32)
    kept = jnp.ones((regions, units), F32)
    year = jnp.zeros((regions, units), F32)
    for h in range(hours):
        d = get(decay, h)
        bar = 2.0 * clip(-tau * get(costs, h), -high, high)
        year = year + bar
        level = d * level + bar
        kept = kept * d
        put(run, h, level)
        put(scale, h, kept)
    entering = carry_in(kept, level, False)
    first, second = halves(year)
    total = year_scale * jnp.where(lane_ids(year.shape) < LANES // 2, first, second)
    block_ref[...] = jnp.zeros_like(block_ref)
    block_ref[:regions, :] = kept
    block_ref[PAD_ROWS : PAD_ROWS + regions, :] = jnp.maximum(sigma * (total - year_bound * annual), 0.0)
    after = jnp.zeros((regions, units), F32)
    after_kept = jnp.ones((regions, units), F32)
    for h in reversed(range(hours)):
        d = get(decay, h)
        level = get(run, h) + get(scale, h) * entering
        stored = level_scale * jnp.maximum(sigma * (level_scale * level - energy), 0.0)
        put(dual, h, stored)
        after = d * (stored + after)
        after_kept = after_kept * d
        put(suffix, h, after)
        put(suffix_scale, h, after_kept)
    closing = carry_in(after_kept, after, True)
    for h in range(hours):
        later = closing if h == hours - 1 else get(suffix, h + 1) + get(suffix_scale, h + 1) * closing
        put(grad, h, get(costs, h) + (get(dual, h) + later))
    carry_pieces(carries_ref, rows, (entering, closing))


def storage_again_kernel(
    count, year_scale, place_ref, omega_ref, costs, decay, grad, block_ref, received_ref, upper_ref,
    bus_ref, came_ref, order_ref, carries_ref, year_ref, grown_ref, back, rows,
):
    del order_ref
    n, units = costs.shape
    regions = upper_ref.shape[0]
    hours = n // regions
    get, _ = strided(regions, hours)
    grow(bus_ref, came_ref, grown_ref)
    omega = omega_ref[0:1, 0:1]
    tau = step_ratio / omega
    high = owned(place_ref[0], upper_ref[:, :units])
    kept = block_ref[:regions, :]
    year_dual = block_ref[PAD_ROWS : PAD_ROWS + regions, :]
    x = collect(received_ref, count, -(-2 * n // LANES))
    back[...] = x[:n] + swap_halves(x[n : 2 * n])
    level = jnp.zeros((regions, units), F32)
    year = jnp.zeros((regions, units), F32)
    for h in range(hours):
        old = clip(-tau * get(costs, h), -high, high)
        new = clip(old - tau * (get(grad, h) + get(back, h) + year_scale * year_dual), -high, high)
        bar = 2.0 * new - old
        year = year + bar
        level = get(decay, h) * level + bar
    carry_pieces(carries_ref, rows, (carry_in(kept, level, False),))
    diagonal = lax.broadcasted_iota(jnp.int32, (regions, units), 0) == lane_ids((regions, units))
    for part, column in enumerate(halves(year)):
        line = jnp.sum(jnp.where(diagonal, year_scale * column, 0.0), axis=0, keepdims=True)
        year_ref[:, part * LANES : (part + 1) * LANES] = jnp.broadcast_to(line, (year_ref.shape[0], LANES))


def second_kernel(
    units, year_scale, year_bound,
    omega_ref, received_ref, cost_ref, back_ref, upper_ref, annual_ref, carries_ref,
    sent_ref, dual_ref, rows, dual, out, sems,
):
    regions, hours, width = cost_ref.shape
    omega = omega_ref[0:1, 0:1]
    tau, sigma = step_ratio / omega, step_ratio * omega
    rows[...] = jnp.zeros_like(rows)
    totals = year_totals(received_ref, rows.shape[0] // LANES, regions)
    for t, total in enumerate(totals):
        at = slice(t * LANES, (t + 1) * LANES)
        dual[:, at] = jnp.maximum(sigma * (total - year_bound * annual_ref[:, at]), 0.0)
    leaving = begin(dual, dual_ref, sems.at[1])
    for r in range(regions):
        high = upper_ref[r : r + 1, units:]
        costs = cost_ref[r, :, units:].astype(F32)
        old = clip(-tau * costs, 0.0, high)
        grad = costs + back_ref[r * hours : (r + 1) * hours, units:] + year_scale * dual[r : r + 1, units:]
        bar = 2.0 * clip(old - tau * grad, 0.0, high) - old
        sums = year_scale * jnp.sum(bar, axis=0, keepdims=True)
        for t in range(1, width // LANES):
            rows[t * PAD_ROWS + r : t * PAD_ROWS + r + 1, :] = sums[:, t * LANES - units : (t + 1) * LANES - units]
    year_pieces(rows, out)
    move_pieces(out, rows.shape[0] // LANES, out.shape[0] // (LANES // 2), carries_ref)
    begin(out, sent_ref, sems.at[0]).wait()
    leaving.wait()


def last_kernel(
    shifts, units, count, level_scale, year_scale, year_bound,
    place_ref, omega_ref, cost_ref, back_ref, upper_ref, dual_ref, conversion_ref, demand_ref, prices_ref,
    annual_ref, ends_ref, bus_ref, came_ref, received_ref, decay_ref, energy_ref,
    primal_ref, flows_ref, new_prices_ref, base_ref, slope_ref, year_ref,
    bar, held, demand, old_prices, dual, ends, annual, bus, bus_rows_ref, costs, decay, back, stored, new_stored, sems,
):
    copy, *others = [
        begin(source, target, sems.at[k])
        for k, (source, target) in enumerate(
            (
                (dual_ref, dual),
                (conversion_ref, held),
                (demand_ref, demand),
                (prices_ref, old_prices),
                (annual_ref, annual),
            )
        )
    ]
    regions, hours, width = cost_ref.shape
    bus_rows = demand_ref.shape[2]
    lines = flows_ref.shape[1]
    n = regions * hours
    get, put = strided(regions, hours)
    omega = omega_ref[0:1, 0:1]
    tau, sigma = step_ratio / omega, step_ratio * omega

    costs[...] = cost_ref[:, :, :units].astype(F32).reshape(n, units)
    decay[...] = decay_ref[...].reshape(n, units)
    back[...] = back_ref[:, :units]
    high = upper_ref[:, :units]
    energy = energy_ref[...]
    level, later = collect_carries(received_ref, count, regions, 2)
    for h in range(hours):
        level = get(decay, h) * level + 2.0 * clip(-tau * get(costs, h), -high, high)
        put(stored, h, jnp.maximum(sigma * (level_scale * level - energy), 0.0))
    copy.wait()
    year_part = year_scale * dual[:, :units]
    for h in reversed(range(hours)):
        weight = level_scale * get(stored, h) + later
        later = get(decay, h) * weight
        old = clip(-tau * get(costs, h), -high, high)
        put(new_stored, h, clip(old - tau * (get(costs, h) + get(back, h) + weight + year_part), -high, high))
    level = jnp.zeros((regions, units), F32)
    kept = jnp.ones((regions, units), F32)
    for h in range(hours):
        d = get(decay, h)
        second = 2.0 * get(new_stored, h) - clip(-tau * get(costs, h), -high, high)
        level = d * level + second
        kept = d * kept
        put(base_ref, h, get(stored, h) + sigma * (level_scale * level - energy))
        put(slope_ref, h, (sigma * level_scale) * kept)
        put(back, h, second)
    bar[:, :units] = back[...]
    for r in range(regions):
        at = slice(r * hours, (r + 1) * hours)
        high = upper_ref[r : r + 1, units:]
        row_costs = cost_ref[r, :, units:].astype(F32)
        old = clip(-tau * row_costs, 0.0, high)
        grad = row_costs + back_ref[at, units:] + year_scale * dual[r : r + 1, units:]
        new = clip(old - tau * grad, 0.0, high)
        bar[at, units:] = 2.0 * new - old
        primal_ref[r, :, :units] = new_stored[at, :].astype(BF16)
        primal_ref[r, :, units:] = new.astype(BF16)
    for other in others:
        other.wait()
    step = 256
    image = None
    for k in range(0, width, step):
        part = dot3(split(bar[:, k : k + step]), split(held[k : k + step, :]), ((1,), (0,)))
        image = part if image is None else image + part
    loads = demand[...].astype(F32).reshape(n, bus_rows)
    new_prices_ref[...] = old_prices[...] + sigma * (image - loads)

    year_ref[...] = dual[...] - (sigma * year_bound) * annual[...]
    grow(bus_ref, came_ref, bus)
    groups, reach = bus.shape
    regions_all = groups * regions
    first_region = place_ref[0] * regions
    for r in range(regions):
        moved = bus[...] if r == 0 else pltpu.roll(bus[...], reach - r * hours, 1)
        bus_rows_ref[r * groups : (r + 1) * groups, :] = moved[:, :LANES]

    def exact(a, b, dims):
        return lax.dot_general(
            a, b, (dims, ((), ())), precision=lax.Precision.HIGHEST, preferred_element_type=F32
        )

    def incidence(ids):
        ids = ids + first_region
        ids = jnp.where(ids >= regions_all, ids - regions_all, ids).astype(F32)
        return (ids == ends[1:2, :]).astype(F32) - (ids == ends[0:1, :]).astype(F32)

    ids = lane_ids((1, LANES))
    for part in range(3):
        for first in range(0, groups * lines, LANES):
            row = jnp.zeros((1, LANES), F32)
            for at in range(0, LANES, lines):
                g = (first + at) // lines
                turn = (at - (LANES - (3 - part) * lines)) % LANES
                moved = ends_ref[g : g + 1, :] if turn == 0 else pltpu.roll(ends_ref[g : g + 1, :], turn, 1)
                row = jnp.where(jnp.logical_and(ids >= at, ids < at + lines), moved, row)
            ends[part : part + 1, first : first + LANES] = row

    def rows_like(count):
        return lax.broadcasted_iota(jnp.int32, (count, ends.shape[1]), 0)

    caps = ends[2:3, :]
    at = rows_like(regions_all)
    place = lax.shift_right_logical(at, groups.bit_length() - 1)
    for k, shift in enumerate(shifts):
        bit = lax.bitwise_and(lax.shift_right_logical(at, k), 1)
        place = place + bit * (shift * regions)
    grad = exact(bus_rows_ref[...], incidence(place), ((0,), (0,)))
    flows = clip(-tau * grad[:hours, :], -caps, caps)
    own = flows[:, :lines]
    for g in range(1, groups):
        own = jnp.where(place_ref[0] == g, flows[:, g * lines : (g + 1) * lines], own)
    flows_ref[...] = own
    inflow = exact(2.0 * flows, incidence(rows_like(LANES)), ((1,), (1,)))
    ids = lane_ids(inflow.shape)
    for r in range(regions):
        moved = inflow if r == 0 else pltpu.roll(inflow, LANES - r, 1)
        at = slice(r * hours, (r + 1) * hours)
        new_prices_ref[at, :LANES] = new_prices_ref[at, :LANES] + sigma * jnp.where(ids == 0, moved, 0.0)


def finish_kernel(count, omega_ref, received_ref, base_ref, slope_ref, rest_ref, storage_ref, year_ref):
    regions = rest_ref.shape[0]
    hours = base_ref.shape[0] // regions
    sigma = step_ratio * omega_ref[0:1, 0:1]
    for t, total in enumerate(year_totals(received_ref, count, regions)):
        at = slice(t * LANES, (t + 1) * LANES)
        year_ref[:, at] = jnp.maximum(rest_ref[:, at] + sigma * total, 0.0)
    (entering,) = collect_carries(received_ref, count, regions, 1)
    for r in range(regions):
        at = slice(r * hours, (r + 1) * hours)
        storage_ref[at, :] = jnp.maximum(base_ref[at, :] + slope_ref[at, :] * entering[r : r + 1, :], 0.0)


def exchange(x):
    blocks = lax.axis_size("tm")
    pieces = x.reshape(blocks, 1, x.size // blocks)
    return lax.all_to_all(pieces, "tm", 0, 0, tiled=True).reshape(x.shape)


def per_device(cost, demand, conversion, upper, decay, energy_cap, annual_cap, line_ends, line_cap):
    hours, regions, width = cost.shape
    bus_rows = demand.shape[2]
    units = decay.shape[2]
    lines = line_ends.shape[0]
    blocks = lax.axis_size("tm")
    groups = lax.axis_size("region")
    hours_all = hours * blocks
    scale = 1.0 / math.sqrt(hours_all)
    bound = math.sqrt(hours_all)
    n = regions * hours
    year_rows = 2 * PAD_ROWS * (width // LANES)
    year_count = year_rows // LANES
    turned_count = 4 * n // LANES
    back_count = -(-2 * n // LANES)
    rows = lambda k: pltpu.VMEM((k, LANES), F32)
    sems = lambda k: pltpu.SemaphoreType.DMA((k,))
    pieces = lambda count: struct(blocks * count, LANES)
    sent = lambda count: in_hbm(blocks * count, LANES)
    cost = jnp.transpose(cost, (1, 0, 2))
    demand = jnp.transpose(demand, (1, 0, 2))
    decay = jnp.transpose(decay, (1, 0, 2))
    tm_place = lax.axis_index("tm").astype(jnp.int32).reshape(1)
    region_place = lax.axis_index("region").astype(jnp.int32).reshape(1)

    shifts = (1, 4, 2)

    def from_ahead(x, reach):
        return lax.ppermute(x, "region", [((z + reach) % groups, z) for z in range(groups)])

    sums = call(
        sums_kernel,
        in_hbm(groups, LANES),
        "sums",
        [HBM] * 4,
        [
            pltpu.VMEM((regions, hours, width), BF16),
            pltpu.VMEM((regions, hours, bus_rows), BF16),
            pltpu.VMEM((2, lines), jnp.int32),
            pltpu.VMEM((1, lines), F32),
            rows(groups),
            sems(5),
        ],
        HBM,
    )(keep(cost), keep(demand), keep(line_ends.T), keep(line_cap.reshape(1, -1)))
    sums = lax.all_to_all(sums.reshape(groups, 1, LANES), "region", 0, 0, tiled=True).reshape(groups, LANES)
    turned = call(turn_kernel, pieces(turned_count), "turn", [VMEM] * 2, [rows(4 * n)])(cost, decay)
    joined_count = 1 + turned_count
    joined = call(
        join_kernel, sent(joined_count), "join", [VMEM] * 2, [rows(blocks * joined_count), sems(1)], HBM
    )(sums, turned)
    joined = exchange(joined)
    reach = -(-n // LANES) * LANES
    omega, bus, first = call(
        functools.partial(first_kernel, units, scale),
        (struct(8, LANES), struct(1, reach), sent(year_count)),
        "first_primal",
        [VMEM] * 5,
        [rows(blocks * year_count), rows(year_rows), rows(reach), sems(1)],
        (VMEM, VMEM, HBM),
    )(joined, cost, upper, demand, conversion[:, :1].T)
    first = exchange(first)

    prices, back, back_turned = call(
        functools.partial(prices_kernel, units),
        (in_hbm(n, bus_rows), struct(n, width), pieces(back_count)),
        "first_prices",
        [VMEM] * 3 + [HBM, VMEM],
        [
            pltpu.VMEM((n, width), F32),
            rows(back_count * LANES),
            pltpu.VMEM((regions, hours, bus_rows), BF16),
            pltpu.VMEM((n, bus_rows), F32),
            sems(2),
        ],
        (HBM, VMEM, VMEM),
        flops=4000000000,
        nbytes=5000000,
    )(omega, cost, upper, keep(demand), conversion)

    second_count = year_count + back_count
    second, bus = call(
        functools.partial(sum_kernel, year_count),
        (sent(second_count), struct(2, reach)),
        "year_sum",
        [VMEM] * 4,
        [rows(blocks * second_count), sems(1)],
        (HBM, VMEM),
    )(first, back_turned, bus, from_ahead(bus, shifts[0]))
    second = exchange(second)

    carries, costs_all, decay_all, grad_all, block = call(
        functools.partial(storage_kernel, scale, scale, bound),
        (pieces(1),) + (struct(n, units),) * 3 + (struct(2 * PAD_ROWS, units),),
        "storage",
        [SMEM] + [VMEM] * 2 + [ANY] + [VMEM] * 3,
        [rows(n) for _ in range(5)] + [rows(LANES)],
        flops=4000000000,
    )(tm_place, omega, joined, first, upper, energy_cap, annual_cap)

    third, year_dual = call(
        functools.partial(second_kernel, units, scale, bound),
        (sent(year_count + 1), in_hbm(regions, width)),
        "second_primal",
        [VMEM] * 7,
        [
            rows(year_rows),
            pltpu.VMEM((regions, width), F32),
            rows(blocks * (year_count + 1)),
            sems(2),
        ],
        (HBM, HBM),
    )(omega, second, cost, back, upper, annual_cap, carries)
    third = exchange(third)

    carry, stored_year, bus = call(
        functools.partial(storage_again_kernel, year_count, scale),
        (pieces(1), struct(8, year_rows), struct(4, reach)),
        "storage_again",
        [SMEM] + [VMEM] * 9 + [HBM],
        [rows(n), rows(LANES)],
        flops=4000000000,
    )(tm_place, omega, costs_all, decay_all, grad_all, block, second, upper, bus, from_ahead(bus, shifts[1]), keep(year_dual))

    fourth = call(
        functools.partial(sum_with_stored_kernel, year_count),
        sent(year_count + 1),
        "year_sum_2",
        [VMEM] * 3,
        [rows(blocks * (year_count + 1)), sems(1)],
        HBM,
    )(third, stored_year, carry)
    fourth = exchange(fourth)

    new_primal, flows, prices, base, slope, rest = call(
        functools.partial(last_kernel, shifts, units, year_count, scale, scale, bound),
        (
            struct(regions, hours, width, dtype=BF16),
            struct(hours, lines),
            struct(n, bus_rows),
            struct(n, units),
            struct(n, units),
            struct(regions, width),
        ),
        "second_prices",
        [SMEM] + [VMEM] * 4 + [HBM] * 5 + [VMEM] * 6,
        [
            pltpu.VMEM((n, width), F32),
            pltpu.VMEM((width, bus_rows), F32),
            pltpu.VMEM((regions, hours, bus_rows), BF16),
            pltpu.VMEM((n, bus_rows), F32),
            pltpu.VMEM((regions, width), F32),
            pltpu.VMEM((3, groups * lines), F32),
            pltpu.VMEM((regions, width), F32),
            pltpu.VMEM((groups, reach), F32),
            rows(groups * regions),
        ]
        + [rows(n) for _ in range(5)]
        + [sems(5)],
        flops=3000000000,
        nbytes=6000000,
    )(
        region_place, omega, cost, back, upper, keep(year_dual), keep(conversion), keep(demand), keep(prices),
        keep(annual_cap), sums, bus, from_ahead(bus, shifts[2]), third, decay, energy_cap,
    )
    storage_dual, year_dual = call(
        functools.partial(finish_kernel, year_count),
        (struct(n, units), struct(regions, width)),
        "finish",
        [VMEM] * 5,
    )(omega, fourth, base, slope, rest)
    turn = lambda x, last: jnp.transpose(x.reshape(regions, hours, last), (1, 0, 2))
    return (
        jnp.transpose(new_primal, (1, 0, 2)),
        flows,
        turn(prices, bus_rows),
        turn(storage_dual, units),
        year_dual,
    )


def solution(mesh):
    in_specs = (
        P("tm", "region", None),
        P("tm", "region", None),
        P(),
        P("region", None),
        P("tm", "region", None),
        P("region", None),
        P("region", None),
        P("region", None),
        P("region"),
    )
    out_specs = (
        P("tm", "region", None),
        P("tm", "region"),
        P("tm", "region", None),
        P("tm", "region", None),
        P("region", None),
    )
    return jax.shard_map(
        per_device, mesh=mesh, in_specs=in_specs, out_specs=out_specs, check_vma=False
    )
```

```python
import functools
import math

import jax
import jax.numpy as jnp
from jax import lax
from jax.experimental import pallas as pl
from jax.experimental.pallas import tpu as pltpu
from jax.sharding import PartitionSpec as P

F32 = jnp.float32
BF16 = jnp.bfloat16
LANES = 128
PAD_ROWS = 16
step_ratio = 0.5


VMEM = pl.BlockSpec(memory_space=pltpu.VMEM)
SMEM = pl.BlockSpec(memory_space=pltpu.SMEM)
HBM = pl.BlockSpec(memory_space=pltpu.HBM)
ANY = pl.BlockSpec(memory_space=pl.ANY)


def call(kernel, out_shape, name, in_specs, scratch=(), out_specs=None, aliases=None, flops=1000000, nbytes=1000000):
    if out_specs is None:
        out_specs = jax.tree.map(lambda _: VMEM, out_shape)
    return pl.pallas_call(
        kernel,
        out_shape=out_shape,
        in_specs=in_specs,
        out_specs=out_specs,
        scratch_shapes=list(scratch),
        name=name,
        input_output_aliases=aliases or {},
        compiler_params=pltpu.CompilerParams(vmem_limit_bytes=24 * 1024 * 1024),
        cost_estimate=pl.CostEstimate(flops=flops, bytes_accessed=nbytes, transcendentals=0),
    )


def struct(*shape, dtype=F32):
    return jax.ShapeDtypeStruct(shape, dtype)


def begin(source, target, sem):
    copy = pltpu.make_async_copy(source, target, sem)
    copy.start()
    return copy


def in_hbm(*shape, dtype=F32):
    return pltpu.HBM(shape, dtype)


def keep(x):
    return pltpu.with_memory_space_constraint(x, pltpu.HBM)


def lane_ids(shape):
    return lax.broadcasted_iota(jnp.int32, shape, len(shape) - 1)


def swap_halves(x):
    return pltpu.roll(x, LANES // 2, 1)


def spread(scratch):
    return jnp.transpose(scratch)[: LANES // 2, :]


def put_pieces(out_ref, first, per, value):
    for q in range(value.shape[1] // LANES):
        out_ref[pl.ds(first + q, LANES // 2, stride=per), :] = value[:, q * LANES : (q + 1) * LANES]


def move_pieces(out_ref, first, per, in_ref):
    count = in_ref.shape[0] // (LANES // 2)
    for q in range(count):
        out_ref[pl.ds(first + q, LANES // 2, stride=per), :] = in_ref[pl.ds(q, LANES // 2, stride=count), :]


def collect(ref, first, count):
    per = ref.shape[0] // (LANES // 2)
    parts = []
    for q in range(first, first + count):
        rows = ref[pl.ds(q, LANES // 2, stride=per), :]
        parts.append(jnp.transpose(jnp.concatenate([rows, jnp.zeros_like(rows)], axis=0)))
    return jnp.concatenate(parts, axis=0)


def sum_pieces(ref, count):
    per = ref.shape[0] // (LANES // 2)
    return [jnp.sum(ref[pl.ds(q, LANES // 2, stride=per), :], axis=0, keepdims=True) for q in range(count)]


def split(x):
    high = x.astype(BF16)
    return high, (x - high.astype(F32)).astype(BF16)


def dot(a, b, dims):
    return lax.dot_general(a, b, (dims, ((), ())), preferred_element_type=F32)


def dot3(a, b, dims):
    (ah, al), (bh, bl) = a, b
    return dot(ah, bh, dims) + (dot(ah, bl, dims) + dot(al, bh, dims))


def bounds(upper_row, units):
    return jnp.where(lane_ids(upper_row.shape) < units, -upper_row, 0.0), upper_row


def clip(x, low, high):
    return jnp.minimum(jnp.maximum(x, low), high)


def sums_kernel(
    cost_ref, demand_ref, ends_ref, caps_ref, sent_ref, cost, demand, ends, caps, out, sems
):
    regions = cost.shape[0]
    half = regions // 2
    copies = [
        begin(source, target, sems.at[k])
        for k, (source, target) in enumerate(
            (
                (cost_ref.at[pl.ds(0, half)], cost.at[pl.ds(0, half)]),
                (cost_ref.at[pl.ds(half, regions - half)], cost.at[pl.ds(half, regions - half)]),
                (demand_ref, demand),
                (ends_ref, ends),
                (caps_ref, caps),
            )
        )
    ]

    def add(ref, first, last, acc):
        for r in range(first, last):
            x = ref[r].astype(F32)
            acc = x * x if acc is None else acc + x * x
        return acc

    def total(acc):
        return jnp.sum(jnp.sum(acc, axis=0, keepdims=True), axis=1, keepdims=True)

    copies[0].wait()
    acc = add(cost, 0, half, None)
    copies[1].wait()
    cost_sum = total(add(cost, half, regions, acc))
    copies[2].wait()
    load_sum = total(add(demand, 0, regions, None))
    ids = lane_ids((1, LANES))
    row = jnp.where(ids == 0, cost_sum, jnp.where(ids == 1, load_sum, 0.0))
    copies[3].wait()
    copies[4].wait()
    lines = ends.shape[1]
    ends_row = ends[...].astype(F32)
    row = row + jnp.concatenate(
        [jnp.zeros((1, LANES - 3 * lines), F32), ends_row[0:1, :], ends_row[1:2, :], caps[...]], axis=1
    )
    out[...] = jnp.broadcast_to(row, out.shape)
    begin(out, sent_ref, sems.at[0]).wait()


def join_kernel(sums_ref, turned_ref, sent_ref, out, sems):
    per = out.shape[0] // (LANES // 2)
    row = jnp.sum(sums_ref[...], axis=0, keepdims=True)
    out[pl.ds(0, LANES // 2, stride=per), :] = jnp.broadcast_to(row, (LANES // 2, LANES))
    move_pieces(out, 1, per, turned_ref)
    begin(out, sent_ref, sems.at[0]).wait()


def turn_kernel(cost_ref, decay_ref, out_ref, rows):
    regions, hours, units = decay_ref.shape
    n = regions * hours
    costs = cost_ref[:, :, :units].astype(F32).reshape(n, units)
    decay = decay_ref[...].reshape(n, units)
    for place, x in enumerate((costs, swap_halves(costs), decay, swap_halves(decay))):
        rows[place * n : (place + 1) * n, :] = x
    put_pieces(out_ref, 0, out_ref.shape[0] // (LANES // 2), spread(rows[...]))


def year_pieces(rows, out_ref):
    half = rows.shape[0] // 2
    rows[half:, :] = swap_halves(rows[:half, :])
    put_pieces(out_ref, 0, out_ref.shape[0] // (LANES // 2), spread(rows[...]))


def year_totals(received_ref, count, regions):
    x = collect(received_ref, 0, count)
    half = x.shape[0] // 2
    tiles = []
    for t in range(half // PAD_ROWS):
        at = t * PAD_ROWS
        tile = x[at : at + PAD_ROWS, :] + swap_halves(x[half + at : half + at + PAD_ROWS, :])
        tiles.append(tile[:regions, :])
    return tiles


def first_kernel(
    units, year_scale, joined_ref, cost_ref, upper_ref, demand_ref, line_ref,
    omega_ref, bus_ref, sent_ref, out_ref, rows, column, sems
):
    regions, hours, width = cost_ref.shape
    (s,) = sum_pieces(joined_ref, 1)
    ids = lane_ids(s.shape)
    cost_sum = jnp.sum(jnp.where(ids == 0, s, 0.0), axis=1, keepdims=True)
    load_sum = jnp.sum(jnp.where(ids == 1, s, 0.0), axis=1, keepdims=True)
    omega = jnp.sqrt(cost_sum / load_sum)
    omega_ref[...] = jnp.broadcast_to(omega, omega_ref.shape)
    tau, sigma = step_ratio / omega, step_ratio * omega
    column[...] = jnp.zeros_like(column)
    rows[...] = jnp.zeros_like(rows)
    for r in range(regions):
        low, high = bounds(upper_ref[r : r + 1, :], units)
        primal = clip(-tau * cost_ref[r].astype(F32), low, high)
        image = jnp.sum((2.0 * primal) * line_ref[...], axis=1, keepdims=True)
        price = sigma * (image - demand_ref[r, :, 0:1].astype(F32))
        column[r * hours : (r + 1) * hours, :] = jnp.broadcast_to(price, (hours, LANES))
        sums = (2.0 * year_scale) * jnp.sum(primal, axis=0, keepdims=True)
        for t in range(width // LANES):
            rows[t * PAD_ROWS + r : t * PAD_ROWS + r + 1, :] = sums[:, t * LANES : (t + 1) * LANES]
    year_pieces(rows, out_ref)
    copy = begin(out_ref, sent_ref, sems.at[0])
    bus_ref[...] = jnp.transpose(column[...])[0:1, :]
    copy.wait()


def prices_kernel(
    units, omega_ref, cost_ref, upper_ref, demand_ref, conversion_ref,
    prices_ref, back_ref, turned_ref, bar, rows, held, demand, new_prices, sems,
):
    copy = begin(conversion_ref, held, sems.at[0])
    demand_copy = begin(demand_ref, demand, sems.at[1])
    regions, hours, width = cost_ref.shape
    bus_rows = demand_ref.shape[2]
    n = regions * hours
    omega = omega_ref[0:1, 0:1]
    tau, sigma = step_ratio / omega, step_ratio * omega
    for r in range(regions):
        low, high = bounds(upper_ref[r : r + 1, :], units)
        bar[r * hours : (r + 1) * hours, :] = 2.0 * clip(-tau * cost_ref[r].astype(F32), low, high)
    copy.wait()
    step = 256
    image = None
    for k in range(0, width, step):
        part = dot3(split(bar[:, k : k + step]), split(held[k : k + step, :]), ((1,), (0,)))
        image = part if image is None else image + part
    demand_copy.wait()
    loads = demand[...].astype(F32).reshape(n, bus_rows)
    prices = sigma * (image - loads)
    new_prices[...] = prices
    leaving = begin(new_prices, prices_ref, sems.at[0])
    cut = split(prices)
    for k in range(0, width, step):
        back_ref[:, k : k + step] = dot3(cut, split(held[k : k + step, :]), ((1,), (1,)))
    stored = back_ref[:, :units]
    rows[:n, :] = stored
    rows[n : 2 * n, :] = swap_halves(stored)
    rows[2 * n :, :] = jnp.zeros_like(rows[2 * n :, :])
    put_pieces(turned_ref, 0, turned_ref.shape[0] // (LANES // 2), spread(rows[...]))
    leaving.wait()


def sum_kernel(count, received_ref, added_ref, bus_ref, came_ref, sent_ref, grown_ref, out_ref, sems):
    per = out_ref.shape[0] // (LANES // 2)
    for q, total in enumerate(sum_pieces(received_ref, count)):
        out_ref[pl.ds(q, LANES // 2, stride=per), :] = jnp.broadcast_to(total, (LANES // 2, LANES))
    move_pieces(out_ref, count, per, added_ref)
    copy = begin(out_ref, sent_ref, sems.at[0])
    grow(bus_ref, came_ref, grown_ref)
    copy.wait()


def grow(bus_ref, came_ref, grown_ref):
    grown_ref[: bus_ref.shape[0], :] = bus_ref[...]
    grown_ref[bus_ref.shape[0] :, :] = came_ref[...]


def sum_with_stored_kernel(count, received_ref, stored_ref, added_ref, sent_ref, out_ref, sems):
    per = out_ref.shape[0] // (LANES // 2)
    for q, total in enumerate(sum_pieces(received_ref, count)):
        if q % (count // 2) == 0:
            stored = stored_ref[0:1, (q // (count // 2)) * LANES : (q // (count // 2) + 1) * LANES]
            total = jnp.where(lane_ids(total.shape) < PAD_ROWS, stored, total)
        out_ref[pl.ds(q, LANES // 2, stride=per), :] = jnp.broadcast_to(total, (LANES // 2, LANES))
    move_pieces(out_ref, count, per, added_ref)
    begin(out_ref, sent_ref, sems.at[0]).wait()


def before(x, k, reverse):
    ids = lax.rem(lane_ids(x.shape), LANES // 2)
    if reverse:
        return pltpu.roll(x, LANES - k, 1), ids < LANES // 2 - k
    return pltpu.roll(x, k, 1), ids >= k


def carry_in(scale, offset, reverse):
    k = 1
    while k < LANES // 2:
        scale_before, ok = before(scale, k, reverse)
        offset_before, _ = before(offset, k, reverse)
        offset = jnp.where(ok, scale * offset_before + offset, offset)
        scale = jnp.where(ok, scale * scale_before, scale)
        k *= 2
    entering, ok = before(offset, 1, reverse)
    return jnp.where(ok, entering, 0.0)


def strided(regions, hours):
    def get(ref, h):
        return ref[pl.ds(h, regions, stride=hours), :]

    def put(ref, h, value):
        ref[pl.ds(h, regions, stride=hours), :] = value

    return get, put


def owned(place, x):
    ids = lane_ids(x.shape)
    half = LANES // 2
    first = jnp.sum(jnp.where(ids == place, x, 0.0), axis=1, keepdims=True)
    second = jnp.sum(jnp.where(ids == place + half, x, 0.0), axis=1, keepdims=True)
    return jnp.where(ids < half, first, second)


def halves(x):
    left = lane_ids(x.shape) < LANES // 2
    return (
        jnp.sum(jnp.where(left, x, 0.0), axis=1, keepdims=True),
        jnp.sum(jnp.where(left, 0.0, x), axis=1, keepdims=True),
    )


def carry_pieces(out_ref, rows, carries):
    regions = carries[0].shape[0]
    rows[...] = jnp.zeros_like(rows)
    for k, carry in enumerate(carries):
        at = 2 * k * PAD_ROWS
        rows[at : at + regions, :] = carry
        rows[at + PAD_ROWS : at + PAD_ROWS + regions, :] = swap_halves(carry)
    put_pieces(out_ref, 0, 1, spread(rows[...]))


def collect_carries(ref, q, regions, count):
    x = collect(ref, q, 1)
    found = []
    for k in range(count):
        at = 2 * k * PAD_ROWS
        found.append(x[at : at + regions, :] + swap_halves(x[at + PAD_ROWS : at + PAD_ROWS + regions, :]))
    return found


def storage_kernel(
    level_scale, year_scale, year_bound,
    place_ref, omega_ref, joined_ref, order_ref, upper_ref, energy_ref, annual_ref,
    carries_ref, costs, decay, grad, block_ref, run, scale, dual, suffix, suffix_scale, rows,
):
    del order_ref
    regions, units = energy_ref.shape
    n = costs.shape[0]
    hours = n // regions
    get, put = strided(regions, hours)
    place = place_ref[0]
    omega = omega_ref[0:1, 0:1]
    tau, sigma = step_ratio / omega, step_ratio * omega
    high = owned(place, upper_ref[:, :units])
    energy = owned(place, energy_ref[...])
    annual = owned(place, annual_ref[:, :units])
    x = collect(joined_ref, 1, 4 * n // LANES)
    costs[...] = x[:n] + swap_halves(x[n : 2 * n])
    decay[...] = x[2 * n : 3 * n] + swap_halves(x[3 * n :])

    level = jnp.zeros((regions, units), F32)
    kept = jnp.ones((regions, units), F32)
    year = jnp.zeros((regions, units), F32)
    for h in range(hours):
        d = get(decay, h)
        bar = 2.0 * clip(-tau * get(costs, h), -high, high)
        year = year + bar
        level = d * level + bar
        kept = kept * d
        put(run, h, level)
        put(scale, h, kept)
    entering = carry_in(kept, level, False)
    first, second = halves(year)
    total = year_scale * jnp.where(lane_ids(year.shape) < LANES // 2, first, second)
    block_ref[...] = jnp.zeros_like(block_ref)
    block_ref[:regions, :] = kept
    block_ref[PAD_ROWS : PAD_ROWS + regions, :] = jnp.maximum(sigma * (total - year_bound * annual), 0.0)
    after = jnp.zeros((regions, units), F32)
    after_kept = jnp.ones((regions, units), F32)
    for h in reversed(range(hours)):
        d = get(decay, h)
        level = get(run, h) + get(scale, h) * entering
        stored = level_scale * jnp.maximum(sigma * (level_scale * level - energy), 0.0)
        put(dual, h, stored)
        after = d * (stored + after)
        after_kept = after_kept * d
        put(suffix, h, after)
        put(suffix_scale, h, after_kept)
    closing = carry_in(after_kept, after, True)
    for h in range(hours):
        later = closing if h == hours - 1 else get(suffix, h + 1) + get(suffix_scale, h + 1) * closing
        put(grad, h, get(costs, h) + (get(dual, h) + later))
    carry_pieces(carries_ref, rows, (entering, closing))


def storage_again_kernel(
    count, year_scale, place_ref, omega_ref, costs, decay, grad, block_ref, received_ref, upper_ref,
    bus_ref, came_ref, order_ref, carries_ref, year_ref, grown_ref, back, rows,
):
    del order_ref
    n, units = costs.shape
    regions = upper_ref.shape[0]
    hours = n // regions
    get, _ = strided(regions, hours)
    grow(bus_ref, came_ref, grown_ref)
    omega = omega_ref[0:1, 0:1]
    tau = step_ratio / omega
    high = owned(place_ref[0], upper_ref[:, :units])
    kept = block_ref[:regions, :]
    year_dual = block_ref[PAD_ROWS : PAD_ROWS + regions, :]
    x = collect(received_ref, count, -(-2 * n // LANES))
    back[...] = x[:n] + swap_halves(x[n : 2 * n])
    level = jnp.zeros((regions, units), F32)
    year = jnp.zeros((regions, units), F32)
    for h in range(hours):
        old = clip(-tau * get(costs, h), -high, high)
        new = clip(old - tau * (get(grad, h) + get(back, h) + year_scale * year_dual), -high, high)
        bar = 2.0 * new - old
        year = year + bar
        level = get(decay, h) * level + bar
    carry_pieces(carries_ref, rows, (carry_in(kept, level, False),))
    diagonal = lax.broadcasted_iota(jnp.int32, (regions, units), 0) == lane_ids((regions, units))
    for part, column in enumerate(halves(year)):
        line = jnp.sum(jnp.where(diagonal, year_scale * column, 0.0), axis=0, keepdims=True)
        year_ref[:, part * LANES : (part + 1) * LANES] = jnp.broadcast_to(line, (year_ref.shape[0], LANES))


def second_kernel(
    units, year_scale, year_bound,
    omega_ref, received_ref, cost_ref, back_ref, upper_ref, annual_ref, carries_ref,
    sent_ref, dual_ref, rows, dual, out, sems,
):
    regions, hours, width = cost_ref.shape
    omega = omega_ref[0:1, 0:1]
    tau, sigma = step_ratio / omega, step_ratio * omega
    rows[...] = jnp.zeros_like(rows)
    totals = year_totals(received_ref, rows.shape[0] // LANES, regions)
    for t, total in enumerate(totals):
        at = slice(t * LANES, (t + 1) * LANES)
        dual[:, at] = jnp.maximum(sigma * (total - year_bound * annual_ref[:, at]), 0.0)
    leaving = begin(dual, dual_ref, sems.at[1])
    for r in range(regions):
        high = upper_ref[r : r + 1, units:]
        costs = cost_ref[r, :, units:].astype(F32)
        old = clip(-tau * costs, 0.0, high)
        grad = costs + back_ref[r * hours : (r + 1) * hours, units:] + year_scale * dual[r : r + 1, units:]
        bar = 2.0 * clip(old - tau * grad, 0.0, high) - old
        sums = year_scale * jnp.sum(bar, axis=0, keepdims=True)
        for t in range(1, width // LANES):
            rows[t * PAD_ROWS + r : t * PAD_ROWS + r + 1, :] = sums[:, t * LANES - units : (t + 1) * LANES - units]
    year_pieces(rows, out)
    move_pieces(out, rows.shape[0] // LANES, out.shape[0] // (LANES // 2), carries_ref)
    begin(out, sent_ref, sems.at[0]).wait()
    leaving.wait()


def last_kernel(
    shifts, units, count, level_scale, year_scale, year_bound,
    place_ref, omega_ref, cost_ref, back_ref, upper_ref, dual_ref, conversion_ref, demand_ref, prices_ref,
    annual_ref, ends_ref, bus_ref, came_ref, received_ref, decay_ref, energy_ref,
    primal_ref, flows_ref, new_prices_ref, base_ref, slope_ref, year_ref,
    bar, held, demand, old_prices, dual, ends, annual, bus, bus_rows_ref, costs, decay, back, stored, new_stored, sems,
):
    copy, *others = [
        begin(source, target, sems.at[k])
        for k, (source, target) in enumerate(
            (
                (dual_ref, dual),
                (conversion_ref, held),
                (demand_ref, demand),
                (prices_ref, old_prices),
                (annual_ref, annual),
            )
        )
    ]
    regions, hours, width = cost_ref.shape
    bus_rows = demand_ref.shape[2]
    lines = flows_ref.shape[1]
    n = regions * hours
    get, put = strided(regions, hours)
    omega = omega_ref[0:1, 0:1]
    tau, sigma = step_ratio / omega, step_ratio * omega

    costs[...] = cost_ref[:, :, :units].astype(F32).reshape(n, units)
    decay[...] = decay_ref[...].reshape(n, units)
    back[...] = back_ref[:, :units]
    high = upper_ref[:, :units]
    energy = energy_ref[...]
    level, later = collect_carries(received_ref, count, regions, 2)
    for h in range(hours):
        level = get(decay, h) * level + 2.0 * clip(-tau * get(costs, h), -high, high)
        put(stored, h, jnp.maximum(sigma * (level_scale * level - energy), 0.0))
    copy.wait()
    year_part = year_scale * dual[:, :units]
    for h in reversed(range(hours)):
        weight = level_scale * get(stored, h) + later
        later = get(decay, h) * weight
        old = clip(-tau * get(costs, h), -high, high)
        put(new_stored, h, clip(old - tau * (get(costs, h) + get(back, h) + weight + year_part), -high, high))
    level = jnp.zeros((regions, units), F32)
    kept = jnp.ones((regions, units), F32)
    for h in range(hours):
        d = get(decay, h)
        second = 2.0 * get(new_stored, h) - clip(-tau * get(costs, h), -high, high)
        level = d * level + second
        kept = d * kept
        put(base_ref, h, get(stored, h) + sigma * (level_scale * level - energy))
        put(slope_ref, h, (sigma * level_scale) * kept)
        put(back, h, second)
    bar[:, :units] = back[...]
    for r in range(regions):
        at = slice(r * hours, (r + 1) * hours)
        high = upper_ref[r : r + 1, units:]
        row_costs = cost_ref[r, :, units:].astype(F32)
        old = clip(-tau * row_costs, 0.0, high)
        grad = row_costs + back_ref[at, units:] + year_scale * dual[r : r + 1, units:]
        new = clip(old - tau * grad, 0.0, high)
        bar[at, units:] = 2.0 * new - old
        primal_ref[r, :, :units] = new_stored[at, :].astype(BF16)
        primal_ref[r, :, units:] = new.astype(BF16)
    for other in others:
        other.wait()
    step = 256
    image = None
    for k in range(0, width, step):
        part = dot3(split(bar[:, k : k + step]), split(held[k : k + step, :]), ((1,), (0,)))
        image = part if image is None else image + part
    loads = demand[...].astype(F32).reshape(n, bus_rows)
    new_prices_ref[...] = old_prices[...] + sigma * (image - loads)

    year_ref[...] = dual[...] - (sigma * year_bound) * annual[...]
    grow(bus_ref, came_ref, bus)
    groups, reach = bus.shape
    regions_all = groups * regions
    first_region = place_ref[0] * regions
    for r in range(regions):
        moved = bus[...] if r == 0 else pltpu.roll(bus[...], reach - r * hours, 1)
        bus_rows_ref[r * groups : (r + 1) * groups, :] = moved[:, :LANES]

    def exact(a, b, dims):
        return lax.dot_general(
            a, b, (dims, ((), ())), precision=lax.Precision.HIGHEST, preferred_element_type=F32
        )

    def incidence(ids):
        ids = ids + first_region
        ids = jnp.where(ids >= regions_all, ids - regions_all, ids).astype(F32)
        return (ids == ends[1:2, :]).astype(F32) - (ids == ends[0:1, :]).astype(F32)

    ids = lane_ids((1, LANES))
    for part in range(3):
        for first in range(0, groups * lines, LANES):
            row = jnp.zeros((1, LANES), F32)
            for at in range(0, LANES, lines):
                g = (first + at) // lines
                turn = (at - (LANES - (3 - part) * lines)) % LANES
                moved = ends_ref[g : g + 1, :] if turn == 0 else pltpu.roll(ends_ref[g : g + 1, :], turn, 1)
                row = jnp.where(jnp.logical_and(ids >= at, ids < at + lines), moved, row)
            ends[part : part + 1, first : first + LANES] = row

    def rows_like(count):
        return lax.broadcasted_iota(jnp.int32, (count, ends.shape[1]), 0)

    caps = ends[2:3, :]
    at = rows_like(regions_all)
    place = lax.shift_right_logical(at, groups.bit_length() - 1)
    for k, shift in enumerate(shifts):
        bit = lax.bitwise_and(lax.shift_right_logical(at, k), 1)
        place = place + bit * (shift * regions)
    grad = exact(bus_rows_ref[...], incidence(place), ((0,), (0,)))
    flows = clip(-tau * grad[:hours, :], -caps, caps)
    own = flows[:, :lines]
    for g in range(1, groups):
        own = jnp.where(place_ref[0] == g, flows[:, g * lines : (g + 1) * lines], own)
    flows_ref[...] = own
    inflow = exact(2.0 * flows, incidence(rows_like(LANES)), ((1,), (1,)))
    ids = lane_ids(inflow.shape)
    for r in range(regions):
        moved = inflow if r == 0 else pltpu.roll(inflow, LANES - r, 1)
        at = slice(r * hours, (r + 1) * hours)
        new_prices_ref[at, :LANES] = new_prices_ref[at, :LANES] + sigma * jnp.where(ids == 0, moved, 0.0)


def finish_kernel(count, omega_ref, received_ref, base_ref, slope_ref, rest_ref, storage_ref, year_ref):
    regions = rest_ref.shape[0]
    hours = base_ref.shape[0] // regions
    sigma = step_ratio * omega_ref[0:1, 0:1]
    for t, total in enumerate(year_totals(received_ref, count, regions)):
        at = slice(t * LANES, (t + 1) * LANES)
        year_ref[:, at] = jnp.maximum(rest_ref[:, at] + sigma * total, 0.0)
    (entering,) = collect_carries(received_ref, count, regions, 1)
    for r in range(regions):
        at = slice(r * hours, (r + 1) * hours)
        storage_ref[at, :] = jnp.maximum(base_ref[at, :] + slope_ref[at, :] * entering[r : r + 1, :], 0.0)


def exchange(x):
    blocks = lax.axis_size("tm")
    pieces = x.reshape(blocks, 1, x.size // blocks)
    return lax.all_to_all(pieces, "tm", 0, 0, tiled=True).reshape(x.shape)


def per_device(cost, demand, conversion, upper, decay, energy_cap, annual_cap, line_ends, line_cap):
    hours, regions, width = cost.shape
    bus_rows = demand.shape[2]
    units = decay.shape[2]
    lines = line_ends.shape[0]
    blocks = lax.axis_size("tm")
    groups = lax.axis_size("region")
    hours_all = hours * blocks
    scale = 1.0 / math.sqrt(hours_all)
    bound = math.sqrt(hours_all)
    n = regions * hours
    year_rows = 2 * PAD_ROWS * (width // LANES)
    year_count = year_rows // LANES
    turned_count = 4 * n // LANES
    back_count = -(-2 * n // LANES)
    rows = lambda k: pltpu.VMEM((k, LANES), F32)
    sems = lambda k: pltpu.SemaphoreType.DMA((k,))
    pieces = lambda count: struct(blocks * count, LANES)
    sent = lambda count: in_hbm(blocks * count, LANES)
    cost = jnp.transpose(cost, (1, 0, 2))
    demand = jnp.transpose(demand, (1, 0, 2))
    decay = jnp.transpose(decay, (1, 0, 2))
    tm_place = lax.axis_index("tm").astype(jnp.int32).reshape(1)
    region_place = lax.axis_index("region").astype(jnp.int32).reshape(1)

    shifts = (1, 4, 2)

    def from_ahead(x, reach):
        return lax.ppermute(x, "region", [((z + reach) % groups, z) for z in range(groups)])

    sums = call(
        sums_kernel,
        in_hbm(groups, LANES),
        "sums",
        [HBM] * 4,
        [
            pltpu.VMEM((regions, hours, width), BF16),
            pltpu.VMEM((regions, hours, bus_rows), BF16),
            pltpu.VMEM((2, lines), jnp.int32),
            pltpu.VMEM((1, lines), F32),
            rows(groups),
            sems(5),
        ],
        HBM,
    )(keep(cost), keep(demand), keep(line_ends.T), keep(line_cap.reshape(1, -1)))
    sums = lax.all_to_all(sums.reshape(groups, 1, LANES), "region", 0, 0, tiled=True).reshape(groups, LANES)
    turned = call(turn_kernel, pieces(turned_count), "turn", [VMEM] * 2, [rows(4 * n)])(cost, decay)
    joined_count = 1 + turned_count
    joined = call(
        join_kernel, sent(joined_count), "join", [VMEM] * 2, [rows(blocks * joined_count), sems(1)], HBM
    )(sums, turned)
    joined = exchange(joined)
    reach = -(-n // LANES) * LANES
    omega, bus, first = call(
        functools.partial(first_kernel, units, scale),
        (struct(8, LANES), struct(1, reach), sent(year_count)),
        "first_primal",
        [VMEM] * 5,
        [rows(blocks * year_count), rows(year_rows), rows(reach), sems(1)],
        (VMEM, VMEM, HBM),
    )(joined, cost, upper, demand, conversion[:, :1].T)
    first = exchange(first)

    prices, back, back_turned = call(
        functools.partial(prices_kernel, units),
        (in_hbm(n, bus_rows), struct(n, width), pieces(back_count)),
        "first_prices",
        [VMEM] * 3 + [HBM] * 2,
        [
            pltpu.VMEM((n, width), F32),
            rows(back_count * LANES),
            pltpu.VMEM((width, bus_rows), F32),
            pltpu.VMEM((regions, hours, bus_rows), BF16),
            pltpu.VMEM((n, bus_rows), F32),
            sems(2),
        ],
        (HBM, VMEM, VMEM),
        flops=4000000000,
        nbytes=5000000,
    )(omega, cost, upper, keep(demand), keep(conversion))

    second_count = year_count + back_count
    second, bus = call(
        functools.partial(sum_kernel, year_count),
        (sent(second_count), struct(2, reach)),
        "year_sum",
        [VMEM] * 4,
        [rows(blocks * second_count), sems(1)],
        (HBM, VMEM),
    )(first, back_turned, bus, from_ahead(bus, shifts[0]))
    second = exchange(second)

    carries, costs_all, decay_all, grad_all, block = call(
        functools.partial(storage_kernel, scale, scale, bound),
        (pieces(1),) + (struct(n, units),) * 3 + (struct(2 * PAD_ROWS, units),),
        "storage",
        [SMEM] + [VMEM] * 2 + [ANY] + [VMEM] * 3,
        [rows(n) for _ in range(5)] + [rows(LANES)],
        flops=4000000000,
    )(tm_place, omega, joined, first, upper, energy_cap, annual_cap)

    third, year_dual = call(
        functools.partial(second_kernel, units, scale, bound),
        (sent(year_count + 1), in_hbm(regions, width)),
        "second_primal",
        [VMEM] * 7,
        [
            rows(year_rows),
            pltpu.VMEM((regions, width), F32),
            rows(blocks * (year_count + 1)),
            sems(2),
        ],
        (HBM, HBM),
    )(omega, second, cost, back, upper, annual_cap, carries)
    third = exchange(third)

    carry, stored_year, bus = call(
        functools.partial(storage_again_kernel, year_count, scale),
        (pieces(1), struct(8, year_rows), struct(4, reach)),
        "storage_again",
        [SMEM] + [VMEM] * 9 + [HBM],
        [rows(n), rows(LANES)],
        flops=4000000000,
    )(tm_place, omega, costs_all, decay_all, grad_all, block, second, upper, bus, from_ahead(bus, shifts[1]), keep(year_dual))

    fourth = call(
        functools.partial(sum_with_stored_kernel, year_count),
        sent(year_count + 1),
        "year_sum_2",
        [VMEM] * 3,
        [rows(blocks * (year_count + 1)), sems(1)],
        HBM,
    )(third, stored_year, carry)
    fourth = exchange(fourth)

    new_primal, flows, prices, base, slope, rest = call(
        functools.partial(last_kernel, shifts, units, year_count, scale, scale, bound),
        (
            struct(regions, hours, width, dtype=BF16),
            struct(hours, lines),
            struct(n, bus_rows),
            struct(n, units),
            struct(n, units),
            struct(regions, width),
        ),
        "second_prices",
        [SMEM] + [VMEM] * 4 + [HBM] * 5 + [VMEM] * 6,
        [
            pltpu.VMEM((n, width), F32),
            pltpu.VMEM((width, bus_rows), F32),
            pltpu.VMEM((regions, hours, bus_rows), BF16),
            pltpu.VMEM((n, bus_rows), F32),
            pltpu.VMEM((regions, width), F32),
            pltpu.VMEM((3, groups * lines), F32),
            pltpu.VMEM((regions, width), F32),
            pltpu.VMEM((groups, reach), F32),
            rows(groups * regions),
        ]
        + [rows(n) for _ in range(5)]
        + [sems(5)],
        flops=3000000000,
        nbytes=6000000,
    )(
        region_place, omega, cost, back, upper, keep(year_dual), keep(conversion), keep(demand), keep(prices),
        keep(annual_cap), sums, bus, from_ahead(bus, shifts[2]), third, decay, energy_cap,
    )
    storage_dual, year_dual = call(
        functools.partial(finish_kernel, year_count),
        (struct(n, units), struct(regions, width)),
        "finish",
        [VMEM] * 5,
    )(omega, fourth, base, slope, rest)
    turn = lambda x, last: jnp.transpose(x.reshape(regions, hours, last), (1, 0, 2))
    return (
        jnp.transpose(new_primal, (1, 0, 2)),
        flows,
        turn(prices, bus_rows),
        turn(storage_dual, units),
        year_dual,
    )


def solution(mesh):
    in_specs = (
        P("tm", "region", None),
        P("tm", "region", None),
        P(),
        P("region", None),
        P("tm", "region", None),
        P("region", None),
        P("region", None),
        P("region", None),
        P("region"),
    )
    out_specs = (
        P("tm", "region", None),
        P("tm", "region"),
        P("tm", "region", None),
        P("tm", "region", None),
        P("region", None),
    )
    return jax.shard_map(
        per_device, mesh=mesh, in_specs=in_specs, out_specs=out_specs, check_vma=False
    )
```

```python
import functools
import math

import jax
import jax.numpy as jnp
from jax import lax
from jax.experimental import pallas as pl
from jax.experimental.pallas import tpu as pltpu
from jax.sharding import PartitionSpec as P

F32 = jnp.float32
BF16 = jnp.bfloat16
LANES = 128
PAD_ROWS = 16
step_ratio = 0.5


VMEM = pl.BlockSpec(memory_space=pltpu.VMEM)
SMEM = pl.BlockSpec(memory_space=pltpu.SMEM)
HBM = pl.BlockSpec(memory_space=pltpu.HBM)
ANY = pl.BlockSpec(memory_space=pl.ANY)


def call(kernel, out_shape, name, in_specs, scratch=(), out_specs=None, aliases=None, flops=1000000, nbytes=1000000):
    if out_specs is None:
        out_specs = jax.tree.map(lambda _: VMEM, out_shape)
    return pl.pallas_call(
        kernel,
        out_shape=out_shape,
        in_specs=in_specs,
        out_specs=out_specs,
        scratch_shapes=list(scratch),
        name=name,
        input_output_aliases=aliases or {},
        compiler_params=pltpu.CompilerParams(vmem_limit_bytes=24 * 1024 * 1024),
        cost_estimate=pl.CostEstimate(flops=flops, bytes_accessed=nbytes, transcendentals=0),
    )


def struct(*shape, dtype=F32):
    return jax.ShapeDtypeStruct(shape, dtype)


def begin(source, target, sem):
    copy = pltpu.make_async_copy(source, target, sem)
    copy.start()
    return copy


def in_hbm(*shape, dtype=F32):
    return pltpu.HBM(shape, dtype)


def keep(x):
    return pltpu.with_memory_space_constraint(x, pltpu.HBM)


def lane_ids(shape):
    return lax.broadcasted_iota(jnp.int32, shape, len(shape) - 1)


def swap_halves(x):
    return pltpu.roll(x, LANES // 2, 1)


def spread(scratch):
    return jnp.transpose(scratch)[: LANES // 2, :]


def put_pieces(out_ref, first, per, value):
    for q in range(value.shape[1] // LANES):
        out_ref[pl.ds(first + q, LANES // 2, stride=per), :] = value[:, q * LANES : (q + 1) * LANES]


def move_pieces(out_ref, first, per, in_ref):
    count = in_ref.shape[0] // (LANES // 2)
    for q in range(count):
        out_ref[pl.ds(first + q, LANES // 2, stride=per), :] = in_ref[pl.ds(q, LANES // 2, stride=count), :]


def collect(ref, first, count):
    per = ref.shape[0] // (LANES // 2)
    parts = []
    for q in range(first, first + count):
        rows = ref[pl.ds(q, LANES // 2, stride=per), :]
        parts.append(jnp.transpose(jnp.concatenate([rows, jnp.zeros_like(rows)], axis=0)))
    return jnp.concatenate(parts, axis=0)


def sum_pieces(ref, count):
    per = ref.shape[0] // (LANES // 2)
    return [jnp.sum(ref[pl.ds(q, LANES // 2, stride=per), :], axis=0, keepdims=True) for q in range(count)]


def split(x):
    high = x.astype(BF16)
    return high, (x - high.astype(F32)).astype(BF16)


def dot(a, b, dims):
    return lax.dot_general(a, b, (dims, ((), ())), preferred_element_type=F32)


def dot3(a, b, dims):
    (ah, al), (bh, bl) = a, b
    return dot(ah, bh, dims) + (dot(ah, bl, dims) + dot(al, bh, dims))


def bounds(upper_row, units):
    return jnp.where(lane_ids(upper_row.shape) < units, -upper_row, 0.0), upper_row


def clip(x, low, high):
    return jnp.minimum(jnp.maximum(x, low), high)


def sums_kernel(
    cost_ref, demand_ref, ends_ref, caps_ref, sent_ref, cost, demand, ends, caps, out, sems
):
    regions = cost.shape[0]
    half = regions // 2
    copies = [
        begin(source, target, sems.at[k])
        for k, (source, target) in enumerate(
            (
                (cost_ref.at[pl.ds(0, half)], cost.at[pl.ds(0, half)]),
                (cost_ref.at[pl.ds(half, regions - half)], cost.at[pl.ds(half, regions - half)]),
                (demand_ref, demand),
                (ends_ref, ends),
                (caps_ref, caps),
            )
        )
    ]

    def add(ref, first, last, acc):
        for r in range(first, last):
            x = ref[r].astype(F32)
            acc = x * x if acc is None else acc + x * x
        return acc

    def total(acc):
        return jnp.sum(jnp.sum(acc, axis=0, keepdims=True), axis=1, keepdims=True)

    copies[0].wait()
    acc = add(cost, 0, half, None)
    copies[1].wait()
    cost_sum = total(add(cost, half, regions, acc))
    copies[2].wait()
    load_sum = total(add(demand, 0, regions, None))
    ids = lane_ids((1, LANES))
    row = jnp.where(ids == 0, cost_sum, jnp.where(ids == 1, load_sum, 0.0))
    copies[3].wait()
    copies[4].wait()
    lines = ends.shape[1]
    ends_row = ends[...].astype(F32)
    row = row + jnp.concatenate(
        [jnp.zeros((1, LANES - 3 * lines), F32), ends_row[0:1, :], ends_row[1:2, :], caps[...]], axis=1
    )
    out[...] = jnp.broadcast_to(row, out.shape)
    begin(out, sent_ref, sems.at[0]).wait()


def join_kernel(sums_ref, turned_ref, sent_ref, out, sems):
    per = out.shape[0] // (LANES // 2)
    row = jnp.sum(sums_ref[...], axis=0, keepdims=True)
    out[pl.ds(0, LANES // 2, stride=per), :] = jnp.broadcast_to(row, (LANES // 2, LANES))
    move_pieces(out, 1, per, turned_ref)
    begin(out, sent_ref, sems.at[0]).wait()


def turn_kernel(cost_ref, decay_ref, out_ref, rows):
    regions, hours, units = decay_ref.shape
    n = regions * hours
    costs = cost_ref[:, :, :units].astype(F32).reshape(n, units)
    decay = decay_ref[...].reshape(n, units)
    for place, x in enumerate((costs, swap_halves(costs), decay, swap_halves(decay))):
        rows[place * n : (place + 1) * n, :] = x
    put_pieces(out_ref, 0, out_ref.shape[0] // (LANES // 2), spread(rows[...]))


def year_pieces(rows, out_ref):
    half = rows.shape[0] // 2
    rows[half:, :] = swap_halves(rows[:half, :])
    put_pieces(out_ref, 0, out_ref.shape[0] // (LANES // 2), spread(rows[...]))


def year_totals(received_ref, count, regions):
    x = collect(received_ref, 0, count)
    half = x.shape[0] // 2
    tiles = []
    for t in range(half // PAD_ROWS):
        at = t * PAD_ROWS
        tile = x[at : at + PAD_ROWS, :] + swap_halves(x[half + at : half + at + PAD_ROWS, :])
        tiles.append(tile[:regions, :])
    return tiles


def first_kernel(
    units, year_scale, joined_ref, cost_ref, upper_ref, demand_ref, line_ref,
    omega_ref, bus_ref, sent_ref, out_ref, rows, column, sems
):
    regions, hours, width = cost_ref.shape
    (s,) = sum_pieces(joined_ref, 1)
    ids = lane_ids(s.shape)
    cost_sum = jnp.sum(jnp.where(ids == 0, s, 0.0), axis=1, keepdims=True)
    load_sum = jnp.sum(jnp.where(ids == 1, s, 0.0), axis=1, keepdims=True)
    omega = jnp.sqrt(cost_sum / load_sum)
    omega_ref[...] = jnp.broadcast_to(omega, omega_ref.shape)
    tau, sigma = step_ratio / omega, step_ratio * omega
    column[...] = jnp.zeros_like(column)
    rows[...] = jnp.zeros_like(rows)
    for r in range(regions):
        low, high = bounds(upper_ref[r : r + 1, :], units)
        primal = clip(-tau * cost_ref[r].astype(F32), low, high)
        image = jnp.sum((2.0 * primal) * line_ref[...], axis=1, keepdims=True)
        price = sigma * (image - demand_ref[r, :, 0:1].astype(F32))
        column[r * hours : (r + 1) * hours, :] = jnp.broadcast_to(price, (hours, LANES))
        sums = (2.0 * year_scale) * jnp.sum(primal, axis=0, keepdims=True)
        for t in range(width // LANES):
            rows[t * PAD_ROWS + r : t * PAD_ROWS + r + 1, :] = sums[:, t * LANES : (t + 1) * LANES]
    year_pieces(rows, out_ref)
    copy = begin(out_ref, sent_ref, sems.at[0])
    bus_ref[...] = jnp.transpose(column[...])[0:1, :]
    copy.wait()


def prices_kernel(
    units, omega_ref, cost_ref, upper_ref, demand_ref, conversion_ref,
    prices_ref, back_ref, turned_ref, bar, rows, held, demand, new_prices, sems,
):
    copy = begin(conversion_ref, held, sems.at[0])
    demand_copy = begin(demand_ref, demand, sems.at[1])
    regions, hours, width = cost_ref.shape
    bus_rows = demand_ref.shape[2]
    n = regions * hours
    omega = omega_ref[0:1, 0:1]
    tau, sigma = step_ratio / omega, step_ratio * omega
    for r in range(regions):
        low, high = bounds(upper_ref[r : r + 1, :], units)
        bar[r * hours : (r + 1) * hours, :] = 2.0 * clip(-tau * cost_ref[r].astype(F32), low, high)
    copy.wait()
    step = 256
    image = None
    for k in range(0, width, step):
        part = dot3(split(bar[:, k : k + step]), split(held[k : k + step, :]), ((1,), (0,)))
        image = part if image is None else image + part
    demand_copy.wait()
    loads = demand[...].astype(F32).reshape(n, bus_rows)
    prices = sigma * (image - loads)
    new_prices[...] = prices
    leaving = begin(new_prices, prices_ref, sems.at[0])
    cut = split(prices)
    for k in range(0, width, step):
        back_ref[:, k : k + step] = dot3(cut, split(held[k : k + step, :]), ((1,), (1,)))
    stored = back_ref[:, :units]
    rows[:n, :] = stored
    rows[n : 2 * n, :] = swap_halves(stored)
    rows[2 * n :, :] = jnp.zeros_like(rows[2 * n :, :])
    put_pieces(turned_ref, 0, turned_ref.shape[0] // (LANES // 2), spread(rows[...]))
    leaving.wait()


def sum_kernel(count, received_ref, added_ref, bus_ref, came_ref, sent_ref, grown_ref, out_ref, sems):
    per = out_ref.shape[0] // (LANES // 2)
    for q, total in enumerate(sum_pieces(received_ref, count)):
        out_ref[pl.ds(q, LANES // 2, stride=per), :] = jnp.broadcast_to(total, (LANES // 2, LANES))
    move_pieces(out_ref, count, per, added_ref)
    copy = begin(out_ref, sent_ref, sems.at[0])
    grow(bus_ref, came_ref, grown_ref)
    copy.wait()


def grow(bus_ref, came_ref, grown_ref):
    grown_ref[: bus_ref.shape[0], :] = bus_ref[...]
    grown_ref[bus_ref.shape[0] :, :] = came_ref[...]


def sum_with_stored_kernel(count, received_ref, stored_ref, added_ref, sent_ref, out_ref, sems):
    per = out_ref.shape[0] // (LANES // 2)
    for q, total in enumerate(sum_pieces(received_ref, count)):
        if q % (count // 2) == 0:
            stored = stored_ref[0:1, (q // (count // 2)) * LANES : (q // (count // 2) + 1) * LANES]
            total = jnp.where(lane_ids(total.shape) < PAD_ROWS, stored, total)
        out_ref[pl.ds(q, LANES // 2, stride=per), :] = jnp.broadcast_to(total, (LANES // 2, LANES))
    move_pieces(out_ref, count, per, added_ref)
    begin(out_ref, sent_ref, sems.at[0]).wait()


def before(x, k, reverse):
    ids = lax.rem(lane_ids(x.shape), LANES // 2)
    if reverse:
        return pltpu.roll(x, LANES - k, 1), ids < LANES // 2 - k
    return pltpu.roll(x, k, 1), ids >= k


def carry_in(scale, offset, reverse):
    k = 1
    while k < LANES // 2:
        scale_before, ok = before(scale, k, reverse)
        offset_before, _ = before(offset, k, reverse)
        offset = jnp.where(ok, scale * offset_before + offset, offset)
        scale = jnp.where(ok, scale * scale_before, scale)
        k *= 2
    entering, ok = before(offset, 1, reverse)
    return jnp.where(ok, entering, 0.0)


def strided(regions, hours):
    def get(ref, h):
        return ref[pl.ds(h, regions, stride=hours), :]

    def put(ref, h, value):
        ref[pl.ds(h, regions, stride=hours), :] = value

    return get, put


def owned(place, x):
    ids = lane_ids(x.shape)
    half = LANES // 2
    first = jnp.sum(jnp.where(ids == place, x, 0.0), axis=1, keepdims=True)
    second = jnp.sum(jnp.where(ids == place + half, x, 0.0), axis=1, keepdims=True)
    return jnp.where(ids < half, first, second)


def halves(x):
    left = lane_ids(x.shape) < LANES // 2
    return (
        jnp.sum(jnp.where(left, x, 0.0), axis=1, keepdims=True),
        jnp.sum(jnp.where(left, 0.0, x), axis=1, keepdims=True),
    )


def carry_pieces(out_ref, rows, carries):
    regions = carries[0].shape[0]
    rows[...] = jnp.zeros_like(rows)
    for k, carry in enumerate(carries):
        at = 2 * k * PAD_ROWS
        rows[at : at + regions, :] = carry
        rows[at + PAD_ROWS : at + PAD_ROWS + regions, :] = swap_halves(carry)
    put_pieces(out_ref, 0, 1, spread(rows[...]))


def collect_carries(ref, q, regions, count):
    x = collect(ref, q, 1)
    found = []
    for k in range(count):
        at = 2 * k * PAD_ROWS
        found.append(x[at : at + regions, :] + swap_halves(x[at + PAD_ROWS : at + PAD_ROWS + regions, :]))
    return found


def storage_kernel(
    level_scale, year_scale, year_bound,
    place_ref, omega_ref, joined_ref, order_ref, upper_ref, energy_ref, annual_ref,
    carries_ref, costs, decay, grad, block_ref, run, scale, dual, suffix, suffix_scale, rows,
):
    del order_ref
    regions, units = energy_ref.shape
    hours = costs.shape[0] // PAD_ROWS
    n = regions * hours
    get, put = strided(regions, hours)
    place = place_ref[0]
    omega = omega_ref[0:1, 0:1]
    tau, sigma = step_ratio / omega, step_ratio * omega
    high = owned(place, upper_ref[:, :units])
    energy = owned(place, energy_ref[...])
    annual = owned(place, annual_ref[:, :units])
    x = collect(joined_ref, 1, 4 * n // LANES)
    costs[:n, :] = x[:n] + swap_halves(x[n : 2 * n])
    decay[:n, :] = x[2 * n : 3 * n] + swap_halves(x[3 * n :])

    level = jnp.zeros((regions, units), F32)
    kept = jnp.ones((regions, units), F32)
    year = jnp.zeros((regions, units), F32)
    for h in range(hours):
        d = get(decay, h)
        bar = 2.0 * clip(-tau * get(costs, h), -high, high)
        year = year + bar
        level = d * level + bar
        kept = kept * d
        put(run, h, level)
        put(scale, h, kept)
    entering = carry_in(kept, level, False)
    first, second = halves(year)
    total = year_scale * jnp.where(lane_ids(year.shape) < LANES // 2, first, second)
    block_ref[...] = jnp.zeros_like(block_ref)
    block_ref[:regions, :] = kept
    block_ref[PAD_ROWS : PAD_ROWS + regions, :] = jnp.maximum(sigma * (total - year_bound * annual), 0.0)
    after = jnp.zeros((regions, units), F32)
    after_kept = jnp.ones((regions, units), F32)
    for h in reversed(range(hours)):
        d = get(decay, h)
        level = get(run, h) + get(scale, h) * entering
        stored = level_scale * jnp.maximum(sigma * (level_scale * level - energy), 0.0)
        put(dual, h, stored)
        after = d * (stored + after)
        after_kept = after_kept * d
        put(suffix, h, after)
        put(suffix_scale, h, after_kept)
    closing = carry_in(after_kept, after, True)
    for h in range(hours):
        later = closing if h == hours - 1 else get(suffix, h + 1) + get(suffix_scale, h + 1) * closing
        put(grad, h, get(costs, h) + (get(dual, h) + later))
    carry_pieces(carries_ref, rows, (entering, closing))


def storage_again_kernel(
    count, year_scale, place_ref, omega_ref, costs, decay, grad, block_ref, received_ref, upper_ref,
    bus_ref, came_ref, order_ref, carries_ref, year_ref, grown_ref, back, rows,
):
    del order_ref
    units = costs.shape[1]
    regions = upper_ref.shape[0]
    hours = costs.shape[0] // PAD_ROWS
    n = regions * hours
    get, _ = strided(regions, hours)
    grow(bus_ref, came_ref, grown_ref)
    omega = omega_ref[0:1, 0:1]
    tau = step_ratio / omega
    high = owned(place_ref[0], upper_ref[:, :units])
    kept = block_ref[:regions, :]
    year_dual = block_ref[PAD_ROWS : PAD_ROWS + regions, :]
    x = collect(received_ref, count, -(-2 * n // LANES))
    back[:n, :] = x[:n] + swap_halves(x[n : 2 * n])
    level = jnp.zeros((regions, units), F32)
    year = jnp.zeros((regions, units), F32)
    for h in range(hours):
        old = clip(-tau * get(costs, h), -high, high)
        new = clip(old - tau * (get(grad, h) + get(back, h) + year_scale * year_dual), -high, high)
        bar = 2.0 * new - old
        year = year + bar
        level = get(decay, h) * level + bar
    carry_pieces(carries_ref, rows, (carry_in(kept, level, False),))
    diagonal = lax.broadcasted_iota(jnp.int32, (regions, units), 0) == lane_ids((regions, units))
    for part, column in enumerate(halves(year)):
        line = jnp.sum(jnp.where(diagonal, year_scale * column, 0.0), axis=0, keepdims=True)
        year_ref[:, part * LANES : (part + 1) * LANES] = jnp.broadcast_to(line, (year_ref.shape[0], LANES))


def second_kernel(
    units, year_scale, year_bound,
    omega_ref, received_ref, cost_ref, back_ref, upper_ref, annual_ref, carries_ref,
    sent_ref, dual_ref, rows, dual, out, sems,
):
    regions, hours, width = cost_ref.shape
    omega = omega_ref[0:1, 0:1]
    tau, sigma = step_ratio / omega, step_ratio * omega
    rows[...] = jnp.zeros_like(rows)
    totals = year_totals(received_ref, rows.shape[0] // LANES, regions)
    for t, total in enumerate(totals):
        at = slice(t * LANES, (t + 1) * LANES)
        dual[:, at] = jnp.maximum(sigma * (total - year_bound * annual_ref[:, at]), 0.0)
    leaving = begin(dual, dual_ref, sems.at[1])
    for r in range(regions):
        high = upper_ref[r : r + 1, units:]
        costs = cost_ref[r, :, units:].astype(F32)
        old = clip(-tau * costs, 0.0, high)
        grad = costs + back_ref[r * hours : (r + 1) * hours, units:] + year_scale * dual[r : r + 1, units:]
        bar = 2.0 * clip(old - tau * grad, 0.0, high) - old
        sums = year_scale * jnp.sum(bar, axis=0, keepdims=True)
        for t in range(1, width // LANES):
            rows[t * PAD_ROWS + r : t * PAD_ROWS + r + 1, :] = sums[:, t * LANES - units : (t + 1) * LANES - units]
    year_pieces(rows, out)
    move_pieces(out, rows.shape[0] // LANES, out.shape[0] // (LANES // 2), carries_ref)
    begin(out, sent_ref, sems.at[0]).wait()
    leaving.wait()


def last_kernel(
    shifts, units, count, level_scale, year_scale, year_bound,
    place_ref, omega_ref, cost_ref, back_ref, upper_ref, dual_ref, conversion_ref, demand_ref, prices_ref,
    annual_ref, ends_ref, bus_ref, came_ref, received_ref, decay_ref, energy_ref,
    primal_ref, flows_ref, new_prices_ref, base_ref, slope_ref, year_ref,
    bar, held, demand, old_prices, dual, ends, annual, bus, bus_rows_ref, costs, decay, back, stored, new_stored, sems,
):
    copy, *others = [
        begin(source, target, sems.at[k])
        for k, (source, target) in enumerate(
            (
                (dual_ref, dual),
                (conversion_ref, held),
                (demand_ref, demand),
                (prices_ref, old_prices),
                (annual_ref, annual),
            )
        )
    ]
    regions, hours, width = cost_ref.shape
    bus_rows = demand_ref.shape[2]
    lines = flows_ref.shape[1]
    n = regions * hours
    get, put = strided(regions, hours)
    omega = omega_ref[0:1, 0:1]
    tau, sigma = step_ratio / omega, step_ratio * omega

    costs[:n, :] = cost_ref[:, :, :units].astype(F32).reshape(n, units)
    decay[:n, :] = decay_ref[...].reshape(n, units)
    back[:n, :] = back_ref[:, :units]
    high = upper_ref[:, :units]
    energy = energy_ref[...]
    level, later = collect_carries(received_ref, count, regions, 2)
    for h in range(hours):
        level = get(decay, h) * level + 2.0 * clip(-tau * get(costs, h), -high, high)
        put(stored, h, jnp.maximum(sigma * (level_scale * level - energy), 0.0))
    copy.wait()
    year_part = year_scale * dual[:, :units]
    for h in reversed(range(hours)):
        weight = level_scale * get(stored, h) + later
        later = get(decay, h) * weight
        old = clip(-tau * get(costs, h), -high, high)
        put(new_stored, h, clip(old - tau * (get(costs, h) + get(back, h) + weight + year_part), -high, high))
    level = jnp.zeros((regions, units), F32)
    kept = jnp.ones((regions, units), F32)
    for h in range(hours):
        d = get(decay, h)
        second = 2.0 * get(new_stored, h) - clip(-tau * get(costs, h), -high, high)
        level = d * level + second
        kept = d * kept
        put(base_ref, h, get(stored, h) + sigma * (level_scale * level - energy))
        put(slope_ref, h, (sigma * level_scale) * kept)
        put(back, h, second)
    bar[:, :units] = back[:n, :]
    for r in range(regions):
        at = slice(r * hours, (r + 1) * hours)
        high = upper_ref[r : r + 1, units:]
        row_costs = cost_ref[r, :, units:].astype(F32)
        old = clip(-tau * row_costs, 0.0, high)
        grad = row_costs + back_ref[at, units:] + year_scale * dual[r : r + 1, units:]
        new = clip(old - tau * grad, 0.0, high)
        bar[at, units:] = 2.0 * new - old
        primal_ref[r, :, :units] = new_stored[at, :].astype(BF16)
        primal_ref[r, :, units:] = new.astype(BF16)
    for other in others:
        other.wait()
    step = 256
    image = None
    for k in range(0, width, step):
        part = dot3(split(bar[:, k : k + step]), split(held[k : k + step, :]), ((1,), (0,)))
        image = part if image is None else image + part
    loads = demand[...].astype(F32).reshape(n, bus_rows)
    new_prices_ref[...] = old_prices[...] + sigma * (image - loads)

    year_ref[...] = dual[...] - (sigma * year_bound) * annual[...]
    grow(bus_ref, came_ref, bus)
    groups, reach = bus.shape
    regions_all = groups * regions
    first_region = place_ref[0] * regions
    for r in range(regions):
        moved = bus[...] if r == 0 else pltpu.roll(bus[...], reach - r * hours, 1)
        bus_rows_ref[r * groups : (r + 1) * groups, :] = moved[:, :LANES]

    def exact(a, b, dims):
        return lax.dot_general(
            a, b, (dims, ((), ())), precision=lax.Precision.HIGHEST, preferred_element_type=F32
        )

    def incidence(ids):
        ids = ids + first_region
        ids = jnp.where(ids >= regions_all, ids - regions_all, ids).astype(F32)
        return (ids == ends[1:2, :]).astype(F32) - (ids == ends[0:1, :]).astype(F32)

    ids = lane_ids((1, LANES))
    for part in range(3):
        for first in range(0, groups * lines, LANES):
            row = jnp.zeros((1, LANES), F32)
            for at in range(0, LANES, lines):
                g = (first + at) // lines
                turn = (at - (LANES - (3 - part) * lines)) % LANES
                moved = ends_ref[g : g + 1, :] if turn == 0 else pltpu.roll(ends_ref[g : g + 1, :], turn, 1)
                row = jnp.where(jnp.logical_and(ids >= at, ids < at + lines), moved, row)
            ends[part : part + 1, first : first + LANES] = row

    def rows_like(count):
        return lax.broadcasted_iota(jnp.int32, (count, ends.shape[1]), 0)

    caps = ends[2:3, :]
    at = rows_like(regions_all)
    place = lax.shift_right_logical(at, groups.bit_length() - 1)
    for k, shift in enumerate(shifts):
        bit = lax.bitwise_and(lax.shift_right_logical(at, k), 1)
        place = place + bit * (shift * regions)
    grad = exact(bus_rows_ref[...], incidence(place), ((0,), (0,)))
    flows = clip(-tau * grad[:hours, :], -caps, caps)
    own = flows[:, :lines]
    for g in range(1, groups):
        own = jnp.where(place_ref[0] == g, flows[:, g * lines : (g + 1) * lines], own)
    flows_ref[...] = own
    inflow = exact(2.0 * flows, incidence(rows_like(LANES)), ((1,), (1,)))
    ids = lane_ids(inflow.shape)
    for r in range(regions):
        moved = inflow if r == 0 else pltpu.roll(inflow, LANES - r, 1)
        at = slice(r * hours, (r + 1) * hours)
        new_prices_ref[at, :LANES] = new_prices_ref[at, :LANES] + sigma * jnp.where(ids == 0, moved, 0.0)


def finish_kernel(count, omega_ref, received_ref, base_ref, slope_ref, rest_ref, storage_ref, year_ref):
    regions = rest_ref.shape[0]
    hours = base_ref.shape[0] // PAD_ROWS
    sigma = step_ratio * omega_ref[0:1, 0:1]
    for t, total in enumerate(year_totals(received_ref, count, regions)):
        at = slice(t * LANES, (t + 1) * LANES)
        year_ref[:, at] = jnp.maximum(rest_ref[:, at] + sigma * total, 0.0)
    (entering,) = collect_carries(received_ref, count, regions, 1)
    for r in range(regions):
        at = slice(r * hours, (r + 1) * hours)
        storage_ref[at, :] = jnp.maximum(base_ref[at, :] + slope_ref[at, :] * entering[r : r + 1, :], 0.0)


def exchange(x):
    blocks = lax.axis_size("tm")
    pieces = x.reshape(blocks, 1, x.size // blocks)
    return lax.all_to_all(pieces, "tm", 0, 0, tiled=True).reshape(x.shape)


def per_device(cost, demand, conversion, upper, decay, energy_cap, annual_cap, line_ends, line_cap):
    hours, regions, width = cost.shape
    bus_rows = demand.shape[2]
    units = decay.shape[2]
    lines = line_ends.shape[0]
    blocks = lax.axis_size("tm")
    groups = lax.axis_size("region")
    hours_all = hours * blocks
    scale = 1.0 / math.sqrt(hours_all)
    bound = math.sqrt(hours_all)
    n = regions * hours
    spaced = PAD_ROWS * hours
    year_rows = 2 * PAD_ROWS * (width // LANES)
    year_count = year_rows // LANES
    turned_count = 4 * n // LANES
    back_count = -(-2 * n // LANES)
    rows = lambda k: pltpu.VMEM((k, LANES), F32)
    sems = lambda k: pltpu.SemaphoreType.DMA((k,))
    pieces = lambda count: struct(blocks * count, LANES)
    sent = lambda count: in_hbm(blocks * count, LANES)
    cost = jnp.transpose(cost, (1, 0, 2))
    demand = jnp.transpose(demand, (1, 0, 2))
    decay = jnp.transpose(decay, (1, 0, 2))
    tm_place = lax.axis_index("tm").astype(jnp.int32).reshape(1)
    region_place = lax.axis_index("region").astype(jnp.int32).reshape(1)

    shifts = (1, 4, 2)

    def from_ahead(x, reach):
        return lax.ppermute(x, "region", [((z + reach) % groups, z) for z in range(groups)])

    sums = call(
        sums_kernel,
        in_hbm(groups, LANES),
        "sums",
        [HBM] * 4,
        [
            pltpu.VMEM((regions, hours, width), BF16),
            pltpu.VMEM((regions, hours, bus_rows), BF16),
            pltpu.VMEM((2, lines), jnp.int32),
            pltpu.VMEM((1, lines), F32),
            rows(groups),
            sems(5),
        ],
        HBM,
    )(keep(cost), keep(demand), keep(line_ends.T), keep(line_cap.reshape(1, -1)))
    sums = lax.all_to_all(sums.reshape(groups, 1, LANES), "region", 0, 0, tiled=True).reshape(groups, LANES)
    turned = call(turn_kernel, pieces(turned_count), "turn", [VMEM] * 2, [rows(4 * n)])(cost, decay)
    joined_count = 1 + turned_count
    joined = call(
        join_kernel, sent(joined_count), "join", [VMEM] * 2, [rows(blocks * joined_count), sems(1)], HBM
    )(sums, turned)
    joined = exchange(joined)
    reach = -(-n // LANES) * LANES
    omega, bus, first = call(
        functools.partial(first_kernel, units, scale),
        (struct(8, LANES), struct(1, reach), sent(year_count)),
        "first_primal",
        [VMEM] * 5,
        [rows(blocks * year_count), rows(year_rows), rows(reach), sems(1)],
        (VMEM, VMEM, HBM),
    )(joined, cost, upper, demand, conversion[:, :1].T)
    first = exchange(first)

    prices, back, back_turned = call(
        functools.partial(prices_kernel, units),
        (in_hbm(n, bus_rows), struct(n, width), pieces(back_count)),
        "first_prices",
        [VMEM] * 3 + [HBM] * 2,
        [
            pltpu.VMEM((n, width), F32),
            rows(back_count * LANES),
            pltpu.VMEM((width, bus_rows), F32),
            pltpu.VMEM((regions, hours, bus_rows), BF16),
            pltpu.VMEM((n, bus_rows), F32),
            sems(2),
        ],
        (HBM, VMEM, VMEM),
        flops=4000000000,
        nbytes=5000000,
    )(omega, cost, upper, keep(demand), keep(conversion))

    second_count = year_count + back_count
    second, bus = call(
        functools.partial(sum_kernel, year_count),
        (sent(second_count), struct(2, reach)),
        "year_sum",
        [VMEM] * 4,
        [rows(blocks * second_count), sems(1)],
        (HBM, VMEM),
    )(first, back_turned, bus, from_ahead(bus, shifts[0]))
    second = exchange(second)

    carries, costs_all, decay_all, grad_all, block = call(
        functools.partial(storage_kernel, scale, scale, bound),
        (pieces(1),) + (struct(spaced, units),) * 3 + (struct(2 * PAD_ROWS, units),),
        "storage",
        [SMEM] + [VMEM] * 2 + [ANY] + [VMEM] * 3,
        [rows(spaced) for _ in range(5)] + [rows(LANES)],
        flops=4000000000,
    )(tm_place, omega, joined, first, upper, energy_cap, annual_cap)

    third, year_dual = call(
        functools.partial(second_kernel, units, scale, bound),
        (sent(year_count + 1), in_hbm(regions, width)),
        "second_primal",
        [VMEM] * 7,
        [
            rows(year_rows),
            pltpu.VMEM((regions, width), F32),
            rows(blocks * (year_count + 1)),
            sems(2),
        ],
        (HBM, HBM),
    )(omega, second, cost, back, upper, annual_cap, carries)
    third = exchange(third)

    carry, stored_year, bus = call(
        functools.partial(storage_again_kernel, year_count, scale),
        (pieces(1), struct(8, year_rows), struct(4, reach)),
        "storage_again",
        [SMEM] + [VMEM] * 9 + [HBM],
        [rows(spaced), rows(LANES)],
        flops=4000000000,
    )(tm_place, omega, costs_all, decay_all, grad_all, block, second, upper, bus, from_ahead(bus, shifts[1]), keep(year_dual))

    fourth = call(
        functools.partial(sum_with_stored_kernel, year_count),
        sent(year_count + 1),
        "year_sum_2",
        [VMEM] * 3,
        [rows(blocks * (year_count + 1)), sems(1)],
        HBM,
    )(third, stored_year, carry)
    fourth = exchange(fourth)

    new_primal, flows, prices, base, slope, rest = call(
        functools.partial(last_kernel, shifts, units, year_count, scale, scale, bound),
        (
            struct(regions, hours, width, dtype=BF16),
            struct(hours, lines),
            struct(n, bus_rows),
            struct(spaced, units),
            struct(spaced, units),
            struct(regions, width),
        ),
        "second_prices",
        [SMEM] + [VMEM] * 4 + [HBM] * 5 + [VMEM] * 6,
        [
            pltpu.VMEM((n, width), F32),
            pltpu.VMEM((width, bus_rows), F32),
            pltpu.VMEM((regions, hours, bus_rows), BF16),
            pltpu.VMEM((n, bus_rows), F32),
            pltpu.VMEM((regions, width), F32),
            pltpu.VMEM((3, groups * lines), F32),
            pltpu.VMEM((regions, width), F32),
            pltpu.VMEM((groups, reach), F32),
            rows(groups * regions),
        ]
        + [rows(spaced) for _ in range(5)]
        + [sems(5)],
        flops=3000000000,
        nbytes=6000000,
    )(
        region_place, omega, cost, back, upper, keep(year_dual), keep(conversion), keep(demand), keep(prices),
        keep(annual_cap), sums, bus, from_ahead(bus, shifts[2]), third, decay, energy_cap,
    )
    storage_dual, year_dual = call(
        functools.partial(finish_kernel, year_count),
        (struct(n, units), struct(regions, width)),
        "finish",
        [VMEM] * 5,
    )(omega, fourth, base, slope, rest)
    turn = lambda x, last: jnp.transpose(x.reshape(regions, hours, last), (1, 0, 2))
    return (
        jnp.transpose(new_primal, (1, 0, 2)),
        flows,
        turn(prices, bus_rows),
        turn(storage_dual, units),
        year_dual,
    )


def solution(mesh):
    in_specs = (
        P("tm", "region", None),
        P("tm", "region", None),
        P(),
        P("region", None),
        P("tm", "region", None),
        P("region", None),
        P("region", None),
        P("region", None),
        P("region"),
    )
    out_specs = (
        P("tm", "region", None),
        P("tm", "region"),
        P("tm", "region", None),
        P("tm", "region", None),
        P("region", None),
    )
    return jax.shard_map(
        per_device, mesh=mesh, in_specs=in_specs, out_specs=out_specs, check_vma=False
    )
```
